32 devices in a mesh: dp: 4 (over z), tm: 2 (over x), pos: 4 (over y, core).
Axes of the slice: x: 2, y: 2, z: 4, core: 2. Of those that a mesh axis runs over, the one named last changes fastest.
Arguments:
- tokens: bfloat16 [8, 16, 196, 768], P('dp', 'tm', 'pos'), may hold values from -6 to 6
- cotangent: bfloat16 [8, 16, 196, 768], P('dp', 'tm', 'pos'), may hold values from -6 to 6
- frame_counts: int32 [8], P('dp'), may hold values from 1 to 16, as said below
- weight_in: float32 [768, 9984], P('dp')
- weight_out: float32 [3072, 768], P('dp'), may hold values from -0.109375 to 0.109375
- vectors: float32 [768, 18], P('dp')
- moment_in: float32 [768, 9984], P('dp'), may hold values from -0.00048828125 to 0.00048828125
- moment_out: float32 [3072, 768], P('dp'), may hold values from -0.00048828125 to 0.00048828125
- moment_vec: float32 [768, 18], P('dp'), may hold values from -0.00048828125 to 0.00048828125
- square_in: float32 [768, 9984], P('dp'), may hold values from 9.959334e-11 to 3.9837336e-10
- square_out: float32 [3072, 768], P('dp'), may hold values from 9.959334e-11 to 3.9837336e-10
- square_vec: float32 [768, 18], P('dp'), may hold values from 9.959334e-11 to 3.9837336e-10
Outputs:
- block_out: bfloat16 [8, 16, 196, 768], P('dp', 'tm', 'pos')
- input_grad: float32 [8, 16, 196, 768], P('dp', 'tm', 'pos')
- grad_norm: float32 [], replicated
- new_in: float32 [768, 9984], P('dp')
- new_out: float32 [3072, 768], P('dp')
- new_vec: float32 [768, 18], P('dp')
- first_in: float32 [768, 9984], P('dp')
- first_out: float32 [3072, 768], P('dp')
- first_vec: float32 [768, 18], P('dp')
- second_in: float32 [768, 9984], P('dp')
- second_out: float32 [3072, 768], P('dp')
- second_vec: float32 [768, 18], P('dp')
- bias_down_grad: float32 [768], P('dp')
The draws below stay inside these ranges and needn't reach their ends.
Inputs may be any that keep to these rules, and one draw needn't show every extreme that they name: `frame_counts`: among the 2 clips of each index of dp (consecutive rows of one device) one has 16 frames.
All inputs are finite; a program needn't handle non-finite values.
Results may differ from the reference program's by a relative error of at most 0.019.
Values may be sent and summed in bfloat16 or wider, within the bound.
No kernel may reach another device: no remote copies, remote signals or barrier semaphores. Data moves between devices by JAX's collectives and lax.ppermute only.
A program may use at most 320 MiB of HBM per device.

```python
import math
import jax
import jax.numpy as jnp
from jax import lax

HEADS = 12
HD = 64
D = 768
FF = 3072
NV = 18
WCOLS = 9984
NPAR = 10040832
P_SIZE = 196
FMAX = 16
CL = 2
CLIPS = 8
STEP = 10


def draw_frame_counts(key, part):
    key = jax.random.fold_in(key, 1)
    first_key, second_key = jax.random.split(key)
    counts = jax.random.randint(first_key, (CLIPS,), 1, FMAX + 1, dtype=jnp.int32)
    chosen = jax.random.randint(second_key, (CLIPS // CL, 1), 0, CL, dtype=jnp.int32)
    slots = jnp.arange(CL, dtype=jnp.int32)[None, :]
    full = (slots == chosen).reshape(CLIPS)
    return jnp.where(full, FMAX, counts).astype(jnp.int32)


def draw_weight_in(key, part):
    key = jax.random.fold_in(key, 2)
    column = jnp.arange(WCOLS, dtype=jnp.int32)
    scale = jnp.where((column >= 3 * D) & (column < 4 * D), 2.0, 1.0)
    scale = jnp.where((column >= 8 * D) & (column < 9 * D), 5.0, scale)
    values = jax.random.normal(key, (D, WCOLS), jnp.float32)
    return (values * scale[None, :] * D ** (-0.5)).astype(jnp.float32)


def draw_vectors(key, part):
    key = jax.random.fold_in(key, 3)
    first_key, second_key = jax.random.split(key)
    column = jnp.arange(NV, dtype=jnp.int32)
    is_gain = (column == 0) | (column == 6) | (column == 11)
    rising = 0.5 + jnp.arange(D, dtype=jnp.float32) / D
    spread = jax.random.uniform(first_key, (D, NV), jnp.float32, 0.8, 1.25)
    shifts = 0.2 * jax.random.normal(second_key, (D, NV), jnp.float32)
    return jnp.where(is_gain[None, :], rising[:, None] * spread, shifts).astype(jnp.float32)


def level_of(key, shape, shards, least, high):
    def one(axis_at, shards_of):
        steps = jax.random.uniform(jax.random.fold_in(jax.random.fold_in(key, 6), axis_at), (shards_of,), jnp.float32, least / len(shards), high / len(shards))
        return jnp.repeat(jnp.exp(steps), shape[axis_at] // shards_of).reshape((-1,) + (1,) * (len(shape) - axis_at - 1))

    factor_of = one(*shards[0])
    for cut in shards[1:]:
        factor_of = factor_of * one(*cut)
    return factor_of


def normal_values(stream_key, dims, scale, reach, shards=(), kind=jnp.bfloat16):
    entries = jax.random.normal(stream_key, dims, jnp.float32) * scale
    if len(shards) > 0:
        entries = level_of(stream_key, dims, shards, -0.22, 0.18) * entries
    return jnp.clip(entries, min=-reach, max=reach).astype(kind)


def setup_inputs(seed: int = 0) -> dict:
    arg_keys = jax.random.split(jax.random.key(seed), 13)
    tokens = normal_values(arg_keys[0], (CLIPS, FMAX, P_SIZE, D), 1.0, 6.0, ((0, 4), (1, 2), (2, 4)))
    cotangent = normal_values(arg_keys[1], (CLIPS, FMAX, P_SIZE, D), 1.0, 6.0, ((0, 4), (1, 2), (2, 4)))
    frame_counts = draw_frame_counts(jax.random.fold_in(arg_keys[12], 71), 0)
    weight_in = draw_weight_in(jax.random.fold_in(arg_keys[12], 71), 0)
    weight_out = normal_values(arg_keys[4], (FF, D), FF ** -0.5, 0.109375, ((0, 4),), jnp.float32)
    vectors = draw_vectors(jax.random.fold_in(arg_keys[12], 71), 0)
    moment_in = normal_values(arg_keys[6], (D, WCOLS), (0.111 * NPAR ** -0.5), 0.00048828125, ((0, 4),), jnp.float32)
    moment_out = normal_values(arg_keys[7], (FF, D), (0.111 * NPAR ** -0.5), 0.00048828125, ((0, 4),), jnp.float32)
    moment_vec = normal_values(arg_keys[8], (D, NV), (0.111 * NPAR ** -0.5), 0.00048828125, ((0, 4),), jnp.float32)
    square_in = jnp.clip(jnp.exp(math.log(3.9837336207604324e-10) - 1.3862944 * jax.random.uniform(arg_keys[9], (D, WCOLS), jnp.float32) ** level_of(arg_keys[9], (D, WCOLS), ((0, 4),), -0.2, 0.2)), 9.959334051901081e-11, 3.9837336207604324e-10)
    square_out = jnp.clip(jnp.exp(math.log(3.9837336207604324e-10) - 1.3862944 * jax.random.uniform(arg_keys[10], (FF, D), jnp.float32) ** level_of(arg_keys[10], (FF, D), ((0, 4),), -0.2, 0.2)), 9.959334051901081e-11, 3.9837336207604324e-10)
    square_vec = jnp.clip(jnp.exp(math.log(3.9837336207604324e-10) - 1.3862944 * jax.random.uniform(arg_keys[11], (D, NV), jnp.float32) ** level_of(arg_keys[11], (D, NV), ((0, 4),), -0.2, 0.2)), 9.959334051901081e-11, 3.9837336207604324e-10)
    return dict(tokens=tokens, cotangent=cotangent, frame_counts=frame_counts, weight_in=weight_in, weight_out=weight_out, vectors=vectors, moment_in=moment_in, moment_out=moment_out, moment_vec=moment_vec, square_in=square_in, square_out=square_out, square_vec=square_vec)


NORM_EPSILON = 1e-06
CLIP_NORM = 1.0
LEARN_RATE = 0.03
LEARN_RATE_VEC = 0.25
BETA_FIRST = 0.9
BETA_SECOND = 0.999
ADAM_EPSILON = 1e-08
WEIGHT_DECAY = 0.05
MASKED_SCORE = -1e+30
PRECISE = lax.Precision.HIGHEST

@jax.custom_vjp
def low(v):
    return lax.optimization_barrier(v.astype(jnp.bfloat16)).astype(jnp.float32)

@jax.custom_vjp
def low_back(v):
    return v

def low_keep(v):
    return (low(v), None)

def low_pass(kept, grad):
    return (grad,)

def back_keep(v):
    return (v, None)

def back_low(kept, grad):
    return (low(grad),)
low.defvjp(low_keep, low_pass)
low_back.defvjp(back_keep, back_low)

def rounded_both(value):
    return low_back(low(value))

def layer_norm(inputs, gain, shift):
    centre = lax.optimization_barrier(jnp.mean(inputs, axis=-1, keepdims=True))
    centred = inputs - centre
    variance = lax.optimization_barrier(jnp.mean(centred * centred, axis=-1, keepdims=True))
    return centred * lax.rsqrt(variance + NORM_EPSILON) * gain + shift

def project(inputs, weight):
    return jnp.einsum('...i,ij->...j', inputs, weight, precision=PRECISE)

def with_heads(inputs):
    return inputs.reshape(inputs.shape[:-1] + (HEADS, HD))

def attend(queries, keys, values, score_form, out_form, key_mask):
    scores = jnp.einsum(score_form, with_heads(queries), with_heads(keys), precision=PRECISE) * HD ** (-0.5)
    if key_mask is not None:
        scores = jnp.where(key_mask, scores, MASKED_SCORE)
    weights = low(jax.nn.softmax(low_back(scores), axis=-1))
    mixed = jnp.einsum(out_form, weights, with_heads(values), precision=PRECISE)
    return mixed.reshape(mixed.shape[:-2] + (D,))

def forward(inputs, weight_in, weight_out, vectors, key_valid):
    weights = low(weight_in)
    down = low(weight_out)
    params = low(vectors)
    time_mask = key_valid[None, None, None, :]
    normed = low(layer_norm(inputs, params[:, 0], params[:, 1]))
    mixed = project(normed, weights[:, :3 * D])
    queries = rounded_both(mixed[..., :D] + params[:, 2])
    keys = rounded_both(mixed[..., D:2 * D])
    values = rounded_both(mixed[..., 2 * D:] + params[:, 3])
    attended = rounded_both(attend(queries, keys, values, 'fphd,gphd->phfg', 'phfg,gphd->fphd', time_mask))
    projected = rounded_both(project(attended, weights[:, 3 * D:4 * D]) + params[:, 4])
    after_time = inputs + low_back(project(projected, weights[:, 4 * D:5 * D]) + params[:, 5])
    normed = low(layer_norm(after_time, params[:, 6], params[:, 7]))
    mixed = project(normed, weights[:, 5 * D:8 * D])
    queries = rounded_both(mixed[..., :D] + params[:, 8])
    keys = rounded_both(mixed[..., D:2 * D])
    values = rounded_both(mixed[..., 2 * D:] + params[:, 9])
    attended = rounded_both(attend(queries, keys, values, 'fphd,fqhd->fhpq', 'fhpq,fqhd->fphd', None))
    after_space = after_time + low_back(project(attended, weights[:, 8 * D:9 * D]) + params[:, 10])
    normed = low(layer_norm(after_space, params[:, 11], params[:, 12]))
    bias_up = params[:, 13:17].T.reshape(FF)
    hidden = low_back(project(normed, weights[:, 9 * D:]) + bias_up)
    activated = low(jax.nn.gelu(hidden, approximate=False))
    return after_space + low_back(project(activated, down) + params[:, 17])

def adam_update(weight, grad, moment, square, decay, factor, rate):
    grad = grad * factor
    moment = BETA_FIRST * moment + (1.0 - BETA_FIRST) * grad
    square = BETA_SECOND * square + (1.0 - BETA_SECOND) * grad * grad
    moment_hat = moment / (1.0 - BETA_FIRST ** STEP)
    square_hat = square / (1.0 - BETA_SECOND ** STEP)
    fresh = weight - rate * (moment_hat / (jnp.sqrt(square_hat) + ADAM_EPSILON) + decay * weight)
    return (fresh, moment, square)

def reference(tokens, cotangent, frame_counts, weight_in, weight_out, vectors, moment_in, moment_out, moment_vec, square_in, square_out, square_vec):
    frame_ids = jnp.arange(FMAX, dtype=jnp.int32)

    def per_clip(totals, inputs):
        clip_tokens, clip_cot, clip_count = inputs
        key_valid = frame_ids < clip_count

        def run_clip(clip_value, first_weight, second_weight, third_weight):
            return forward(clip_value, first_weight, second_weight, third_weight, key_valid)
        clip_out, pullback = jax.vjp(run_clip, clip_tokens.astype(jnp.float32), weight_in, weight_out, vectors)
        frame_weight = key_valid.astype(jnp.float32)[:, None, None]
        grads = pullback(clip_cot.astype(jnp.float32) * frame_weight)
        totals = (totals[0] + grads[1], totals[1] + grads[2], totals[2] + grads[3])
        return (totals, (clip_out.astype(jnp.bfloat16), grads[0]))
    zeros = (jnp.zeros_like(weight_in), jnp.zeros_like(weight_out), jnp.zeros_like(vectors))
    totals, stacked = lax.scan(per_clip, zeros, (tokens, cotangent, frame_counts))
    block_out, input_grad = stacked
    total_square = jnp.sum(totals[0] * totals[0]) + jnp.sum(totals[1] * totals[1]) + jnp.sum(totals[2] * totals[2])
    grad_norm = jnp.sqrt(total_square)
    factor = CLIP_NORM / jnp.maximum(grad_norm, CLIP_NORM)
    new_in, first_in, second_in = adam_update(weight_in, totals[0], moment_in, square_in, WEIGHT_DECAY, factor, LEARN_RATE)
    new_out, first_out, second_out = adam_update(weight_out, totals[1], moment_out, square_out, WEIGHT_DECAY, factor, LEARN_RATE)
    new_vec, first_vec, second_vec = adam_update(vectors, totals[2], moment_vec, square_vec, 0.0, factor, LEARN_RATE_VEC)
    bias_down_grad = totals[2][:, 17] * factor
    return (block_out, input_grad, grad_norm, new_in, new_out, new_vec, first_in, first_out, first_vec, second_in, second_out, second_vec, bias_down_grad)
```

```python
import functools

import jax
import jax.numpy as jnp
from jax import lax
from jax.experimental import pallas as pl
from jax.experimental.pallas import tpu as pltpu
from jax.sharding import PartitionSpec as P

HEADS = 12
HD = 64
D = 768
FF = 3072
STEP = 10

NORM_EPSILON = 1e-06
CLIP_NORM = 1.0
LEARN_RATE = 0.03
LEARN_RATE_VEC = 0.25
BETA_FIRST = 0.9
BETA_SECOND = 0.999
ADAM_EPSILON = 1e-08
WEIGHT_DECAY = 0.05
MASKED_SCORE = -1e30
SCALE = HD ** (-0.5)

F32 = jnp.float32
BF16 = jnp.bfloat16
PAIR = 2 * HD
PAIRS = D // PAIR
NB = 256
ROWB = 112
VMEM_LIMIT = 56 * 1024 * 1024
SMALL_VMEM = 24 * 1024 * 1024

G_T, B_T, C_T, E_T, O_T, F_T, G_S, B_S, C_S, E_S, O_S, G_M, B_M, U_1, U_2 = (
    0, 1, 2, 3, 4, 5, 6, 7, 8, 9, 10, 11, 12, 13, 17,
)


COUNT_AT, T_AT, P_AT, Z_AT, C_AT, Q_AT = 0, 1, 2, 3, 4, 5
A_AT, B_AT, PAIR_AT, ODD_AT = 13, 14, 15, 16
OTHERS = (1, 3, 2)
PIECE = 48
VROWS = 24


def dot_nn(a, b):
    return lax.dot_general(a, b, (((1,), (0,)), ((), ())), preferred_element_type=F32)


def dot_nt(a, b):
    return lax.dot_general(a, b, (((1,), (1,)), ((), ())), preferred_element_type=F32)


def dot_tn(a, b):
    return lax.dot_general(a, b, (((0,), (0,)), ((), ())), preferred_element_type=F32)


def loop(count, body, unroll=1):
    def step(i, carry):
        body(i)
        return carry

    lax.fori_loop(0, count, step, 0, unroll=unroll)


def block(i, size):
    return pl.ds(pl.multiple_of(i * size, size), size)


def row_blocks(rows, body):
    loop(rows // ROWB, lambda i: body(pl.ds(pl.multiple_of(i * ROWB, 16), ROWB)))


def col_blocks(cols, body):
    loop(cols // NB, lambda i: body(block(i, NB)))


LANES = 128
TILES = D // LANES


def put_slot(xs, s, slots, value):
    for j in range(TILES):
        xs[j, pl.ds(s, value.shape[0], stride=slots), :] = value[:, j * LANES : (j + 1) * LANES]


def get_slot(xs, s, slots, count):
    return jnp.concatenate([xs[j, pl.ds(s, count, stride=slots), :] for j in range(TILES)], axis=1)


def get_rows(xs, r):
    return jnp.concatenate([xs[j, r, :] for j in range(TILES)], axis=1)


def put_rows(xs, r, value):
    for j in range(TILES):
        xs[j, r, :] = value[:, j * LANES : (j + 1) * LANES]


def put_cols(xs, i, value):
    per = NB // LANES
    for j in range(per):
        xs[i * per + j] = value[:, j * LANES : (j + 1) * LANES]


def normalise(x):
    centred = x - jnp.mean(x, axis=-1, keepdims=True)
    variance = jnp.mean(centred * centred, axis=-1, keepdims=True)
    inverse = lax.rsqrt(variance + NORM_EPSILON)
    return centred * inverse, inverse


def norm_back(x, grad, gain):
    z_hat, inverse = normalise(x)
    h = grad * gain
    first = jnp.mean(h, axis=-1, keepdims=True)
    second = jnp.mean(h * z_hat, axis=-1, keepdims=True)
    dz = inverse * (h - first - z_hat * second)
    return dz, jnp.sum(grad * z_hat, axis=0, keepdims=True), jnp.sum(grad, axis=0, keepdims=True)


def softmax_rows(scores):
    top = jnp.max(scores, axis=-1, keepdims=True)
    e = jnp.exp(scores - top)
    return e * (1.0 / jnp.sum(e, axis=-1, keepdims=True))


def head_masks():
    lane = lax.broadcasted_iota(jnp.int32, (1, PAIR), 1)
    return [(lane < HD).astype(BF16), (lane >= HD).astype(BF16)]


def gelu_parts(a):
    z = jnp.abs(a) * 0.7071067811865476
    t = 1.0 / (1.0 + 0.3275911 * z)
    e = jnp.exp(-z * z)
    poly = t * (0.254829592 + t * (-0.284496736 + t * (1.421413741 + t * (-1.453152027 + t * 1.061405429))))
    tail = 0.5 * poly * e
    phi_low = jnp.where(a < 0.0, tail, 1.0 - tail)
    return a * phi_low, phi_low + a * (0.3989422804014327 * e)


class Weight:
    def __init__(self, cols, rows=D, whole=None, shard=None, blocks=None, pieces=(), offset=0, tall=False):
        self.rows, self.cols, self.whole, self.offset, self.tall = rows, cols, whole, offset, tall
        self.blocks = blocks
        self.arrays = [whole] if whole is not None else [shard, *pieces]

    def scratch(self):
        count = 1 if self.whole is not None else len(self.blocks) + 8 * len(OTHERS)
        return [pltpu.VMEM((self.rows, self.cols), BF16), pltpu.SemaphoreType.DMA((count,))]

    def copies(self, refs, scal, dst, sems):
        if self.whole is not None:
            return [pltpu.make_async_copy(refs[0], dst, sems.at[0])]
        shard = self.rows // 4
        z, c = scal[Z_AT], scal[C_AT]
        own_rows = pl.ds(pl.multiple_of(z * shard, 16), shard)
        out, at = [], 0
        for first, size in self.blocks:
            if self.tall:
                src, to = refs[0].at[first : first + size, :], dst.at[own_rows, :]
            else:
                src, to = refs[0].at[:, first : first + size], dst.at[own_rows, at : at + size]
            at += size
            out.append(pltpu.make_async_copy(src, to, sems.at[len(out)]))
        width = self.cols if self.tall else self.cols // 2
        for k in range(8):
            half = c if k < 4 else 1 - c
            quarter = scal[Q_AT + k]
            for j, m in enumerate(OTHERS):
                row = jnp.bitwise_xor(z, m) * shard + quarter * PIECE
                col = 0
                if self.tall:
                    row = row + half * (shard // 2)
                else:
                    col = pl.multiple_of(half * width, 128)
                src = refs[1 + k].at[j, :, self.offset : self.offset + width]
                to = dst.at[pl.ds(pl.multiple_of(row, 16), PIECE), pl.ds(col, width)]
                out.append(pltpu.make_async_copy(src, to, sems.at[len(out)]))
        return out


class Loaded:
    def __init__(self, ref, copies):
        self.ref, self.copies, self.waited = ref, copies, False

    def get(self):
        if not self.waited:
            for c in self.copies:
                c.wait()
            self.waited = True
        return self.ref


def sds(shape, dtype):
    return jax.ShapeDtypeStruct(shape, dtype)


def cost(microseconds):
    return pl.CostEstimate(flops=int(microseconds * 1e9), bytes_accessed=0, transcendentals=0)


COSTS = {
    "time_in": 12, "time_attn": 11, "time_mid": 9, "space_in": 10, "space_mid": 15, "cot": 3, "cut": 3, "join": 3,
    "mlp": 50, "mlp_out": 14, "space_back": 22, "space_out": 17, "time_proj": 14, "time_attn_back": 28, "time_out": 20,
}


def call(kernel, scal, ins, weights, outs, scratch=(), after=()):
    n_in, n_out, n_scr = len(ins), len(outs), len(scratch)
    arrays = [a for w in weights for a in w.arrays]

    def body(scal_ref, *refs):
        in_refs, refs = refs[:n_in], refs[n_in:]
        array_refs, refs = refs[: len(arrays)], refs[len(arrays) + len(after) :]
        out_refs, refs = refs[:n_out], refs[n_out:]
        own, refs = refs[:n_scr], refs[n_scr:]
        loaded, at = [], 0
        for i, w in enumerate(weights):
            dst, sems = refs[2 * i : 2 * i + 2]
            copies = w.copies(array_refs[at : at + len(w.arrays)], scal_ref, dst, sems)
            at += len(w.arrays)
            for c in copies:
                c.start()
            loaded.append(Loaded(dst, copies))
        kernel(scal_ref, *in_refs, *loaded, *out_refs, *own)
        for w in loaded:
            w.get()

    in_vmem = pl.BlockSpec(memory_space=pltpu.VMEM)
    name = getattr(kernel, "func", kernel).__name__.removesuffix("_kernel")
    return pl.pallas_call(
        body,
        name=name,
        out_shape=tuple(outs),
        in_specs=[pl.BlockSpec(memory_space=pltpu.SMEM)]
        + [in_vmem] * n_in
        + [pl.BlockSpec(memory_space=pl.ANY)] * (len(arrays) + len(after)),
        out_specs=tuple(in_vmem for _ in outs),
        scratch_shapes=list(scratch) + [x for w in weights for x in w.scratch()],
        compiler_params=pltpu.CompilerParams(vmem_limit_bytes=VMEM_LIMIT),
        cost_estimate=cost(COSTS[name]),
    )(scal, *ins, *arrays, *after)


def grad_cols(width, body):
    loop(width // NB, lambda i: body(pl.multiple_of(i * NB, NB), NB))
    if width % NB:
        body(width - width % NB, width % NB)


def weight_grad(left_t, right, scal, mine, theirs):
    width = mine.shape[1]
    for out, half in ((theirs, 1 - scal[C_AT]), (mine, scal[C_AT])):

        def body(at, size, out=out, half=half):
            c = pl.ds(pl.multiple_of(half * width + at, 128), size)
            out[:, pl.ds(at, size)] = dot_nn(left_t[...], right[:, c]).astype(BF16)

        grad_cols(width, body)


def time_mask(scal, slots):
    row = lax.broadcasted_iota(jnp.int32, (ROWB, ROWB), 0)
    col = lax.broadcasted_iota(jnp.int32, (ROWB, ROWB), 1)
    frame = jnp.bitwise_xor(col % slots, scal[T_AT] * (slots // 2))
    return (row // slots == col // slots) & (frame < scal[COUNT_AT])


def project_qkv(h, w, par, q_row, v_row, out):
    for part, row in enumerate((q_row, None, v_row)):

        def cols(i, part=part, row=row):
            c = pl.ds(pl.multiple_of(part * D + i * NB, NB), NB)
            value = dot_nn(h[...], w[:, c])
            if row is not None:
                value = value + par[row : row + 1, block(i, NB)]
            out[:, c] = value.astype(BF16)

        loop(D // NB, cols)


def time_in_kernel(scal, own, peer, w_load, vec_load, x_out, h_out, qkv_out, par, xs):
    half, here = own.shape[0], own.shape[1]
    slots = 2 * half
    for s in range(slots):
        src = own if s < half else peer
        put_slot(xs, s, slots, src[s % half].astype(F32))
    vec = vec_load.get()
    par[...] = vec[:, :LANES].astype(F32).T[:VROWS, :]
    gain, shift = par[G_T : G_T + 1, :], par[B_T : B_T + 1, :]

    def rows(r):
        x = get_rows(xs, r)
        x_out[r, :] = x.astype(BF16)
        h_out[r, :] = (normalise(x)[0] * gain + shift).astype(BF16)

    row_blocks(xs.shape[1], rows)
    project_qkv(h_out, w_load.get(), par, C_T, E_T, qkv_out)


def time_attn_kernel(slots, scal, qkv, y_out):
    mask = time_mask(scal, slots)
    masks = head_masks()

    def group(r):
        for j in range(PAIRS):
            q = qkv[r, j * PAIR : (j + 1) * PAIR]
            k = qkv[r, D + j * PAIR : D + (j + 1) * PAIR]
            v = qkv[r, 2 * D + j * PAIR : 2 * D + (j + 1) * PAIR]
            y = 0.0
            for h in range(2):
                s = jnp.where(mask, dot_nt(q * masks[h], k) * SCALE, MASKED_SCORE)
                y += dot_nn(softmax_rows(s).astype(BF16), v * masks[h])
            y_out[r, j * PAIR : (j + 1) * PAIR] = y.astype(BF16)

    row_blocks(y_out.shape[0], group)


def time_mid_kernel(scal, y, x, par, w_load, z_out, b0, b1, b2, b3, xs):
    here, per = b0.shape[1], b0.shape[0]
    slots = 4 * per
    w = w_load.get()

    def proj(i):
        c = block(i, NB)
        z_out[:, c] = (dot_nn(y[...], w[:, c]) + par[O_T : O_T + 1, c]).astype(BF16)

    loop(D // NB, proj)

    def after(i):
        c = block(i, NB)
        fc = dot_nn(z_out[...], w[:, pl.ds(pl.multiple_of(D + i * NB, NB), NB)])
        put_cols(xs, i, x[:, c].astype(F32) + (fc + par[F_T : F_T + 1, c]))

    loop(D // NB, after)
    for r, out in enumerate((b0, b1, b2, b3)):
        first = jnp.bitwise_xor(scal[P_AT], r) * per
        for i in range(per):
            out[i] = get_slot(xs, first + i, slots, here).astype(BF16)


def fill_space(blocks, xs):
    per, here = blocks[0].shape[0], blocks[0].shape[1]
    whole = here * len(blocks)
    for f in range(per):
        for r, b in enumerate(blocks):
            xs[f * whole + r * here : f * whole + (r + 1) * here, :] = b[f].astype(F32)


def cot_kernel(scal, b0, b1, b2, b3, dy_out, xs):
    per, here = b0.shape[0], b0.shape[1]
    fill_space((b0, b1, b2, b3), xs)
    whole = 4 * here
    rows = xs.shape[0]
    row = lax.broadcasted_iota(jnp.int32, (rows, 1), 0)
    slot = scal[P_AT] * per
    weight = jnp.zeros((rows, 1), F32)
    for f in range(per):
        frame = jnp.bitwise_xor(slot + f, scal[T_AT] * (2 * per))
        live = (frame < scal[COUNT_AT]).astype(F32)
        weight = jnp.where((row >= f * whole) & (row < (f + 1) * whole), live, weight)
    dy_out[...] = (xs[...] * weight).astype(BF16)


def cut_kernel(scal, own, peer, b0, b1, b2, b3):
    half, per = own.shape[0], b0.shape[0]
    for r, out in enumerate((b0, b1, b2, b3)):
        first = jnp.bitwise_xor(scal[P_AT], r) * per
        for i in range(per):
            for src, low in ((own, 0), (peer, half)):

                @pl.when((first >= low) & (first < low + half))
                def put(src=src, low=low):
                    out[i] = src[first - low + i]


def join_kernel(scal, b0, b1, b2, b3, own, peer):
    half, per = own.shape[0], b0.shape[0]
    for r, src in enumerate((b0, b1, b2, b3)):
        first = jnp.bitwise_xor(scal[P_AT], r) * per
        for i in range(per):
            for out, low in ((own, 0), (peer, half)):

                @pl.when((first >= low) & (first < low + half))
                def put(out=out, low=low):
                    out[first - low + i] = src[i]


def space_in_kernel(scal, b0, b1, b2, b3, par, w_load, x_out, h_out, qkv_out, xs):
    fill_space((b0, b1, b2, b3), xs)
    gain, shift = par[G_S : G_S + 1, :], par[B_S : B_S + 1, :]

    def rows(r):
        x = xs[r, :]
        x_out[r, :] = x.astype(BF16)
        h_out[r, :] = (normalise(x)[0] * gain + shift).astype(BF16)

    row_blocks(xs.shape[0], rows)
    project_qkv(h_out, w_load.get(), par, C_S, E_S, qkv_out)


def space_windows(rows, per):
    whole = rows // per
    step = whole // 16 * 16
    width = rows - step * (per - 1)
    return whole, step, width


def space_mid_kernel(per, scal, qkv, x, par, w_load, y_out, x2_out, m_out, ys):
    rows = x.shape[0]
    whole, step, width = space_windows(rows, per)
    masks = head_masks()
    ys[...] = jnp.zeros_like(ys)
    key = lax.broadcasted_iota(jnp.int32, (1, width), 1)
    query = lax.broadcasted_iota(jnp.int32, (width, 1), 0)

    def frame(f):
        r = pl.ds(pl.multiple_of(f * step, 16), width)
        first = f * (whole - step)
        keys = (key >= first) & (key < first + whole)
        queries = ((query >= first) & (query < first + whole)).astype(F32)
        for j in range(PAIRS):
            q = qkv[r, j * PAIR : (j + 1) * PAIR]
            k = qkv[r, D + j * PAIR : D + (j + 1) * PAIR]
            v = qkv[r, 2 * D + j * PAIR : 2 * D + (j + 1) * PAIR]
            y = 0.0
            for h in range(2):
                s = jnp.where(keys, dot_nt(q * masks[h], k) * SCALE, MASKED_SCORE)
                y += dot_nn(softmax_rows(s).astype(BF16), v * masks[h])
            ys[r, j * PAIR : (j + 1) * PAIR] += y * queries

    loop(per, frame)
    y_out[...] = ys[...].astype(BF16)
    w = w_load.get()

    def proj(i):
        c = block(i, NB)
        x2_out[:, c] = x[:, c].astype(F32) + (dot_nn(y_out[...], w[:, c]) + par[O_S : O_S + 1, c])

    loop(D // NB, proj)
    gain, shift = par[G_M : G_M + 1, :], par[B_M : B_M + 1, :]

    def norm(r):
        m_out[r, :] = (normalise(x2_out[r, :])[0] * gain + shift).astype(BF16)

    row_blocks(rows, norm)


def mlp_kernel(scal, m, dy, par, w1_load, w2_load, x3_out, dm_out, dw1, dw1_their, dw2, dw2_their, dup, es, das, mt):
    mt[...] = m[...].T
    w1, w2 = w1_load.get(), w2_load.get()

    def hidden(i):
        c = block(i, D)
        a = dot_nn(m[...], w1[:, c]) + par[pl.ds(U_1 + i, 1), :]
        g = dot_nt(dy[...], w2[c, :])
        value, slope = gelu_parts(a)
        da = (g * slope).astype(BF16)
        es[:, c] = value.astype(BF16)
        das[:, c] = da
        dup[pl.ds(i, 1), :] = jnp.sum(da.astype(F32), axis=0, keepdims=True)

    loop(FF // D, hidden)
    weight_grad(mt, das, scal, dw1, dw1_their)
    rows = D // 4

    def down(i):
        value = dot_tn(es[:, block(i, D)], dy[...]).astype(BF16)
        for j in range(4):
            part, to = value[j * rows : (j + 1) * rows, :], slice(j % 2 * D, (j % 2 + 1) * D)

            @pl.when(scal[C_AT] == j // 2)
            def keep(part=part, to=to):
                dw2[block(i, rows), to] = part

            @pl.when(scal[C_AT] != j // 2)
            def send(part=part, to=to):
                dw2_their[block(i, rows), to] = part

    loop(FF // D, down)

    def outs(c):
        x3_out[:, c] = dot_nn(es[...], w2[:, c])
        dm_out[:, c] = dot_nt(das[...], w1[c, :])

    col_blocks(D, outs)


def mlp_out_kernel(per, scal, x2, x3, dm, dy, y, par, w_load, dx2_out, dys_out, dw, dw_their, dvec, b0, b1, b2, b3, xs, yt):
    rows = x2.shape[0]
    here = b0.shape[1]
    gain = par[G_M : G_M + 1, :]
    dvec[...] = jnp.zeros_like(dvec)
    yt[...] = y[...].T

    def back(r):
        xs[r, :] = x2[r, :] + (x3[r, :] + par[U_2 : U_2 + 1, :])
        dz, dg, db = norm_back(x2[r, :], dm[r, :], gain)
        g = dy[r, :].astype(F32)
        dx2 = g + dz
        dx2_out[r, :] = dx2
        low = dx2.astype(BF16)
        dys_out[r, :] = low
        dvec[0:1, :] += dg
        dvec[1:2, :] += db
        dvec[2:3, :] += jnp.sum(g, axis=0, keepdims=True)
        dvec[3:4, :] += jnp.sum(low.astype(F32), axis=0, keepdims=True)

    row_blocks(rows, back)
    for f in range(per):
        for r, out in enumerate((b0, b1, b2, b3)):
            first = f * 4 * here + r * here
            out[f] = xs[first : first + here, :].astype(BF16)

    weight_grad(yt, dys_out, scal, dw, dw_their)
    w = w_load.get()

    def proj(i):
        c = block(i, NB)
        xs[:, c] = dot_nt(dys_out[...], w[c, :])

    loop(D // NB, proj)
    dys_out[...] = xs[...].astype(BF16)


def space_back_kernel(per, scal, qkv, dy, dqkv_out, dvec, acc):
    rows = dy.shape[0]
    whole, step, width = space_windows(rows, per)
    masks = head_masks()
    acc[...] = jnp.zeros_like(acc)
    key = lax.broadcasted_iota(jnp.int32, (1, width), 1)
    query = lax.broadcasted_iota(jnp.int32, (width, 1), 0)

    def frame(f):
        r = pl.ds(pl.multiple_of(f * step, 16), width)
        first = f * (whole - step)
        keys = (key >= first) & (key < first + whole)
        queries = ((query >= first) & (query < first + whole)).astype(F32)
        for j in range(PAIRS):
            cq = slice(j * PAIR, (j + 1) * PAIR)
            ck = slice(D + j * PAIR, D + (j + 1) * PAIR)
            cv = slice(2 * D + j * PAIR, 2 * D + (j + 1) * PAIR)
            q, k, v, g = qkv[r, cq], qkv[r, ck], qkv[r, cv], dy[r, cq]
            dq = dk = dv = 0.0
            for h in range(2):
                qm, km, gm = q * masks[h], k * masks[h], g * masks[h]
                s = jnp.where(keys, dot_nt(qm, k) * SCALE, MASKED_SCORE)
                p = softmax_rows(s) * queries
                dp = dot_nt(gm, v)
                ds = (p * (dp - jnp.sum(p * dp, axis=-1, keepdims=True))).astype(BF16)
                dq += dot_nn(ds, km)
                dk += dot_tn(ds, qm)
                dv += dot_tn(p.astype(BF16), gm)
            acc[r, cq] += dq * SCALE
            acc[r, ck] += dk * SCALE
            acc[r, cv] += dv

    loop(per, frame)
    low = acc[...].astype(BF16)
    dqkv_out[...] = low
    dvec[...] = jnp.zeros_like(dvec)
    dvec[0:1, :] = jnp.sum(dqkv_out[:, :D].astype(F32), axis=0, keepdims=True)
    dvec[1:2, :] = jnp.sum(dqkv_out[:, 2 * D :].astype(F32), axis=0, keepdims=True)


def space_out_kernel(per, scal, dqkv, h, x, dx2, par, w_load, dw, dw_their, dvec, b0, b1, b2, b3, xs, ht):
    rows = x.shape[0]
    here = b0.shape[1]
    ht[...] = h[...].T
    weight_grad(ht, dqkv, scal, dw, dw_their)
    w = w_load.get()

    def proj(c):
        xs[:, c] = dot_nt(dqkv[...], w[c, :])

    col_blocks(D, proj)
    gain = par[G_S : G_S + 1, :]
    dvec[...] = jnp.zeros_like(dvec)

    def back(r):
        dz, dg, db = norm_back(x[r, :].astype(F32), xs[r, :], gain)
        xs[r, :] = dx2[r, :] + dz
        dvec[0:1, :] += dg
        dvec[1:2, :] += db

    row_blocks(rows, back)
    for f in range(per):
        for r, out in enumerate((b0, b1, b2, b3)):
            first = f * 4 * here + r * here
            out[f] = xs[first : first + here, :].astype(BF16)


def time_proj_kernel(scal, b0, b1, b2, b3, y, z, w_load, dx1_out, dy_out, dw, dw_their, dvec, xs, zt, dz):
    per, here = b0.shape[0], b0.shape[1]
    slots = 4 * per
    for r, src in enumerate((b0, b1, b2, b3)):
        first = jnp.bitwise_xor(scal[P_AT], r) * per
        for i in range(per):
            put_slot(xs, first + i, slots, src[i].astype(F32))
    dvec[...] = jnp.zeros_like(dvec)

    def gather_rows(r):
        value = get_rows(xs, r)
        dx1_out[r, :] = value.astype(BF16)
        dvec[0:1, :] += jnp.sum(value, axis=0, keepdims=True)

    row_blocks(xs.shape[1], gather_rows)
    w = w_load.get()

    def proj_f(i):
        c = block(i, NB)
        dz[:, c] = dot_nt(dx1_out[...], w[c, D:]).astype(BF16)

    loop(D // NB, proj_f)

    def proj_o(i):
        c = block(i, NB)
        dy_out[:, c] = dot_nt(dz[...], w[c, :D]).astype(BF16)

    loop(D // NB, proj_o)
    dvec[1:2, :] = jnp.sum(dz[...].astype(F32), axis=0, keepdims=True)

    def put_grad(half, left, right):
        zt[...] = left[...].T

        def cols(out):
            def body(i):
                out[:, block(i, NB)] = dot_nn(zt[...], right[:, block(i, NB)]).astype(BF16)

            loop(D // NB, body)

        pl.when(scal[C_AT] == half)(lambda: cols(dw))
        pl.when(scal[C_AT] != half)(lambda: cols(dw_their))

    put_grad(1, z, dx1_out)
    put_grad(0, y, dz)


def time_attn_back_kernel(slots, scal, qkv, dys, dqkv_out, dvec):
    mask = time_mask(scal, slots)
    masks = head_masks()

    def group(rr):
        for j in range(PAIRS):
            cq = slice(j * PAIR, (j + 1) * PAIR)
            ck = slice(D + j * PAIR, D + (j + 1) * PAIR)
            cv = slice(2 * D + j * PAIR, 2 * D + (j + 1) * PAIR)
            q, k, v, g = qkv[rr, cq], qkv[rr, ck], qkv[rr, cv], dys[rr, cq]
            dq = dk = dv = 0.0
            for hh in range(2):
                qm, km, gm = q * masks[hh], k * masks[hh], g * masks[hh]
                s = jnp.where(mask, dot_nt(qm, k) * SCALE, MASKED_SCORE)
                p = softmax_rows(s)
                dp = dot_nt(gm, v)
                ds = (p * (dp - jnp.sum(p * dp, axis=-1, keepdims=True))).astype(BF16)
                dq += dot_nn(ds, km)
                dk += dot_tn(ds, qm)
                dv += dot_tn(p.astype(BF16), gm)
            dqkv_out[rr, cq] = (dq * SCALE).astype(BF16)
            dqkv_out[rr, ck] = (dk * SCALE).astype(BF16)
            dqkv_out[rr, cv] = dv.astype(BF16)

    row_blocks(dys.shape[0], group)
    dvec[...] = jnp.zeros_like(dvec)
    dvec[0:1, :] = jnp.sum(dqkv_out[:, :D].astype(F32), axis=0, keepdims=True)
    dvec[1:2, :] = jnp.sum(dqkv_out[:, 2 * D :].astype(F32), axis=0, keepdims=True)


def time_out_kernel(
    scal, dqkv, h, x, dx1, par, v_t, v_a, v_n, v_s, v_m, v_u, w_load, own, peer, dw, dw_their, vec, dvec, xs, ht, vs
):
    half, here = own.shape[0], own.shape[1]
    slots = 2 * half
    w = w_load.get()

    def proj(i):
        put_cols(xs, i, dot_nt(dqkv[...], w[block(i, NB), :]))

    loop(D // NB, proj)
    gain = par[G_T : G_T + 1, :]
    dvec[...] = jnp.zeros_like(dvec)

    def back(r):
        dz, dg, db = norm_back(x[r, :].astype(F32), get_rows(xs, r), gain)
        put_rows(xs, r, dx1[r, :].astype(F32) + dz)
        dvec[0:1, :] += dg
        dvec[1:2, :] += db

    row_blocks(xs.shape[1], back)
    for s in range(slots):
        v = get_slot(xs, s, slots, here)
        if s < half:
            own[s] = v
        else:
            peer[s - half] = v.astype(BF16)
    vs[...] = jnp.zeros_like(vs)
    for at, (src, row, count) in enumerate(
        (
            (dvec, 0, 2), (None, 0, 0), (v_a, 0, 2), (None, 0, 0), (v_t, 1, 1), (v_t, 0, 1), (v_n, 0, 2), (None, 0, 0),
            (v_s, 0, 2), (None, 0, 0), (v_m, 3, 1), (v_m, 0, 2), (None, 0, 0), (None, 0, 0), (None, 0, 0), (None, 0, 0),
            (None, 0, 0), (v_m, 2, 1),
        )
    ):
        if src is not None:
            vs[at : at + count, :] = src[row : row + count, :]
    vs[U_1 : U_1 + FF // D, :] = v_u[: FF // D, :]
    vec[...] = vs[...].T.astype(BF16)
    ht[...] = h[...].T
    weight_grad(ht, dqkv, scal, dw, dw_their)


def add_split_kernel(packs, n_after, sel_at, scal, *refs):
    n = len(packs)
    send, keep = refs[2 * n + n_after], refs[2 * n + n_after + 1]
    sel = scal[sel_at]
    for i, (offset, width) in enumerate(packs):
        mine, other = refs[i], refs[n + i]
        for out, which in ((send, 1 - sel), (keep, sel)):
            value = mine[0, which].astype(F32) + other[0, which].astype(F32)
            out[0, :, offset : offset + width] = value.astype(BF16)


def add_split(scal, sel_at, mine, other, packs, rows, after=()):
    n = mine[0].shape[0]
    out = sds((n, rows, sum(w for _, w in packs)), BF16)

    def spec(a):
        return pl.BlockSpec((1,) + a.shape[1:], lambda i: (i, 0, 0, 0))

    return pl.pallas_call(
        functools.partial(add_split_kernel, packs, len(after), sel_at),
        grid=(n,),
        out_shape=(out, out),
        in_specs=[pl.BlockSpec(memory_space=pltpu.SMEM)]
        + [spec(a) for a in [*mine, *other]]
        + [pl.BlockSpec(memory_space=pl.ANY)] * len(after),
        out_specs=tuple(pl.BlockSpec((1, *out.shape[1:]), lambda i: (i, 0, 0)) for _ in range(2)),
        compiler_params=pltpu.CompilerParams(vmem_limit_bytes=SMALL_VMEM),
        cost_estimate=cost(2),
    )(scal, *mine, *other, *after)


def adam_update(weight, grad, moment, square, decay, factor, rate):
    grad = grad * factor
    moment = BETA_FIRST * moment + (1.0 - BETA_FIRST) * grad
    square = BETA_SECOND * square + (1.0 - BETA_SECOND) * grad * grad
    moment_hat = moment * (1.0 / (1.0 - BETA_FIRST**STEP))
    square_hat = square * (1.0 / (1.0 - BETA_SECOND**STEP))
    fresh = weight - rate * (moment_hat / (jnp.sqrt(square_hat) + ADAM_EPSILON) + decay * weight)
    return (fresh, moment, square)


PLANE = ("tm", "pos")
EVERY = ("dp", "tm", "pos")


def pos_permute(a, r):
    n = lax.axis_size("pos")
    return lax.ppermute(a, "pos", [(i, i ^ r) for i in range(n)]) if r else a


def tm_permute(a):
    n = lax.axis_size("tm")
    return lax.ppermute(a, "tm", [(i, n - 1 - i) for i in range(n)])


def grid_permute(a, move):
    pairs = []
    for z in range(4):
        for x in range(2):
            for p in range(4):
                zz, xx, pp = move(z, x, p)
                pairs.append(((z * 2 + x) * 4 + p, (zz * 2 + xx) * 4 + pp))
    return lax.ppermute(a, EVERY, pairs)


def next_plane(a):
    return grid_permute(a, lambda z, x, p: (z ^ 1, x, p))


def far_plane(a):
    return grid_permute(a, lambda z, x, p: (z ^ 3, x, p))


def first_side(a):
    return grid_permute(a, lambda z, x, p: (z, x, p ^ 2) if p & 1 else (z, x ^ 1, p))


def second_side(a):
    return grid_permute(a, lambda z, x, p: (z, x ^ 1, p) if p & 1 else (z, x, p ^ 2))


def other_core(a):
    return grid_permute(a, lambda z, x, p: (z, x, p ^ 1))


def spread_plane(part):
    side = first_side(part)
    far, both = second_side(part), second_side(side)
    own = [part, side, far, both]
    return own + [other_core(a) for a in own]


def once(value, *others):
    return lax.optimization_barrier((value, *others))[0]


def gather_lines(piece):
    near = next_plane(piece)
    return [near, far_plane(piece), far_plane(near)]


class Group:
    def __init__(self, scal, members):
        self.scal, self.members, self.packs, at = scal, members, [], 0
        for mine, _ in members:
            self.packs.append((at, mine.shape[1]))
            at += mine.shape[1]
        self.width = at
        self.received = [other_core(t) for _, t in members]

    def add(self, mine, theirs):
        self.members = self.members + [(mine, theirs)]
        self.packs.append((self.width, mine.shape[1]))
        self.width += mine.shape[1]
        self.received = self.received + [other_core(theirs)]

    def chip(self, *after):
        mine = [m.reshape(4, 2, -1, m.shape[1]) for m, _ in self.members]
        other = [r.reshape(4, 2, -1, r.shape[1]) for r in self.received]
        self.send, self.keep = add_split(self.scal, A_AT, mine, other, self.packs, 2 * PIECE, after)
        self.received = first_side(self.send)

    def step(self, sel, shape, rows, move, after):
        shape = (*shape, self.width)
        self.send, self.keep = add_split(
            self.scal, sel, [self.keep.reshape(shape)], [self.received.reshape(shape)], [(0, self.width)], rows, after
        )
        self.received = move(self.send)

    def side(self, *after):
        self.step(B_AT, (4, 2, PIECE), PIECE, second_side, after)

    def plane(self, *after):
        self.step(PAIR_AT, (1, 2, 2 * PIECE), 2 * PIECE, far_plane, after)

    def pair(self, *after):
        self.step(ODD_AT, (1, 2, PIECE), PIECE, next_plane, after)

    def total(self):
        return (self.keep[0].astype(F32) + self.received[0].astype(F32)).astype(BF16)


def adam_kernel(jobs, n_arrays, scal, factor, *refs):
    arrays, refs = refs[:n_arrays], refs[n_arrays:]
    ins, outs, grads, sems = refs[:9], refs[9:19], refs[19:22], refs[22]
    step, scale = pl.program_id(0), factor[0]

    @pl.when(step == 0)
    def bring():
        copies = []
        for start, offset, width, to_grad, firsts in jobs:
            for k in range(8):
                half = scal[C_AT] if k < 4 else 1 - scal[C_AT]
                quarter = scal[Q_AT + k] * PIECE
                each = width // len(firsts)
                for j, (low, high) in enumerate(firsts):
                    src = arrays[start + k].at[:, offset + j * each : offset + (j + 1) * each]
                    if to_grad == 1:
                        rows = pl.ds(pl.multiple_of(low + half * (high - low) + quarter, 16), PIECE)
                        to = grads[1].at[rows, :]
                    else:
                        rows = pl.ds(pl.multiple_of(quarter, 16), PIECE)
                        to = grads[to_grad].at[rows, pl.ds(pl.multiple_of(low + half * (high - low), 128), each)]
                    copies.append(pltpu.make_async_copy(src, to, sems.at[len(copies)]))
        for c in copies:
            c.start()
        for c in copies:
            c.wait()
        g = grads[2][:, :LANES].astype(F32).T[: ins[6].shape[0], :]
        fresh = adam_update(ins[6][...], g, ins[7][...], ins[8][...], 0.0, scale, LEARN_RATE_VEC)
        for out, value in zip(outs[6:9], fresh):
            out[...] = value
        outs[9][...] = g[U_2 : U_2 + 1, :] * scale

    for i, grad in enumerate(grads[:2]):
        weight, moment, square = ins[3 * i : 3 * i + 3]
        size = weight.shape[0]
        g = grad[pl.ds(pl.multiple_of(step * size, 16), size), :].astype(F32)
        fresh = adam_update(weight[...], g, moment[...], square[...], WEIGHT_DECAY, scale, LEARN_RATE)
        for out, value in zip(outs[3 * i : 3 * i + 3], fresh):
            out[...] = value


def adam_all(scal, factor, arrays, jobs, blocks, wide, tall, vec):
    anywhere = pl.BlockSpec(memory_space=pl.ANY)
    smem = pl.BlockSpec(memory_space=pltpu.SMEM)
    both = [*wide, *tall]
    specs = [pl.BlockSpec((v.shape[0] // blocks, v.shape[1]), lambda i: (i, 0)) for v in both]
    specs += [pl.BlockSpec(v.shape, lambda i: (0, 0)) for v in vec]
    both = both + list(vec)
    shard = vec[0].shape[1]
    return pl.pallas_call(
        functools.partial(adam_kernel, jobs, len(arrays)),
        grid=(blocks,),
        out_shape=tuple(sds(v.shape, F32) for v in both) + (sds((1, shard), F32),),
        in_specs=[smem, smem] + [anywhere] * len(arrays) + specs,
        out_specs=(*specs, pl.BlockSpec((1, shard), lambda i: (0, 0))),
        scratch_shapes=[
            pltpu.VMEM(wide[0].shape, BF16),
            pltpu.VMEM(tall[0].shape, BF16),
            pltpu.VMEM((shard, 2 * LANES), BF16),
            pltpu.SemaphoreType.DMA((sum(8 * len(j[4]) for j in jobs),)),
        ],
        compiler_params=pltpu.CompilerParams(vmem_limit_bytes=VMEM_LIMIT),
        cost_estimate=cost(25),
    )(scal, factor, *arrays, *both)


def shards(
    tokens,
    cotangent,
    frame_counts,
    weight_in,
    weight_out,
    vectors,
    moment_in,
    moment_out,
    moment_vec,
    square_in,
    square_out,
    square_vec,
):
    clips, half, here, _ = tokens.shape
    tm, n_pos, n_dp = lax.axis_size("tm"), lax.axis_size("pos"), lax.axis_size("dp")
    slots = half * tm
    per = slots // n_pos
    rows = slots * here
    t, p, z = lax.axis_index("tm"), lax.axis_index("pos"), lax.axis_index("dp")
    count = lax.dynamic_index_in_dim(frame_counts, t, keepdims=False)
    line = n_dp == 4
    core = p % 2 if line else 0
    a = jnp.where(core == 0, t, p // 2)
    b = jnp.where(core == 0, p // 2, t)
    quarters = [2 * a + b, 2 * (1 - a) + b, 2 * a + 1 - b, 2 * (1 - a) + 1 - b]
    quarters += [2 * b + a, 2 * (1 - b) + a, 2 * b + 1 - a, 2 * (1 - b) + 1 - a]
    scal = jnp.stack([count, t, p, z, core, *quarters, a, b, z // 2, z % 2]).astype(jnp.int32)

    own_tokens, peer_tokens, own_cot, peer_cot = (
        lax.dynamic_index_in_dim(v, at, keepdims=False) for v in (tokens, cotangent) for at in (t, 1 - t)
    )
    low_in, low_out = weight_in.astype(BF16), weight_out.astype(BF16)
    vec_low = jnp.pad(vectors.astype(BF16), ((0, 0), (0, LANES - vectors.shape[1])))
    vec_low = jnp.concatenate([vec_low, vec_low], axis=1)

    spans = {"at": (0, 3 * D), "ot": (3 * D, 2 * D), "as": (5 * D, 3 * D), "os": (8 * D, D)}

    def whole(low, *after):
        part = low.shape[0] // (tm * n_pos)
        mine = once(lax.dynamic_slice_in_dim(low, (t * n_pos + p) * part, part, axis=0), *after)
        return lax.all_gather(mine, EVERY, axis=0, tiled=True)

    blk = sds((per, here, D), BF16)
    act = sds((rows, D), BF16)
    wide = sds((rows, 3 * D), BF16)
    full = sds((rows, D), F32)
    par_out = sds((VROWS, D), F32)
    vec_out = sds((8, D), F32)
    scr = pltpu.VMEM((rows, D), F32)
    scr_tiled = pltpu.VMEM((TILES, rows, LANES), F32)
    scr_low = pltpu.VMEM((rows, D), BF16)
    scr_hidden = pltpu.VMEM((rows, FF), BF16)
    scr_t = pltpu.VMEM((D, rows), BF16)

    def halves(cols, height=D):
        return [sds((height, cols), BF16)] * 2

    after_in = after_attn = after_mid = after_space = ()
    if line:
        quarter = lax.dynamic_slice_in_dim(weight_in, quarters[0] * PIECE, PIECE, axis=0)
        vec_quarter = lax.dynamic_slice_in_dim(vec_low[:, :LANES], quarters[0] * PIECE, PIECE, axis=0)

        def half_of(first, width):
            return lax.dynamic_slice_in_dim(quarter, first + core * (width // 2), width // 2, axis=1).astype(BF16)

        def lines(piece, near):
            return [near, far_plane(piece), far_plane(near)]

        def sides(first):
            return first_side(first), second_side(first)

        def cores(group):
            return group + [other_core(v) for v in group]

        piece_0 = jnp.concatenate([half_of(*spans["at"]), vec_quarter], axis=1)
        near_0 = next_plane(piece_0)
        lines_0 = lines(piece_0, near_0)
        peer_tokens = tm_permute(peer_tokens)
        piece_1 = half_of(*spans["ot"])
        piece_2 = jnp.concatenate([half_of(*spans[name]) for name in ("as", "os")], axis=1)
        first_0 = jnp.stack(
            once(lines_0, peer_tokens, low_in, low_out, vec_low, own_tokens, scal, piece_1, piece_2)
        )
        side_0, far_0 = sides(first_0)
        up_all, down_all = whole(low_in[:, 9 * D :], first_0), whole(low_out, first_0)
        piece_1 = once(piece_1, first_0)
        near_1 = next_plane(piece_1)
        both_0 = second_side(side_0)
        lines_1 = lines(once(piece_1, far_0, near_1), once(near_1, far_0))
        group_0 = cores([first_0, side_0, far_0, both_0])
        peer_cot = tm_permute(once(peer_cot, both_0))
        first_1 = jnp.stack(once(lines_1, both_0))
        side_1, far_1 = sides(first_1)
        near_2 = next_plane(once(piece_2, first_1))
        w_at = Weight(3 * D, shard=low_in, blocks=[spans["at"]], pieces=group_0)
        w_vec = Weight(2 * LANES, shard=vec_low, blocks=[(0, 2 * LANES)], pieces=group_0, offset=3 * D // 2)
        after_in = (first_1,)
    else:
        peer_tokens, peer_cot = tm_permute(peer_tokens), tm_permute(peer_cot)

        w_at, w_ot, w_as, w_os = (
            Weight(width, whole=whole(low_in[:, first : first + width])) for first, width in spans.values()
        )
        up_all, down_all = whole(low_in[:, 9 * D :]), whole(low_out)
        w_vec = Weight(2 * LANES, whole=lax.all_gather(vec_low, "dp", axis=0, tiled=True))

    x, h_t, qkv_t, par = call(
        time_in_kernel, scal, [own_tokens, peer_tokens], [w_at, w_vec], [act, act, wide, par_out], [scr_tiled], after_in
    )
    if line:
        both_1 = second_side(once(side_1, h_t))
        lines_2 = lines(once(piece_2, h_t, near_2), once(near_2, h_t))
        after_attn = (near_2, side_1, peer_cot)
    (y_t,) = call(functools.partial(time_attn_kernel, slots), scal, [qkv_t], [], [act], [], after_attn)
    if line:
        group_1 = cores(once([first_1, side_1, far_1, both_1], y_t))
        w_ot = Weight(2 * D, shard=low_in, blocks=[spans["ot"]], pieces=group_1)
        first_2 = jnp.stack(once(lines_2, y_t))
        side_2, far_2 = sides(first_2)
        after_mid = (first_2,)
    z_t, *x1 = call(time_mid_kernel, scal, [y_t, x, par], [w_ot], [act, blk, blk, blk, blk], [scr_tiled], after_mid)
    x1 = [pos_permute(v, r) for r, v in enumerate(x1)]
    cot = call(cut_kernel, scal, [own_cot, peer_cot], [], [blk] * 4, [], (z_t,))
    if line:
        both_2 = second_side(once(side_2, z_t))
        group_2 = cores([first_2, side_2, far_2, both_2])
        w_as = Weight(3 * D, shard=low_in, blocks=[spans["as"]], pieces=group_2)
        w_os = Weight(D, shard=low_in, blocks=[spans["os"]], pieces=group_2, offset=3 * D // 2)
        after_space = (cot[0],)

    x1, h_s, qkv_s = call(space_in_kernel, scal, [*x1, par], [w_as], [act, act, wide], [scr], after_space)
    cot = [pos_permute(once(v, h_s), r) for r, v in enumerate(cot)]
    y_s, x2, m = call(
        functools.partial(space_mid_kernel, per), scal, [qkv_s, x1, par], [w_os], [act, full, act], [scr]
    )
    (dy,) = call(cot_kernel, scal, cot, [], [act], [scr], (m,))

    x3, dm, g_1, g_1t, g_2, g_2t, v_u = call(
        mlp_kernel,
        scal,
        [m, dy, par],
        [Weight(FF, whole=up_all), Weight(D, rows=FF, whole=down_all)],
        [full, full, *halves(FF // 2), *halves(FF // 2), vec_out],
        [scr_hidden, scr_hidden, scr_t],
    )
    if line:
        group_a = Group(scal, [(g_1, g_1t), (g_2, g_2t)])
    dx2, dys, g_os, g_ost, v_m, *out = call(
        functools.partial(mlp_out_kernel, per),
        scal,
        [x2, x3, dm, dy, y_s, par],
        [w_os],
        [full, act, *halves(D // 2), vec_out, blk, blk, blk, blk],
        [scr, scr_t],
    )

    wait = ()
    if line:
        group_a.chip(v_m)
        wait = (group_a.send,)
    dqkv_s, v_s = call(
        functools.partial(space_back_kernel, per),
        scal,
        [qkv_s, dys],
        [],
        [wide, vec_out],
        [pltpu.VMEM((rows, 3 * D), F32)],
        wait,
    )
    g_as, g_ast, v_n, *dx1 = call(
        functools.partial(space_out_kernel, per),
        scal,
        [dqkv_s, h_s, x1, dx2, par],
        [w_as],
        [*halves(3 * D // 2), vec_out, blk, blk, blk, blk],
        [scr, scr_t],
    )
    dx1 = [pos_permute(v, r) for r, v in enumerate(dx1)]

    if line:
        group_s = Group(scal, [(g_os, g_ost), (g_as, g_ast)])
        group_a.side(*dx1[1:])
        wait = (group_a.send,)
    dx1, dy_t, g_ot, g_ott, v_t = call(
        time_proj_kernel,
        scal,
        [*dx1, y_t, z_t],
        [w_ot],
        [act, act, *halves(D), vec_out],
        [scr_tiled, scr_t, scr_low],
        wait,
    )
    if line:
        group_s.add(g_ot, g_ott)
        group_a.plane(v_t)
        group_s.chip(group_a.send)
        wait = (group_s.send,)
    out = [pos_permute(once(v, v_t), r) for r, v in enumerate(out)]
    dqkv_t, v_a = call(
        functools.partial(time_attn_back_kernel, slots), scal, [qkv_t, dy_t], [], [wide, vec_out], [], wait
    )
    out_own, out_peer = call(join_kernel, scal, out, [], [sds((half, here, D), BF16)] * 2, [], (v_a,))
    if line:
        group_s.side(v_a)
        group_a.pair(v_a)
        wait = (group_s.send, group_a.send, out_own)
    out_peer = tm_permute(out_peer)
    mine = (jnp.arange(clips, dtype=jnp.int32) == t)[:, None, None, None]
    grad_own, grad_peer, g_at, g_att, g_vec, _ = call(
        time_out_kernel,
        scal,
        [dqkv_t, h_t, x, dx1, par, v_t, v_a, v_n, v_s, v_m, v_u],
        [w_at],
        [
            sds((half, here, D), F32),
            sds((half, here, D), BF16),
            *halves(3 * D // 2),
            sds((D, LANES), BF16),
            vec_out,
        ],
        [scr_tiled, scr_t, pltpu.VMEM((LANES, D), F32)],
        wait,
    )
    if line:
        group_t = Group(scal, [(g_at, g_att), (g_vec, g_vec)])
        group_t.chip()
        group_s.plane(group_t.send)
        sum_a = group_a.total()
        group_t.side()
        group_s.pair(group_t.send)
        group_t.plane()
        sum_s = group_s.total()
        parts = spread_plane(once(sum_a, group_t.send)) + spread_plane(once(sum_s, group_t.send))
        grad_peer = once(grad_peer, group_t.send)
        block_out = once(jnp.where(mine, out_own[None], out_peer[None]), group_t.send)
        group_t.pair()
        sum_t = group_t.total()
        sums = [sum_a, sum_s, sum_t]
        parts = [*parts, *spread_plane(sum_t)]
    else:
        block_out = jnp.where(mine, out_own[None], out_peer[None])
    grad_peer = tm_permute(grad_peer).astype(F32)
    input_grad = jnp.where(mine, grad_own[None], grad_peer[None])

    if line:
        square_sums = []
        for total in sums[:-1]:
            total = total.astype(F32)
            square_sums.append(jnp.sum(total * total))
        last = sums[-1].astype(F32)
        vec_at = group_t.width - LANES
        alone = jnp.where(core == 0, last[:, vec_at:], 0.0)
        square_sums += [jnp.sum(last[:, :vec_at] * last[:, :vec_at]), jnp.sum(alone * alone)]
        total_square = jnp.broadcast_to(sum(square_sums), (8, LANES))
        for move in (next_plane, far_plane, first_side, second_side, other_core):
            total_square = total_square + move(total_square)
        total_square = total_square[0, 0]
    else:
        g_in = jnp.concatenate([g_at, g_att, g_ot, g_ott, g_as, g_ast, g_os, g_ost, g_1, g_1t], axis=1)
        g_out = jnp.concatenate([g_2, g_2t], axis=1).reshape(4, D // 4, 4, D).transpose(0, 2, 1, 3).reshape(FF, D)
        g_vec = g_vec[:, : vectors.shape[1]]

        def reduced(grad):
            mine_rows = lax.psum_scatter(grad, "dp", scatter_dimension=0, tiled=True)
            return lax.psum(mine_rows, PLANE).astype(F32)

        g_in, g_out, g_vec = reduced(g_in), reduced(g_out), reduced(g_vec)
        local_square = jnp.sum(g_in * g_in) + jnp.sum(g_out * g_out) + jnp.sum(g_vec * g_vec)
        total_square = lax.psum(local_square, "dp")

    grad_norm = jnp.sqrt(total_square)
    factor = CLIP_NORM / jnp.maximum(grad_norm, CLIP_NORM)
    wide_in, tall_in = (weight_in, moment_in, square_in), (weight_out, moment_out, square_out)
    vec_in = (vectors, moment_vec, square_vec)
    if line:

        def span(name):
            first, width = spans[name]
            return ((first, first + width // 2),)

        shard = weight_out.shape[0]
        jobs = [
            (0, *group_a.packs[0], 0, ((9 * D, 9 * D + FF // 2),)),
            (0, *group_a.packs[1], 1, ((0, shard // 2), (shard // 4, shard // 4 * 3))),
        ]
        for name, (offset, width) in zip(("os", "as", "ot"), group_s.packs):
            jobs.append((8, offset, width, 0, span(name)))
        jobs.append((16, *group_t.packs[0], 0, span("at")))
        jobs.append((16, *group_t.packs[1], 2, ((0, LANES),)))
        fresh = adam_all(scal, factor.reshape(1), parts, jobs, 12, wide_in, tall_in, [v.T for v in vec_in])
        *fresh, new_v, first_v, second_v, bias_down = fresh
        fresh += [new_v.T, first_v.T, second_v.T]
        bias_down_grad = bias_down.reshape(-1)
    else:
        fresh = [
            *adam_update(weight_in, g_in, moment_in, square_in, WEIGHT_DECAY, factor, LEARN_RATE),
            *adam_update(weight_out, g_out, moment_out, square_out, WEIGHT_DECAY, factor, LEARN_RATE),
            *adam_update(vectors, g_vec, moment_vec, square_vec, 0.0, factor, LEARN_RATE_VEC),
        ]
        bias_down_grad = g_vec[:, U_2] * factor
    new_in, first_in, second_in, new_out, first_out, second_out, new_vec, first_vec, second_vec = fresh
    return (
        block_out,
        input_grad,
        grad_norm,
        new_in,
        new_out,
        new_vec,
        first_in,
        first_out,
        first_vec,
        second_in,
        second_out,
        second_vec,
        bias_down_grad,
    )


def solution(mesh):
    acts, rows = P("dp", "tm", "pos", None), P("dp", None)
    return jax.shard_map(
        shards,
        mesh=mesh,
        in_specs=(acts, acts, P("dp"), *[rows] * 9),
        out_specs=(acts, acts, P(), *[rows] * 9, P("dp")),
        check_vma=False,
    )
```

```python
import functools

import jax
import jax.numpy as jnp
from jax import lax
from jax.experimental import pallas as pl
from jax.experimental.pallas import tpu as pltpu
from jax.sharding import PartitionSpec as P

HEADS = 12
HD = 64
D = 768
FF = 3072
STEP = 10

NORM_EPSILON = 1e-06
CLIP_NORM = 1.0
LEARN_RATE = 0.03
LEARN_RATE_VEC = 0.25
BETA_FIRST = 0.9
BETA_SECOND = 0.999
ADAM_EPSILON = 1e-08
WEIGHT_DECAY = 0.05
MASKED_SCORE = -1e30
SCALE = HD ** (-0.5)

F32 = jnp.float32
BF16 = jnp.bfloat16
PAIR = 2 * HD
PAIRS = D // PAIR
NB = 256
ROWB = 112
WINDOW = 128
VMEM_LIMIT = 56 * 1024 * 1024
SMALL_VMEM = 16 * 1024 * 1024
SPARE_VMEM = 4 * 1024 * 1024
ADAM_VMEM = 20 * 1024 * 1024

G_T, B_T, C_T, E_T, O_T, F_T, G_S, B_S, C_S, E_S, O_S, G_M, B_M, U_1, U_2 = (
    0, 1, 2, 3, 4, 5, 6, 7, 8, 9, 10, 11, 12, 13, 17,
)


COUNT_AT, T_AT, P_AT, Z_AT, C_AT, Q_AT = 0, 1, 2, 3, 4, 5
A_AT, B_AT, PAIR_AT, ODD_AT = 13, 14, 15, 16
OTHERS = (1, 3, 2)
PIECE = 48
VROWS = 24


def dot_nn(a, b):
    return lax.dot_general(a, b, (((1,), (0,)), ((), ())), preferred_element_type=F32)


def dot_nt(a, b):
    return lax.dot_general(a, b, (((1,), (1,)), ((), ())), preferred_element_type=F32)


def dot_tn(a, b):
    return lax.dot_general(a, b, (((0,), (0,)), ((), ())), preferred_element_type=F32)


def loop(count, body, unroll=1):
    def step(i, carry):
        body(i)
        return carry

    lax.fori_loop(0, count, step, 0, unroll=unroll)


def block(i, size):
    return pl.ds(pl.multiple_of(i * size, size), size)


def row_blocks(rows, body):
    loop(rows // ROWB, lambda i: body(pl.ds(pl.multiple_of(i * ROWB, 16), ROWB)))


def col_blocks(cols, body):
    loop(cols // NB, lambda i: body(block(i, NB)))


LANES = 128
TILES = D // LANES


def put_slot(xs, s, slots, value):
    for j in range(TILES):
        xs[j, pl.ds(s, value.shape[0], stride=slots), :] = value[:, j * LANES : (j + 1) * LANES]


def get_slot(xs, s, slots, count):
    return jnp.concatenate([xs[j, pl.ds(s, count, stride=slots), :] for j in range(TILES)], axis=1)


def get_rows(xs, r):
    return jnp.concatenate([xs[j, r, :] for j in range(TILES)], axis=1)


def put_rows(xs, r, value):
    for j in range(TILES):
        xs[j, r, :] = value[:, j * LANES : (j + 1) * LANES]


def put_cols(xs, i, value):
    per = NB // LANES
    for j in range(per):
        xs[i * per + j] = value[:, j * LANES : (j + 1) * LANES]


def normalise(x):
    centred = x - jnp.mean(x, axis=-1, keepdims=True)
    variance = jnp.mean(centred * centred, axis=-1, keepdims=True)
    inverse = lax.rsqrt(variance + NORM_EPSILON)
    return centred * inverse, inverse


def norm_back(x, grad, gain):
    z_hat, inverse = normalise(x)
    h = grad * gain
    first = jnp.mean(h, axis=-1, keepdims=True)
    second = jnp.mean(h * z_hat, axis=-1, keepdims=True)
    dz = inverse * (h - first - z_hat * second)
    return dz, jnp.sum(grad * z_hat, axis=0, keepdims=True), jnp.sum(grad, axis=0, keepdims=True)


def head_masks():
    lane = lax.broadcasted_iota(jnp.int32, (1, PAIR), 1)
    return [(lane < HD).astype(BF16), (lane >= HD).astype(BF16)]


def gelu_parts(a):
    z = jnp.abs(a) * 0.7071067811865476
    t = 1.0 / (1.0 + 0.3275911 * z)
    e = jnp.exp(-z * z)
    poly = t * (0.254829592 + t * (-0.284496736 + t * (1.421413741 + t * (-1.453152027 + t * 1.061405429))))
    tail = 0.5 * poly * e
    phi_low = jnp.where(a < 0.0, tail, 1.0 - tail)
    return a * phi_low, phi_low + a * (0.3989422804014327 * e)


class Weight:
    def __init__(self, cols, rows=D, whole=None, shard=None, blocks=None, pieces=(), offset=0):
        self.rows, self.cols, self.whole, self.offset = rows, cols, whole, offset
        self.blocks = blocks
        self.arrays = [whole] if whole is not None else [shard, *pieces]

    def scratch(self):
        count = 1 if self.whole is not None else len(self.blocks) + 8 * len(OTHERS)
        return [pltpu.VMEM((self.rows, self.cols), BF16), pltpu.SemaphoreType.DMA((count,))]

    def copies(self, refs, scal, dst, sems):
        if self.whole is not None:
            return [pltpu.make_async_copy(refs[0].at[:, self.offset : self.offset + self.cols], dst, sems.at[0])]
        shard = self.rows // 4
        z, c = scal[Z_AT], scal[C_AT]
        own_rows = pl.ds(pl.multiple_of(z * shard, 16), shard)
        out, at = [], 0
        for first, size in self.blocks:
            src, to = refs[0].at[:, first : first + size], dst.at[own_rows, at : at + size]
            at += size
            out.append(pltpu.make_async_copy(src, to, sems.at[len(out)]))
        width = self.cols // 2
        for k in range(8):
            half = c if k < 4 else 1 - c
            quarter = scal[Q_AT + k]
            for j, m in enumerate(OTHERS):
                row = jnp.bitwise_xor(z, m) * shard + quarter * PIECE
                col = pl.multiple_of(half * width, 128)
                src = refs[1 + k].at[j, :, self.offset : self.offset + width]
                to = dst.at[pl.ds(pl.multiple_of(row, 16), PIECE), pl.ds(col, width)]
                out.append(pltpu.make_async_copy(src, to, sems.at[len(out)]))
        return out


class Loaded:
    def __init__(self, ref, copies):
        self.ref, self.copies, self.waited = ref, copies, False

    def get(self):
        if not self.waited:
            for c in self.copies:
                c.wait()
            self.waited = True
        return self.ref


def sds(shape, dtype):
    return jax.ShapeDtypeStruct(shape, dtype)


def cost(microseconds):
    return pl.CostEstimate(flops=int(microseconds * 1e9), bytes_accessed=0, transcendentals=0)


COSTS = {"join": 20, "cut": 20, "cot": 20}


def call(kernel, scal, ins, weights, outs, scratch=(), after=(), anywhere=(), left=()):
    n_in, n_out, n_scr = len(ins), len(outs), len(scratch)
    arrays = [a for w in weights for a in w.arrays]
    n_left = len(left)

    def body(scal_ref, *refs):
        in_refs, refs = refs[: n_in + n_left], refs[n_in + n_left :]
        array_refs, refs = refs[: len(arrays)], refs[len(arrays) + len(after) :]
        out_refs, refs = refs[:n_out], refs[n_out:]
        own, refs = refs[:n_scr], refs[n_scr:]
        loaded, at = [], 0
        for i, w in enumerate(weights):
            dst, sems = refs[2 * i : 2 * i + 2]
            copies = w.copies(array_refs[at : at + len(w.arrays)], scal_ref, dst, sems)
            at += len(w.arrays)
            for c in copies:
                c.start()
            loaded.append(Loaded(dst, copies))
        kernel(scal_ref, *in_refs, *loaded, *out_refs, *own)
        for w in loaded:
            w.get()

    in_vmem = pl.BlockSpec(memory_space=pltpu.VMEM)
    def padded(v):
        lead = 1
        for n in v.shape[:-2]:
            lead *= n
        return lead * (-(-v.shape[-2] // 16) * 16) * (-(-v.shape[-1] // LANES) * LANES) * jnp.dtype(v.dtype).itemsize

    held = [v for v in scratch if v.dtype in (BF16, F32)]
    used = sum(padded(v) for v in held) + sum(w.rows * w.cols * 2 for w in weights)
    limit = used + SPARE_VMEM
    name = getattr(kernel, "func", kernel).__name__.removesuffix("_kernel")
    return pl.pallas_call(
        body,
        name=name,
        out_shape=tuple(outs),
        in_specs=[pl.BlockSpec(memory_space=pltpu.SMEM)]
        + [in_vmem] * n_in
        + [pl.BlockSpec(memory_space=pltpu.HBM)] * n_left
        + [pl.BlockSpec(memory_space=pl.ANY)] * (len(arrays) + len(after)),
        out_specs=tuple(pl.BlockSpec(memory_space=pltpu.HBM) if i in anywhere else in_vmem for i in range(n_out)),
        scratch_shapes=list(scratch) + [x for w in weights for x in w.scratch()],
        compiler_params=pltpu.CompilerParams(vmem_limit_bytes=limit),
        cost_estimate=cost(COSTS.get(name, 0)),
    )(scal, *ins, *left, *arrays, *after)


def grad_cols(width, body):
    loop(width // NB, lambda i: body(pl.multiple_of(i * NB, NB), NB))
    if width % NB:
        body(width - width % NB, width % NB)


def weight_grad(left_t, right, scal, mine, theirs):
    width = mine.shape[1]
    for out, half in ((theirs, 1 - scal[C_AT]), (mine, scal[C_AT])):

        def body(at, size, out=out, half=half):
            c = pl.ds(pl.multiple_of(half * width + at, 128), size)
            out[:, pl.ds(at, size)] = dot_nn(left_t[...], right[:, c]).astype(BF16)

        grad_cols(width, body)


def stack_heads(a, masks):
    return jnp.concatenate([a * masks[0], a * masks[1]], axis=0)


def softmax_cols(scores):
    e = jnp.exp(scores - jnp.max(scores, axis=0, keepdims=True))
    return e * (1.0 / jnp.sum(e, axis=0, keepdims=True))


def pair_cols(j):
    return [slice(part * D + j * PAIR, part * D + (j + 1) * PAIR) for part in range(3)]


def pair_probs(q, kk, bias):
    size = q.shape[0]
    s = dot_nt(kk, q)
    return [softmax_cols(s[h * size : (h + 1) * size] + bias) for h in range(2)]


def pair_forward(q, k, v, bias, masks):
    p = pair_probs(q * BF16(SCALE), stack_heads(k, masks), bias)
    return dot_tn(jnp.concatenate(p, axis=0).astype(BF16), stack_heads(v, masks))


def pair_backward(q, k, v, g, bias, masks, valid=None):
    size = q.shape[0]
    q = q * BF16(SCALE)
    kk, vv = stack_heads(k, masks), stack_heads(v, masks)
    p = pair_probs(q, kk, bias)
    dp = dot_nt(vv, g)
    ds = []
    for h in range(2):
        if valid is not None:
            p[h] = p[h] * valid
        d = dp[h * size : (h + 1) * size]
        ds.append(p[h] * (d - jnp.sum(p[h] * d, axis=0, keepdims=True)))
    ds = jnp.concatenate(ds, axis=0).astype(BF16)
    pp = jnp.concatenate(p, axis=0).astype(BF16)
    dq = dot_tn(ds, kk) * SCALE
    dk, dv = dot_nn(ds, q), dot_nn(pp, g)
    first = lax.broadcasted_iota(jnp.int32, (1, PAIR), 1) < HD
    return dq, jnp.where(first, dk[:size], dk[size:]), jnp.where(first, dv[:size], dv[size:])


def time_bias(scal, slots, size):
    row = lax.broadcasted_iota(jnp.int32, (size, size), 0)
    col = lax.broadcasted_iota(jnp.int32, (size, size), 1)
    frame = jnp.bitwise_xor(row % slots, scal[T_AT] * (slots // 2))
    return jnp.where((row // slots == col // slots) & (frame < scal[COUNT_AT]), 0.0, MASKED_SCORE)


def time_windows(rows, slots, scal, body):
    masks = head_masks()
    bias = time_bias(scal, slots, WINDOW)
    loop(rows // WINDOW, lambda i: body(block(i, WINDOW), bias, masks))
    left = rows % WINDOW
    if left:
        body(pl.ds(rows - left, left), time_bias(scal, slots, left), masks)


def project_qkv(h, w, par, q_row, v_row, out):
    for part, row in enumerate((q_row, None, v_row)):

        def cols(i, part=part, row=row):
            c = pl.ds(pl.multiple_of(part * D + i * NB, NB), NB)
            value = dot_nn(h[...], w[:, c])
            if row is not None:
                value = value + par[row : row + 1, block(i, NB)]
            out[:, c] = value.astype(BF16)

        loop(D // NB, cols)


def time_in_kernel(scal, own, peer, w_load, vec_load, x_out, h_out, qkv_out, par, xs):
    half, here = own.shape[0], own.shape[1]
    slots = 2 * half
    for s in range(slots):
        src = own if s < half else peer
        put_slot(xs, s, slots, src[s % half].astype(F32))
    vec = vec_load.get()
    par[...] = vec[:, :LANES].astype(F32).T[:VROWS, :]
    gain, shift = par[G_T : G_T + 1, :], par[B_T : B_T + 1, :]

    def rows(r):
        x = get_rows(xs, r)
        x_out[r, :] = x.astype(BF16)
        h_out[r, :] = (normalise(x)[0] * gain + shift).astype(BF16)

    row_blocks(xs.shape[1], rows)
    project_qkv(h_out, w_load.get(), par, C_T, E_T, qkv_out)


def time_attn_kernel(slots, scal, qkv, y_out):
    def body(r, bias, masks):
        for j in range(PAIRS):
            cq, ck, cv = pair_cols(j)
            y_out[r, cq] = pair_forward(qkv[r, cq], qkv[r, ck], qkv[r, cv], bias, masks).astype(BF16)

    time_windows(y_out.shape[0], slots, scal, body)


def time_mid_kernel(scal, y, x, par, w_load, z_out, b0, b1, b2, b3, xs):
    here, per = b0.shape[1], b0.shape[0]
    slots = 4 * per
    w = w_load.get()

    def proj(i):
        c = block(i, NB)
        z_out[:, c] = (dot_nn(y[...], w[:, c]) + par[O_T : O_T + 1, c]).astype(BF16)

    loop(D // NB, proj)

    def after(i):
        c = block(i, NB)
        fc = dot_nn(z_out[...], w[:, pl.ds(pl.multiple_of(D + i * NB, NB), NB)])
        put_cols(xs, i, x[:, c].astype(F32) + (fc + par[F_T : F_T + 1, c]))

    loop(D // NB, after)
    for r, out in enumerate((b0, b1, b2, b3)):
        first = jnp.bitwise_xor(scal[P_AT], r) * per
        for i in range(per):
            out[i] = get_slot(xs, first + i, slots, here).astype(BF16)


def fill_space(blocks, xs):
    per, here = blocks[0].shape[0], blocks[0].shape[1]
    whole = here * len(blocks)
    for f in range(per):
        for r, b in enumerate(blocks):
            xs[f * whole + r * here : f * whole + (r + 1) * here, :] = b[f].astype(F32)


def cot_kernel(scal, b0, b1, b2, b3, dy_out, xs):
    per, here = b0.shape[0], b0.shape[1]
    fill_space((b0, b1, b2, b3), xs)
    whole = 4 * here
    rows = xs.shape[0]
    row = lax.broadcasted_iota(jnp.int32, (rows, 1), 0)
    slot = scal[P_AT] * per
    weight = jnp.zeros((rows, 1), F32)
    for f in range(per):
        frame = jnp.bitwise_xor(slot + f, scal[T_AT] * (2 * per))
        live = (frame < scal[COUNT_AT]).astype(F32)
        weight = jnp.where((row >= f * whole) & (row < (f + 1) * whole), live, weight)
    dy_out[...] = (xs[...] * weight).astype(BF16)


def cut_kernel(scal, own, peer, b0, b1, b2, b3):
    half, per = own.shape[0], b0.shape[0]
    for r, out in enumerate((b0, b1, b2, b3)):
        first = jnp.bitwise_xor(scal[P_AT], r) * per
        for i in range(per):
            for src, low in ((own, 0), (peer, half)):

                @pl.when((first >= low) & (first < low + half))
                def put(src=src, low=low):
                    out[i] = src[first - low + i]


def join_kernel(scal, b0, b1, b2, b3, own, peer):
    half, per = own.shape[0], b0.shape[0]
    for r, src in enumerate((b0, b1, b2, b3)):
        first = jnp.bitwise_xor(scal[P_AT], r) * per
        for i in range(per):
            for out, low in ((own, 0), (peer, half)):

                @pl.when((first >= low) & (first < low + half))
                def put(out=out, low=low):
                    out[first - low + i] = src[i]


def space_in_kernel(scal, b0, b1, b2, b3, par, w_load, x_out, h_out, qkv_out, xs):
    fill_space((b0, b1, b2, b3), xs)
    gain, shift = par[G_S : G_S + 1, :], par[B_S : B_S + 1, :]

    def rows(r):
        x = xs[r, :]
        x_out[r, :] = x.astype(BF16)
        h_out[r, :] = (normalise(x)[0] * gain + shift).astype(BF16)

    row_blocks(xs.shape[0], rows)
    project_qkv(h_out, w_load.get(), par, C_S, E_S, qkv_out)


def space_windows(rows, per):
    whole = rows // per
    step = whole // 16 * 16
    width = rows - step * (per - 1)
    return whole, step, width


def space_frame(f, rows, per):
    whole, step, width = space_windows(rows, per)
    first = f * (whole - step)
    row = lax.broadcasted_iota(jnp.int32, (width, 1), 0)
    col = lax.broadcasted_iota(jnp.int32, (1, width), 1)
    by_row, by_col = (row >= first) & (row < first + whole), (col >= first) & (col < first + whole)
    r = pl.ds(pl.multiple_of(f * step, 16), width)
    return r, jnp.where(by_row, 0.0, MASKED_SCORE), by_col.astype(F32), by_row.astype(F32)


def space_mid_kernel(per, scal, qkv, x, par, w_load, y_out, x2_out, m_out, ys):
    rows = x.shape[0]
    masks = head_masks()
    ys[...] = jnp.zeros_like(ys)

    def frame(f):
        r, bias, _, valid = space_frame(f, rows, per)
        for j in range(PAIRS):
            cq, ck, cv = pair_cols(j)
            ys[r, cq] += pair_forward(qkv[r, cq], qkv[r, ck], qkv[r, cv], bias, masks) * valid

    loop(per, frame)
    y_out[...] = ys[...].astype(BF16)
    w = w_load.get()

    def proj(i):
        c = block(i, NB)
        x2_out[:, c] = x[:, c].astype(F32) + (dot_nn(y_out[...], w[:, c]) + par[O_S : O_S + 1, c])

    loop(D // NB, proj)
    gain, shift = par[G_M : G_M + 1, :], par[B_M : B_M + 1, :]

    def norm(r):
        m_out[r, :] = (normalise(x2_out[r, :])[0] * gain + shift).astype(BF16)

    row_blocks(rows, norm)


def mlp_kernel(
    scal, m, dy, par, weights, x3_out, dm_out, dw1, dw1_their, dw2, dw2_their, dup,
    w1, w2, w_sems, e, da, mt, up_buf, up_sems, down_buf, down_sems,
):
    rows = D // 4
    steps = FF // D

    def loads(i):
        at = pl.multiple_of(i * D, 128)
        out = [pltpu.make_async_copy(weights.at[:, pl.ds(at, D)], w1.at[i % 2], w_sems.at[i % 2, 4])]
        for j in range(4):
            src = weights.at[pl.ds(pl.multiple_of(i * rows, 16), rows), FF + j * D : FF + (j + 1) * D]
            to = w2.at[i % 2, j * rows : (j + 1) * rows, :]
            out.append(pltpu.make_async_copy(src, to, w_sems.at[i % 2, j]))
        return out

    for c in loads(0):
        c.start()
    mt[...] = m[...].T
    x3_out[...] = jnp.zeros_like(x3_out)
    dm_out[...] = jnp.zeros_like(dm_out)

    def up_copy(i, k, out):
        to = out.at[:, pl.ds(pl.multiple_of(i % 2 * D + k * NB, NB), NB)]
        return pltpu.make_async_copy(up_buf.at[k], to, up_sems.at[k])

    def down_copy(i, j, out):
        to = out.at[pl.ds(pl.multiple_of(i * rows, 16), rows), j % 2 * D : (j % 2 + 1) * D]
        return pltpu.make_async_copy(down_buf.at[j], to, down_sems.at[j])

    def step(i):
        slot = i % 2
        for c in loads(i):
            c.wait()

        @pl.when(i + 1 < steps)
        def ahead():
            for c in loads(i + 1):
                c.start()

        up_w, down_w = w1.at[slot], w2.at[slot]
        for k in range(D // NB):
            c = slice(k * NB, (k + 1) * NB)
            a = dot_nn(m[...], up_w[:, c]) + par[pl.ds(U_1 + i, 1), c]
            g = dot_nt(dy[...], down_w[c, :])
            value, slope = gelu_parts(a)
            low = (g * slope).astype(BF16)
            e[:, c] = value.astype(BF16)
            da[:, c] = low
            dup[pl.ds(i, 1), c] = jnp.sum(low.astype(F32), axis=0, keepdims=True)
        for k in range(D // NB):
            c = slice(k * NB, (k + 1) * NB)
            value = dot_nn(mt[...], da[:, c]).astype(BF16)
            pl.when(i >= 1)(lambda k=k: up_copy(i - 1, k, dw1).wait())
            up_buf[k] = value
            pl.when(scal[C_AT] == i // 2)(lambda k=k: up_copy(i, k, dw1).start())
            pl.when(scal[C_AT] != i // 2)(lambda k=k: up_copy(i, k, dw1_their).start())
        value = dot_tn(e[...], dy[...]).astype(BF16)
        for j in range(4):
            pl.when(i >= 1)(lambda j=j: down_copy(i - 1, j, dw2).wait())
            down_buf[j] = value[j * rows : (j + 1) * rows, :]
            pl.when(scal[C_AT] == j // 2)(lambda j=j: down_copy(i, j, dw2).start())
            pl.when(scal[C_AT] != j // 2)(lambda j=j: down_copy(i, j, dw2_their).start())
        for k in range(D // NB):
            c = slice(k * NB, (k + 1) * NB)
            x3_out[:, c] += dot_nn(e[...], down_w[:, c])
            dm_out[:, c] += dot_nt(da[...], up_w[c, :])

    loop(steps, step)
    for k in range(D // NB):
        up_copy(steps - 1, k, dw1).wait()
    for j in range(4):
        down_copy(steps - 1, j, dw2).wait()


def mlp_out_kernel(per, scal, x2, x3, dm, dy, y, par, w_load, dx2_out, dys_out, dw, dw_their, dvec, b0, b1, b2, b3, xs, yt):
    rows = x2.shape[0]
    here = b0.shape[1]
    gain = par[G_M : G_M + 1, :]
    dvec[...] = jnp.zeros_like(dvec)
    yt[...] = y[...].T

    def back(r):
        xs[r, :] = x2[r, :] + (x3[r, :] + par[U_2 : U_2 + 1, :])
        dz, dg, db = norm_back(x2[r, :], dm[r, :], gain)
        g = dy[r, :].astype(F32)
        dx2 = g + dz
        dx2_out[r, :] = dx2
        low = dx2.astype(BF16)
        dys_out[r, :] = low
        dvec[0:1, :] += dg
        dvec[1:2, :] += db
        dvec[2:3, :] += jnp.sum(g, axis=0, keepdims=True)
        dvec[3:4, :] += jnp.sum(low.astype(F32), axis=0, keepdims=True)

    row_blocks(rows, back)
    for f in range(per):
        for r, out in enumerate((b0, b1, b2, b3)):
            first = f * 4 * here + r * here
            out[f] = xs[first : first + here, :].astype(BF16)

    weight_grad(yt, dys_out, scal, dw, dw_their)
    w = w_load.get()

    def proj(i):
        c = block(i, NB)
        xs[:, c] = dot_nt(dys_out[...], w[c, :])

    loop(D // NB, proj)
    dys_out[...] = xs[...].astype(BF16)


def space_back_kernel(per, scal, qkv, dy, dqkv_out, dvec, acc):
    rows = dy.shape[0]
    masks = head_masks()
    acc[...] = jnp.zeros_like(acc)

    def frame(f):
        r, bias, valid, _ = space_frame(f, rows, per)
        for j in range(PAIRS):
            cq, ck, cv = pair_cols(j)
            dq, dk, dv = pair_backward(qkv[r, cq], qkv[r, ck], qkv[r, cv], dy[r, cq], bias, masks, valid)
            acc[r, cq] += dq
            acc[r, ck] += dk
            acc[r, cv] += dv

    loop(per, frame)
    low = acc[...].astype(BF16)
    dqkv_out[...] = low
    dvec[...] = jnp.zeros_like(dvec)
    dvec[0:1, :] = jnp.sum(dqkv_out[:, :D].astype(F32), axis=0, keepdims=True)
    dvec[1:2, :] = jnp.sum(dqkv_out[:, 2 * D :].astype(F32), axis=0, keepdims=True)


def space_out_kernel(per, scal, dqkv, h, x, dx2, par, w_load, dw, dw_their, dvec, b0, b1, b2, b3, xs, ht):
    rows = x.shape[0]
    here = b0.shape[1]
    ht[...] = h[...].T
    weight_grad(ht, dqkv, scal, dw, dw_their)
    w = w_load.get()

    def proj(c):
        xs[:, c] = dot_nt(dqkv[...], w[c, :])

    col_blocks(D, proj)
    gain = par[G_S : G_S + 1, :]
    dvec[...] = jnp.zeros_like(dvec)

    def back(r):
        dz, dg, db = norm_back(x[r, :].astype(F32), xs[r, :], gain)
        xs[r, :] = dx2[r, :] + dz
        dvec[0:1, :] += dg
        dvec[1:2, :] += db

    row_blocks(rows, back)
    for f in range(per):
        for r, out in enumerate((b0, b1, b2, b3)):
            first = f * 4 * here + r * here
            out[f] = xs[first : first + here, :].astype(BF16)


def time_proj_kernel(scal, b0, b1, b2, b3, y, z, w_load, dx1_out, dy_out, dw, dw_their, dvec, xs, zt, dz):
    per, here = b0.shape[0], b0.shape[1]
    slots = 4 * per
    for r, src in enumerate((b0, b1, b2, b3)):
        first = jnp.bitwise_xor(scal[P_AT], r) * per
        for i in range(per):
            put_slot(xs, first + i, slots, src[i].astype(F32))
    dvec[...] = jnp.zeros_like(dvec)

    def gather_rows(r):
        value = get_rows(xs, r)
        dx1_out[r, :] = value.astype(BF16)
        dvec[0:1, :] += jnp.sum(value, axis=0, keepdims=True)

    row_blocks(xs.shape[1], gather_rows)
    w = w_load.get()

    def proj_f(i):
        c = block(i, NB)
        dz[:, c] = dot_nt(dx1_out[...], w[c, D:]).astype(BF16)

    loop(D // NB, proj_f)

    def proj_o(i):
        c = block(i, NB)
        dy_out[:, c] = dot_nt(dz[...], w[c, :D]).astype(BF16)

    loop(D // NB, proj_o)
    dvec[1:2, :] = jnp.sum(dz[...].astype(F32), axis=0, keepdims=True)

    def put_grad(half, left, right):
        zt[...] = left[...].T

        def cols(out):
            def body(i):
                out[:, block(i, NB)] = dot_nn(zt[...], right[:, block(i, NB)]).astype(BF16)

            loop(D // NB, body)

        pl.when(scal[C_AT] == half)(lambda: cols(dw))
        pl.when(scal[C_AT] != half)(lambda: cols(dw_their))

    put_grad(1, z, dx1_out)
    put_grad(0, y, dz)


def time_attn_back_kernel(slots, scal, qkv, dys, dqkv_out, dvec):
    def body(r, bias, masks):
        for j in range(PAIRS):
            cq, ck, cv = pair_cols(j)
            dq, dk, dv = pair_backward(qkv[r, cq], qkv[r, ck], qkv[r, cv], dys[r, cq], bias, masks)
            dqkv_out[r, cq] = dq.astype(BF16)
            dqkv_out[r, ck] = dk.astype(BF16)
            dqkv_out[r, cv] = dv.astype(BF16)

    time_windows(dys.shape[0], slots, scal, body)
    dvec[...] = jnp.zeros_like(dvec)
    dvec[0:1, :] = jnp.sum(dqkv_out[:, :D].astype(F32), axis=0, keepdims=True)
    dvec[1:2, :] = jnp.sum(dqkv_out[:, 2 * D :].astype(F32), axis=0, keepdims=True)


def time_out_kernel(
    scal, dqkv, h, x, dx1, par, v_t, v_a, v_n, v_s, v_m, v_u, w_load, own, peer, dw, dw_their, vec, dvec, xs, ht, vs
):
    half, here = own.shape[0], own.shape[1]
    slots = 2 * half
    w = w_load.get()

    def proj(i):
        put_cols(xs, i, dot_nt(dqkv[...], w[block(i, NB), :]))

    loop(D // NB, proj)
    gain = par[G_T : G_T + 1, :]
    dvec[...] = jnp.zeros_like(dvec)

    def back(r):
        dz, dg, db = norm_back(x[r, :].astype(F32), get_rows(xs, r), gain)
        put_rows(xs, r, dx1[r, :].astype(F32) + dz)
        dvec[0:1, :] += dg
        dvec[1:2, :] += db

    row_blocks(xs.shape[1], back)
    for s in range(slots):
        v = get_slot(xs, s, slots, here)
        if s < half:
            own[s] = v
        else:
            peer[s - half] = v.astype(BF16)
    vs[...] = jnp.zeros_like(vs)
    for at, (src, row, count) in enumerate(
        (
            (dvec, 0, 2), (None, 0, 0), (v_a, 0, 2), (None, 0, 0), (v_t, 1, 1), (v_t, 0, 1), (v_n, 0, 2), (None, 0, 0),
            (v_s, 0, 2), (None, 0, 0), (v_m, 3, 1), (v_m, 0, 2), (None, 0, 0), (None, 0, 0), (None, 0, 0), (None, 0, 0),
            (None, 0, 0), (v_m, 2, 1),
        )
    ):
        if src is not None:
            vs[at : at + count, :] = src[row : row + count, :]
    vs[U_1 : U_1 + FF // D, :] = v_u[: FF // D, :]
    vec[...] = vs[...].T.astype(BF16)
    ht[...] = h[...].T
    weight_grad(ht, dqkv, scal, dw, dw_their)


def add_split_kernel(packs, n_after, sel_at, scal, *refs):
    n = len(packs)
    send, keep = refs[2 * n + n_after], refs[2 * n + n_after + 1]
    sel = scal[sel_at]
    for i, (offset, width) in enumerate(packs):
        mine, other = refs[i], refs[n + i]
        for out, which in ((send, 1 - sel), (keep, sel)):
            value = mine[0, which].astype(F32) + other[0, which].astype(F32)
            out[0, :, offset : offset + width] = value.astype(BF16)


def add_split(scal, sel_at, mine, other, packs, rows, after=()):
    n = mine[0].shape[0]
    out = sds((n, rows, sum(w for _, w in packs)), BF16)

    def spec(a):
        return pl.BlockSpec((1,) + a.shape[1:], lambda i: (i, 0, 0, 0))

    return pl.pallas_call(
        functools.partial(add_split_kernel, packs, len(after), sel_at),
        grid=(n,),
        out_shape=(out, out),
        in_specs=[pl.BlockSpec(memory_space=pltpu.SMEM)]
        + [spec(a) for a in [*mine, *other]]
        + [pl.BlockSpec(memory_space=pl.ANY)] * len(after),
        out_specs=tuple(pl.BlockSpec((1, *out.shape[1:]), lambda i: (i, 0, 0)) for _ in range(2)),
        compiler_params=pltpu.CompilerParams(vmem_limit_bytes=SMALL_VMEM),
        cost_estimate=cost(20),
    )(scal, *mine, *other, *after)


def adam_update(weight, grad, moment, square, decay, factor, rate):
    grad = grad * factor
    moment = BETA_FIRST * moment + (1.0 - BETA_FIRST) * grad
    square = BETA_SECOND * square + (1.0 - BETA_SECOND) * grad * grad
    moment_hat = moment * (1.0 / (1.0 - BETA_FIRST**STEP))
    square_hat = square * (1.0 / (1.0 - BETA_SECOND**STEP))
    fresh = weight * (1.0 - rate * decay) - (rate * moment_hat) * (1.0 / (jnp.sqrt(square_hat) + ADAM_EPSILON))
    return (fresh, moment, square)


PLANE = ("tm", "pos")
EVERY = ("dp", "tm", "pos")


def pos_permute(a, r):
    n = lax.axis_size("pos")
    return lax.ppermute(a, "pos", [(i, i ^ r) for i in range(n)]) if r else a


def tm_permute(a):
    n = lax.axis_size("tm")
    return lax.ppermute(a, "tm", [(i, n - 1 - i) for i in range(n)])


def grid_permute(a, move):
    pairs = []
    for z in range(4):
        for x in range(2):
            for p in range(4):
                zz, xx, pp = move(z, x, p)
                pairs.append(((z * 2 + x) * 4 + p, (zz * 2 + xx) * 4 + pp))
    return lax.ppermute(a, EVERY, pairs)


def next_plane(a):
    return grid_permute(a, lambda z, x, p: (z ^ 1, x, p))


def far_plane(a):
    return grid_permute(a, lambda z, x, p: (z ^ 3, x, p))


def first_side(a):
    return grid_permute(a, lambda z, x, p: (z, x, p ^ 2) if p & 1 else (z, x ^ 1, p))


def second_side(a):
    return grid_permute(a, lambda z, x, p: (z, x ^ 1, p) if p & 1 else (z, x, p ^ 2))


def other_core(a):
    return grid_permute(a, lambda z, x, p: (z, x, p ^ 1))


def spread_plane(part):
    side = first_side(part)
    far, both = second_side(part), second_side(side)
    own = [part, side, far, both]
    return own + [other_core(a) for a in own]


def once(value, *others):
    return lax.optimization_barrier((value, *others))[0]


def pack_kernel(n, *refs):
    out, at = refs[-1], 0
    for src in refs[:n]:
        for part in range(src.shape[0] if len(src.shape) == 3 else 1):
            out[at] = src[part] if len(src.shape) == 3 else src[...]
            at += 1


def pack(arrays, *after):
    vmem = pl.BlockSpec(memory_space=pltpu.VMEM)
    return pl.pallas_call(
        functools.partial(pack_kernel, len(arrays)),
        out_shape=sds((sum(v.shape[0] if v.ndim == 3 else 1 for v in arrays), *arrays[0].shape[-2:]), BF16),
        in_specs=[vmem] * len(arrays) + [pl.BlockSpec(memory_space=pl.ANY)] * len(after),
        out_specs=vmem,
        compiler_params=pltpu.CompilerParams(vmem_limit_bytes=SMALL_VMEM),
        cost_estimate=cost(20),
        name="pack",
    )(*arrays, *after)


def gather_lines(piece):
    near = next_plane(piece)
    return [near, far_plane(piece), far_plane(near)]


class Group:
    def __init__(self, scal, members):
        self.scal, self.members, self.packs, at = scal, members, [], 0
        for mine, _ in members:
            self.packs.append((at, mine.shape[1]))
            at += mine.shape[1]
        self.width = at
        self.received = [other_core(t) for _, t in members]

    def add(self, mine, theirs):
        self.members = self.members + [(mine, theirs)]
        self.packs.append((self.width, mine.shape[1]))
        self.width += mine.shape[1]
        self.received = self.received + [other_core(theirs)]

    def chip(self, *after):
        mine = [m.reshape(4, 2, -1, m.shape[1]) for m, _ in self.members]
        other = [r.reshape(4, 2, -1, r.shape[1]) for r in self.received]
        self.send, self.keep = add_split(self.scal, A_AT, mine, other, self.packs, 2 * PIECE, after)
        self.received = first_side(self.send)

    def step(self, sel, shape, rows, move, after, gate=()):
        shape = (*shape, self.width)
        self.send, self.keep = add_split(
            self.scal, sel, [self.keep.reshape(shape)], [self.received.reshape(shape)], [(0, self.width)], rows, after
        )
        self.received = move(once(self.send, *gate) if gate else self.send)

    def side(self, *after, gate=()):
        self.step(B_AT, (4, 2, PIECE), PIECE, second_side, after, gate)

    def plane(self, *after):
        self.step(PAIR_AT, (1, 2, 2 * PIECE), 2 * PIECE, far_plane, after)

    def pair(self, *after):
        self.step(ODD_AT, (1, 2, PIECE), PIECE, next_plane, after)

    def total(self, square, alone=0, *after):
        vmem = pl.BlockSpec(memory_space=pltpu.VMEM)
        return pl.pallas_call(
            functools.partial(total_kernel, self.width - alone),
            out_shape=(sds((PIECE, self.width), BF16), sds(square.shape, F32)),
            in_specs=[pl.BlockSpec(memory_space=pltpu.SMEM), vmem, vmem, vmem]
            + [pl.BlockSpec(memory_space=pl.ANY)] * len(after),
            out_specs=(vmem, vmem),
            compiler_params=pltpu.CompilerParams(vmem_limit_bytes=SMALL_VMEM),
            cost_estimate=cost(20),
        )(self.scal, self.keep.reshape(PIECE, -1), self.received.reshape(PIECE, -1), square, *after)


def total_kernel(alone, scal, keep, received, before, *refs):
    out, square = refs[-2:]
    total = (keep[...].astype(F32) + received[...].astype(F32)).astype(BF16)
    out[...] = total
    total = total.astype(F32)
    found = jnp.sum(total[:, :alone] * total[:, :alone])
    if alone < total.shape[1]:
        found += jnp.where(scal[C_AT] == 0, jnp.sum(total[:, alone:] * total[:, alone:]), 0.0)
    square[...] = before[...] + found


def adam_kernel(jobs, n_arrays, steps, scal, total_square, *refs):
    ins, refs = refs[:9], refs[9:]
    arrays, refs = refs[:n_arrays], refs[n_arrays:]
    outs, grads, sems, buffers, out_sems = refs[:10], refs[10:13], refs[13], refs[14:16], refs[16]
    scale = CLIP_NORM / jnp.maximum(jnp.sqrt(total_square[0:1, 0:1]), CLIP_NORM)
    copies = []
    for start, offset, width, to_grad, firsts in jobs:
        for k in range(8):
            half = scal[C_AT] if k < 4 else 1 - scal[C_AT]
            quarter = scal[Q_AT + k] * PIECE
            each = width // len(firsts)
            for j, (low, high) in enumerate(firsts):
                src = arrays[start + k].at[:, offset + j * each : offset + (j + 1) * each]
                if to_grad == 1:
                    rows = pl.ds(pl.multiple_of(low + half * (high - low) + quarter, 16), PIECE)
                    to = grads[1].at[rows, :]
                else:
                    rows = pl.ds(pl.multiple_of(quarter, 16), PIECE)
                    to = grads[to_grad].at[rows, pl.ds(pl.multiple_of(low + half * (high - low), 128), each)]
                copies.append(pltpu.make_async_copy(src, to, sems.at[len(copies)]))
    for c in copies:
        c.start()
    for c in copies:
        c.wait()

    def rows_of(i, which):
        size = buffers[which].shape[2]
        return pl.ds(pl.multiple_of(i * size, 16), size)

    def copy_out(i, which, j):
        to = outs[3 * which + j].at[rows_of(i, which), :]
        return pltpu.make_async_copy(buffers[which].at[i % 2, j], to, out_sems.at[i % 2, which, j])

    def step(i):
        for which in range(2):
            r = rows_of(i, which)
            weight, moment, square = (v[r, :] for v in ins[3 * which : 3 * which + 3])
            g = grads[which][r, :].astype(F32)
            fresh = adam_update(weight, g, moment, square, WEIGHT_DECAY, scale, LEARN_RATE)
            for j, value in enumerate(fresh):
                pl.when(i >= 2)(lambda j=j: copy_out(i - 2, which, j).wait())
                buffers[which][i % 2, j] = value
                copy_out(i, which, j).start()

    loop(steps, step)
    g = grads[2][:, :LANES].astype(F32).T[: ins[6].shape[0], :]
    fresh = adam_update(ins[6][...], g, ins[7][...], ins[8][...], 0.0, scale, LEARN_RATE_VEC)
    for out, value in zip(outs[6:9], fresh):
        out[...] = value
    outs[9][...] = g[U_2 : U_2 + 1, :] * scale
    for i in (steps - 2, steps - 1):
        for which in range(2):
            for j in range(3):
                copy_out(i, which, j).wait()


def adam_all(scal, total_square, arrays, jobs, steps, wide, tall, vec):
    anywhere, vmem = pl.BlockSpec(memory_space=pl.ANY), pl.BlockSpec(memory_space=pltpu.VMEM)
    both = [*wide, *tall, *vec]
    shard = vec[0].shape[1]
    return pl.pallas_call(
        functools.partial(adam_kernel, jobs, len(arrays), steps),
        out_shape=tuple(sds(v.shape, F32) for v in both) + (sds((1, shard), F32),),
        in_specs=[pl.BlockSpec(memory_space=pltpu.SMEM)] + [vmem] * (1 + len(both)) + [anywhere] * len(arrays),
        out_specs=tuple([pl.BlockSpec(memory_space=pltpu.HBM)] * 6 + [vmem] * 4),
        scratch_shapes=[
            pltpu.VMEM(wide[0].shape, BF16),
            pltpu.VMEM(tall[0].shape, BF16),
            pltpu.VMEM((shard, 2 * LANES), BF16),
            pltpu.SemaphoreType.DMA((sum(8 * len(j[4]) for j in jobs),)),
            pltpu.VMEM((2, 3, wide[0].shape[0] // steps, wide[0].shape[1]), F32),
            pltpu.VMEM((2, 3, tall[0].shape[0] // steps, tall[0].shape[1]), F32),
            pltpu.SemaphoreType.DMA((2, 2, 3)),
        ],
        compiler_params=pltpu.CompilerParams(vmem_limit_bytes=ADAM_VMEM),
        cost_estimate=cost(25),
    )(scal, total_square, *both, *arrays)


def shards(
    tokens,
    cotangent,
    frame_counts,
    weight_in,
    weight_out,
    vectors,
    moment_in,
    moment_out,
    moment_vec,
    square_in,
    square_out,
    square_vec,
):
    clips, half, here, _ = tokens.shape
    tm, n_pos, n_dp = lax.axis_size("tm"), lax.axis_size("pos"), lax.axis_size("dp")
    slots = half * tm
    per = slots // n_pos
    rows = slots * here
    t, p, z = lax.axis_index("tm"), lax.axis_index("pos"), lax.axis_index("dp")
    count = lax.dynamic_index_in_dim(frame_counts, t, keepdims=False)
    line = n_dp == 4
    core = p % 2 if line else 0
    a = jnp.where(core == 0, t, p // 2)
    b = jnp.where(core == 0, p // 2, t)
    quarters = [2 * a + b, 2 * (1 - a) + b, 2 * a + 1 - b, 2 * (1 - a) + 1 - b]
    quarters += [2 * b + a, 2 * (1 - b) + a, 2 * b + 1 - a, 2 * (1 - b) + 1 - a]
    scal = jnp.stack([count, t, p, z, core, *quarters, a, b, z // 2, z % 2]).astype(jnp.int32)

    own_tokens, peer_tokens, own_cot, peer_cot = (
        lax.dynamic_index_in_dim(v, at, keepdims=False) for v in (tokens, cotangent) for at in (t, 1 - t)
    )
    low_in, low_out = weight_in.astype(BF16), weight_out.astype(BF16)
    vec_low = jnp.pad(vectors.astype(BF16), ((0, 0), (0, LANES - vectors.shape[1])))
    vec_low = jnp.concatenate([vec_low, vec_low], axis=1)

    spans = {"at": (0, 3 * D), "ot": (3 * D, 2 * D), "as": (5 * D, 3 * D), "os": (8 * D, D)}

    def whole(low, *after):
        part = low.shape[0] // (tm * n_pos)
        mine = once(lax.dynamic_slice_in_dim(low, (t * n_pos + p) * part, part, axis=0), *after)
        return lax.all_gather(mine, EVERY, axis=0, tiled=True)

    blk = sds((per, here, D), BF16)
    act = sds((rows, D), BF16)
    wide = sds((rows, 3 * D), BF16)
    full = sds((rows, D), F32)
    par_out = sds((VROWS, D), F32)
    vec_out = sds((8, D), F32)
    scr = pltpu.VMEM((rows, D), F32)
    scr_tiled = pltpu.VMEM((TILES, rows, LANES), F32)
    scr_low = pltpu.VMEM((rows, D), BF16)
    scr_hidden = pltpu.VMEM((rows, FF), BF16)
    scr_t = pltpu.VMEM((D, rows), BF16)

    def halves(cols, height=D):
        return [sds((height, cols), BF16)] * 2

    after_in = after_attn = after_mid = after_space = ()
    if line:
        quarter = lax.dynamic_slice_in_dim(weight_in, quarters[0] * PIECE, PIECE, axis=0)
        vec_quarter = lax.dynamic_slice_in_dim(vec_low[:, :LANES], quarters[0] * PIECE, PIECE, axis=0)

        def half_of(first, width):
            return lax.dynamic_slice_in_dim(quarter, first + core * (width // 2), width // 2, axis=1).astype(BF16)

        def lines(piece, near):
            return [near, far_plane(piece), far_plane(near)]

        def sides(first):
            return first_side(first), second_side(first)

        def cores(group):
            return group + [other_core(v) for v in group]

        piece_0 = jnp.concatenate([half_of(*spans["at"]), vec_quarter], axis=1)
        near_0 = next_plane(piece_0)
        lines_0 = lines(piece_0, near_0)
        peer_tokens = tm_permute(peer_tokens)
        piece_1 = half_of(*spans["ot"])
        piece_2 = jnp.concatenate([half_of(*spans[name]) for name in ("as", "os")], axis=1)
        first_0 = pack(lines_0, piece_1, peer_tokens)
        side_0, far_0 = sides(first_0)
        down_quarters = jnp.concatenate(jnp.split(low_out, 4, axis=0), axis=1)
        hidden_part = jnp.concatenate([low_in[:, 9 * D :], down_quarters], axis=1)
        piece_1 = once(piece_1, first_0)
        near_1 = next_plane(piece_1)
        pair_1 = pack([piece_1, near_1])
        far_pair_1 = far_plane(pair_1)
        both_0 = second_side(once(side_0, own_tokens, scal, vec_low, piece_2, hidden_part, pair_1))
        hidden = whole(hidden_part, first_0)
        group_0 = cores([first_0, side_0, far_0, both_0])
        first_1 = pack([near_1, far_pair_1], both_0)
        side_1, far_1 = sides(first_1)
        piece_2 = once(piece_2, first_1)
        near_2 = next_plane(piece_2)
        pair_2 = pack([piece_2, near_2], first_1)
        far_pair_2 = far_plane(pair_2)
        after_in = (first_1, pair_2)
        w_at = Weight(3 * D, shard=low_in, blocks=[spans["at"]], pieces=group_0)
        w_vec = Weight(2 * LANES, shard=vec_low, blocks=[(0, 2 * LANES)], pieces=group_0, offset=3 * D // 2)
    else:
        peer_tokens, peer_cot = tm_permute(peer_tokens), tm_permute(peer_cot)

        w_at, w_ot, w_as, w_os = (
            Weight(width, whole=whole(low_in[:, first : first + width])) for first, width in spans.values()
        )
        up_all, down_all = whole(low_in[:, 9 * D :]), whole(low_out)
        w_vec = Weight(2 * LANES, whole=lax.all_gather(vec_low, "dp", axis=0, tiled=True))

    x, h_t, qkv_t, par = call(
        time_in_kernel, scal, [own_tokens, peer_tokens], [w_at, w_vec], [act, act, wide, par_out], [scr_tiled], after_in
    )
    if line:
        first_2 = pack([near_2, far_pair_2], h_t)
        both_1 = second_side(once(side_1, h_t))
        side_2, far_2 = sides(first_2)
        after_attn = (first_2, side_1)
    (y_t,) = call(functools.partial(time_attn_kernel, slots), scal, [qkv_t], [], [act], [], after_attn)
    if line:
        group_1 = cores(once([first_1, side_1, far_1, both_1], y_t))
        w_ot = Weight(2 * D, shard=low_in, blocks=[spans["ot"]], pieces=group_1)
        both_2 = second_side(once(side_2, y_t))
        after_mid = (side_2,)
    z_t, *x1 = call(time_mid_kernel, scal, [y_t, x, par], [w_ot], [act, blk, blk, blk, blk], [scr_tiled], after_mid)
    x1 = [pos_permute(v, r) for r, v in enumerate(x1)]
    if line:
        peer_cot = tm_permute(once(peer_cot, z_t))
        group_2 = cores(once([first_2, side_2, far_2, both_2], *x1[1:]))
        w_as = Weight(3 * D, shard=low_in, blocks=[spans["as"]], pieces=group_2)
        w_os = Weight(D, shard=low_in, blocks=[spans["os"]], pieces=group_2, offset=3 * D // 2)
        after_space = (peer_cot,)

    x1, h_s, qkv_s = call(space_in_kernel, scal, [*x1, par], [w_as], [act, act, wide], [scr], after_space)
    cot = call(cut_kernel, scal, [own_cot, peer_cot], [], [blk] * 4, [], (h_s,))
    cot = [pos_permute(v, r) for r, v in enumerate(cot)]
    y_s, x2, m = call(
        functools.partial(space_mid_kernel, per), scal, [qkv_s, x1, par], [w_os], [act, full, act], [scr], (cot[0],)
    )
    (dy,) = call(cot_kernel, scal, cot, [], [act], [scr], (m,))

    if not line:
        down_all = down_all.reshape(4, 4, D // 4, D).transpose(0, 2, 1, 3).reshape(D, FF)
        hidden = jnp.concatenate([up_all, down_all], axis=1)
    buffers = [
        pltpu.VMEM((2, D, D), BF16),
        pltpu.VMEM((2, D, D), BF16),
        pltpu.SemaphoreType.DMA((2, 5)),
        scr_low,
        scr_low,
        scr_t,
        pltpu.VMEM((D // NB, D, NB), BF16),
        pltpu.SemaphoreType.DMA((D // NB,)),
        pltpu.VMEM((4, D // 4, D), BF16),
        pltpu.SemaphoreType.DMA((4,)),
    ]
    x3, dm, g_1, g_1t, g_2, g_2t, v_u = call(
        mlp_kernel,
        scal,
        [m, dy, par],
        [],
        [full, full, *halves(FF // 2), *halves(FF // 2), vec_out],
        buffers,
        anywhere=(2, 3, 4, 5),
        left=(hidden,),
    )
    if line:
        group_a = Group(scal, [(g_1, g_1t), (g_2, g_2t)])
    dx2, dys, g_os, g_ost, v_m, *out = call(
        functools.partial(mlp_out_kernel, per),
        scal,
        [x2, x3, dm, dy, y_s, par],
        [w_os],
        [full, act, *halves(D // 2), vec_out, blk, blk, blk, blk],
        [scr, scr_t],
    )
    mine = (jnp.arange(clips, dtype=jnp.int32) == t)[:, None, None, None]

    wait = ()
    if line:
        group_a.chip(v_m)
        wait = (group_a.send,)
    dqkv_s, v_s = call(
        functools.partial(space_back_kernel, per),
        scal,
        [qkv_s, dys],
        [],
        [wide, vec_out],
        [pltpu.VMEM((rows, 3 * D), F32)],
        wait,
    )
    g_as, g_ast, v_n, *dx1 = call(
        functools.partial(space_out_kernel, per),
        scal,
        [dqkv_s, h_s, x1, dx2, par],
        [w_as],
        [*halves(3 * D // 2), vec_out, blk, blk, blk, blk],
        [scr, scr_t],
    )
    dx1 = [pos_permute(v, r) for r, v in enumerate(dx1)]

    if line:
        group_s = Group(scal, [(g_os, g_ost), (g_as, g_ast)])
        group_a.side(v_n, gate=dx1[1:])
        wait = (group_a.send,)
    dx1, dy_t, g_ot, g_ott, v_t = call(
        time_proj_kernel,
        scal,
        [*dx1, y_t, z_t],
        [w_ot],
        [act, act, *halves(D), vec_out],
        [scr_tiled, scr_t, scr_low],
        wait,
    )
    if line:
        group_s.add(g_ot, g_ott)
        group_a.plane(v_t)
        group_s.chip(group_a.send)
        wait = (group_s.send,)
    out = [pos_permute(once(v, v_t), r) for r, v in enumerate(out)]
    dqkv_t, v_a = call(
        functools.partial(time_attn_back_kernel, slots), scal, [qkv_t, dy_t], [], [wide, vec_out], [], wait
    )
    if line:
        group_a.pair(v_a)
        group_s.side(group_a.send)
    out_own, out_peer = call(join_kernel, scal, out, [], [sds((half, here, D), BF16)] * 2, [], (v_a,))
    wait = (group_s.send, out_own) if line else ()
    grad_own, grad_peer, g_at, g_att, g_vec, _ = call(
        time_out_kernel,
        scal,
        [dqkv_t, h_t, x, dx1, par, v_t, v_a, v_n, v_s, v_m, v_u],
        [w_at],
        [
            sds((half, here, D), F32),
            sds((half, here, D), BF16),
            *halves(3 * D // 2),
            sds((D, LANES), BF16),
            vec_out,
        ],
        [scr_tiled, scr_t, pltpu.VMEM((LANES, D), F32)],
        wait,
    )
    if line:
        group_t = Group(scal, [(g_at, g_att), (g_vec, g_vec)])
        square = jnp.zeros((8, LANES), F32)
        sum_a, square = group_a.total(square, 0, g_vec)
        group_s.plane(sum_a)
        sides_a = sides(sum_a)
        group_t.chip(group_s.send)
        group_s.pair(*sides_a, group_t.send)
        group_t.side(group_s.send)
        parts_a = [sum_a, *sides_a, second_side(once(sides_a[0], group_t.send))]
        sum_s, square = group_s.total(square, 0, *parts_a[3:])
        group_t.plane(sum_s)
        sides_s = sides(once(sum_s, group_t.send))
        parts_a = cores(once(parts_a, group_t.send))
        group_t.pair(*sides_s, *parts_a[4:])
        parts_s = cores([sum_s, *sides_s, second_side(once(sides_s[0], group_t.send))])
        parts = parts_a + parts_s
        sum_t, square = group_t.total(square, LANES, *parts_s[4:])
        parts_t = spread_plane(sum_t)
        parts = parts + parts_t
        out_peer, grad_peer = once(out_peer, parts_t[3]), once(grad_peer, parts_t[3])
    out_peer = tm_permute(out_peer)
    block_out = jnp.where(mine, out_own[None], out_peer[None])
    grad_peer = tm_permute(grad_peer).astype(F32)
    input_grad = jnp.where(mine, grad_own[None], grad_peer[None])

    if line:
        for move in (next_plane, far_plane, first_side, second_side, other_core):
            square = square + move(square)
        total_square = square[0, 0]
    else:
        g_in = jnp.concatenate([g_at, g_att, g_ot, g_ott, g_as, g_ast, g_os, g_ost, g_1, g_1t], axis=1)
        g_out = jnp.concatenate([g_2, g_2t], axis=1).reshape(4, D // 4, 4, D).transpose(0, 2, 1, 3).reshape(FF, D)
        g_vec = g_vec[:, : vectors.shape[1]]

        def reduced(grad):
            mine_rows = lax.psum_scatter(grad, "dp", scatter_dimension=0, tiled=True)
            return lax.psum(mine_rows, PLANE).astype(F32)

        g_in, g_out, g_vec = reduced(g_in), reduced(g_out), reduced(g_vec)
        local_square = jnp.sum(g_in * g_in) + jnp.sum(g_out * g_out) + jnp.sum(g_vec * g_vec)
        total_square = lax.psum(local_square, "dp")

    grad_norm = jnp.sqrt(total_square)
    factor = CLIP_NORM / jnp.maximum(grad_norm, CLIP_NORM)
    wide_in, tall_in = (weight_in, moment_in, square_in), (weight_out, moment_out, square_out)
    vec_in = (vectors, moment_vec, square_vec)
    if line:

        def span(name):
            first, width = spans[name]
            return ((first, first + width // 2),)

        shard = weight_out.shape[0]
        jobs = [
            (0, *group_a.packs[0], 0, ((9 * D, 9 * D + FF // 2),)),
            (0, *group_a.packs[1], 1, ((0, shard // 2), (shard // 4, shard // 4 * 3))),
        ]
        for name, (offset, width) in zip(("os", "as", "ot"), group_s.packs):
            jobs.append((8, offset, width, 0, span(name)))
        jobs.append((16, *group_t.packs[0], 0, span("at")))
        jobs.append((16, *group_t.packs[1], 2, ((0, LANES),)))
        fresh = adam_all(scal, square, parts, jobs, 12, wide_in, tall_in, [v.T for v in vec_in])
        *fresh, new_v, first_v, second_v, bias_down = fresh
        fresh += [new_v.T, first_v.T, second_v.T]
        bias_down_grad = bias_down.reshape(-1)
    else:
        fresh = [
            *adam_update(weight_in, g_in, moment_in, square_in, WEIGHT_DECAY, factor, LEARN_RATE),
            *adam_update(weight_out, g_out, moment_out, square_out, WEIGHT_DECAY, factor, LEARN_RATE),
            *adam_update(vectors, g_vec, moment_vec, square_vec, 0.0, factor, LEARN_RATE_VEC),
        ]
        bias_down_grad = g_vec[:, U_2] * factor
    new_in, first_in, second_in, new_out, first_out, second_out, new_vec, first_vec, second_vec = fresh
    return (
        block_out,
        input_grad,
        grad_norm,
        new_in,
        new_out,
        new_vec,
        first_in,
        first_out,
        first_vec,
        second_in,
        second_out,
        second_vec,
        bias_down_grad,
    )


def solution(mesh):
    acts, rows = P("dp", "tm", "pos", None), P("dp", None)
    return jax.shard_map(
        shards,
        mesh=mesh,
        in_specs=(acts, acts, P("dp"), *[rows] * 9),
        out_specs=(acts, acts, P(), *[rows] * 9, P("dp")),
        check_vma=False,
    )
```

```python
import functools

import jax
import jax.numpy as jnp
from jax import lax
from jax.experimental import pallas as pl
from jax.experimental.pallas import tpu as pltpu
from jax.sharding import PartitionSpec as P

HEADS = 12
HD = 64
D = 768
FF = 3072
STEP = 10

NORM_EPSILON = 1e-06
CLIP_NORM = 1.0
LEARN_RATE = 0.03
LEARN_RATE_VEC = 0.25
BETA_FIRST = 0.9
BETA_SECOND = 0.999
ADAM_EPSILON = 1e-08
WEIGHT_DECAY = 0.05
MASKED_SCORE = -1e30
SCALE = HD ** (-0.5)

F32 = jnp.float32
BF16 = jnp.bfloat16
PAIR = 2 * HD
PAIRS = D // PAIR
NB = 256
ROWB = 112
WINDOW = 128
VMEM_LIMIT = 56 * 1024 * 1024
SMALL_VMEM = 16 * 1024 * 1024
SPARE_VMEM = 4 * 1024 * 1024
ADAM_VMEM = 20 * 1024 * 1024

G_T, B_T, C_T, E_T, O_T, F_T, G_S, B_S, C_S, E_S, O_S, G_M, B_M, U_1, U_2 = (
    0, 1, 2, 3, 4, 5, 6, 7, 8, 9, 10, 11, 12, 13, 17,
)


COUNT_AT, T_AT, P_AT, Z_AT, C_AT, Q_AT = 0, 1, 2, 3, 4, 5
A_AT, B_AT, PAIR_AT, ODD_AT = 13, 14, 15, 16
OTHERS = (1, 3, 2)
PIECE = 48
VROWS = 24


def dot_nn(a, b):
    return lax.dot_general(a, b, (((1,), (0,)), ((), ())), preferred_element_type=F32)


def dot_nt(a, b):
    return lax.dot_general(a, b, (((1,), (1,)), ((), ())), preferred_element_type=F32)


def dot_tn(a, b):
    return lax.dot_general(a, b, (((0,), (0,)), ((), ())), preferred_element_type=F32)


def loop(count, body, unroll=1):
    def step(i, carry):
        body(i)
        return carry

    lax.fori_loop(0, count, step, 0, unroll=unroll)


def block(i, size):
    return pl.ds(pl.multiple_of(i * size, size), size)


def row_blocks(rows, body):
    loop(rows // ROWB, lambda i: body(pl.ds(pl.multiple_of(i * ROWB, 16), ROWB)))


def col_blocks(cols, body):
    loop(cols // NB, lambda i: body(block(i, NB)))


LANES = 128
TILES = D // LANES


def put_slot(xs, s, slots, value):
    for j in range(TILES):
        xs[j, pl.ds(s, value.shape[0], stride=slots), :] = value[:, j * LANES : (j + 1) * LANES]


def get_slot(xs, s, slots, count):
    return jnp.concatenate([xs[j, pl.ds(s, count, stride=slots), :] for j in range(TILES)], axis=1)


def get_rows(xs, r):
    return jnp.concatenate([xs[j, r, :] for j in range(TILES)], axis=1)


def put_rows(xs, r, value):
    for j in range(TILES):
        xs[j, r, :] = value[:, j * LANES : (j + 1) * LANES]


def put_cols(xs, i, value):
    per = NB // LANES
    for j in range(per):
        xs[i * per + j] = value[:, j * LANES : (j + 1) * LANES]


def normalise(x):
    centred = x - jnp.mean(x, axis=-1, keepdims=True)
    variance = jnp.mean(centred * centred, axis=-1, keepdims=True)
    inverse = lax.rsqrt(variance + NORM_EPSILON)
    return centred * inverse, inverse


def norm_back(x, grad, gain):
    z_hat, inverse = normalise(x)
    h = grad * gain
    first = jnp.mean(h, axis=-1, keepdims=True)
    second = jnp.mean(h * z_hat, axis=-1, keepdims=True)
    dz = inverse * (h - first - z_hat * second)
    return dz, jnp.sum(grad * z_hat, axis=0, keepdims=True), jnp.sum(grad, axis=0, keepdims=True)


def head_masks():
    lane = lax.broadcasted_iota(jnp.int32, (1, PAIR), 1)
    return [(lane < HD).astype(BF16), (lane >= HD).astype(BF16)]


def gelu_parts(a):
    z = jnp.abs(a) * 0.7071067811865476
    t = 1.0 / (1.0 + 0.3275911 * z)
    e = jnp.exp(-z * z)
    poly = t * (0.254829592 + t * (-0.284496736 + t * (1.421413741 + t * (-1.453152027 + t * 1.061405429))))
    tail = 0.5 * poly * e
    phi_low = jnp.where(a < 0.0, tail, 1.0 - tail)
    return a * phi_low, phi_low + a * (0.3989422804014327 * e)


class Weight:
    def __init__(self, cols, rows=D, whole=None, shard=None, blocks=None, pieces=(), offset=0):
        self.rows, self.cols, self.whole, self.offset = rows, cols, whole, offset
        self.blocks = blocks
        self.arrays = [whole] if whole is not None else [shard, *pieces]

    def scratch(self):
        count = 1 if self.whole is not None else len(self.blocks) + 8 * len(OTHERS)
        return [pltpu.VMEM((self.rows, self.cols), BF16), pltpu.SemaphoreType.DMA((count,))]

    def copies(self, refs, scal, dst, sems):
        if self.whole is not None:
            return [pltpu.make_async_copy(refs[0].at[:, self.offset : self.offset + self.cols], dst, sems.at[0])]
        shard = self.rows // 4
        z, c = scal[Z_AT], scal[C_AT]
        own_rows = pl.ds(pl.multiple_of(z * shard, 16), shard)
        out, at = [], 0
        for first, size in self.blocks:
            src, to = refs[0].at[:, first : first + size], dst.at[own_rows, at : at + size]
            at += size
            out.append(pltpu.make_async_copy(src, to, sems.at[len(out)]))
        width = self.cols // 2
        for k in range(8):
            half = c if k < 4 else 1 - c
            quarter = scal[Q_AT + k]
            for j, m in enumerate(OTHERS):
                row = jnp.bitwise_xor(z, m) * shard + quarter * PIECE
                col = pl.multiple_of(half * width, 128)
                src = refs[1 + k].at[j, :, self.offset : self.offset + width]
                to = dst.at[pl.ds(pl.multiple_of(row, 16), PIECE), pl.ds(col, width)]
                out.append(pltpu.make_async_copy(src, to, sems.at[len(out)]))
        return out


class Loaded:
    def __init__(self, ref, copies):
        self.ref, self.copies, self.waited = ref, copies, False

    def get(self):
        if not self.waited:
            for c in self.copies:
                c.wait()
            self.waited = True
        return self.ref


def sds(shape, dtype):
    return jax.ShapeDtypeStruct(shape, dtype)


def cost(microseconds):
    return pl.CostEstimate(flops=int(microseconds * 1e9), bytes_accessed=0, transcendentals=0)


COSTS = {"join": 20, "cut": 20, "cot": 20}


def call(kernel, scal, ins, weights, outs, scratch=(), after=(), anywhere=(), left=()):
    n_in, n_out, n_scr = len(ins), len(outs), len(scratch)
    arrays = [a for w in weights for a in w.arrays]
    n_left = len(left)

    def body(scal_ref, *refs):
        in_refs, refs = refs[: n_in + n_left], refs[n_in + n_left :]
        array_refs, refs = refs[: len(arrays)], refs[len(arrays) + len(after) :]
        out_refs, refs = refs[:n_out], refs[n_out:]
        own, refs = refs[:n_scr], refs[n_scr:]
        loaded, at = [], 0
        for i, w in enumerate(weights):
            dst, sems = refs[2 * i : 2 * i + 2]
            copies = w.copies(array_refs[at : at + len(w.arrays)], scal_ref, dst, sems)
            at += len(w.arrays)
            for c in copies:
                c.start()
            loaded.append(Loaded(dst, copies))
        kernel(scal_ref, *in_refs, *loaded, *out_refs, *own)
        for w in loaded:
            w.get()

    in_vmem = pl.BlockSpec(memory_space=pltpu.VMEM)
    def padded(v):
        lead = 1
        for n in v.shape[:-2]:
            lead *= n
        return lead * (-(-v.shape[-2] // 16) * 16) * (-(-v.shape[-1] // LANES) * LANES) * jnp.dtype(v.dtype).itemsize

    held = [v for v in scratch if v.dtype in (BF16, F32)]
    used = sum(padded(v) for v in held) + sum(w.rows * w.cols * 2 for w in weights)
    limit = used + SPARE_VMEM
    name = getattr(kernel, "func", kernel).__name__.removesuffix("_kernel")
    return pl.pallas_call(
        body,
        name=name,
        out_shape=tuple(outs),
        in_specs=[pl.BlockSpec(memory_space=pltpu.SMEM)]
        + [in_vmem] * n_in
        + [pl.BlockSpec(memory_space=pltpu.HBM)] * n_left
        + [pl.BlockSpec(memory_space=pl.ANY)] * (len(arrays) + len(after)),
        out_specs=tuple(pl.BlockSpec(memory_space=pltpu.HBM) if i in anywhere else in_vmem for i in range(n_out)),
        scratch_shapes=list(scratch) + [x for w in weights for x in w.scratch()],
        compiler_params=pltpu.CompilerParams(vmem_limit_bytes=limit),
        cost_estimate=cost(COSTS.get(name, 0)),
    )(scal, *ins, *left, *arrays, *after)


def grad_cols(width, body):
    loop(width // NB, lambda i: body(pl.multiple_of(i * NB, NB), NB))
    if width % NB:
        body(width - width % NB, width % NB)


def weight_grad(left_t, right, scal, mine, theirs):
    width = mine.shape[1]
    for out, half in ((theirs, 1 - scal[C_AT]), (mine, scal[C_AT])):

        def body(at, size, out=out, half=half):
            c = pl.ds(pl.multiple_of(half * width + at, 128), size)
            out[:, pl.ds(at, size)] = dot_nn(left_t[...], right[:, c]).astype(BF16)

        grad_cols(width, body)


def stack_heads(a, masks):
    return jnp.concatenate([a * masks[0], a * masks[1]], axis=0)


def softmax_cols(scores):
    e = jnp.exp(scores - jnp.max(scores, axis=0, keepdims=True))
    return e * (1.0 / jnp.sum(e, axis=0, keepdims=True))


def pair_cols(j):
    return [slice(part * D + j * PAIR, part * D + (j + 1) * PAIR) for part in range(3)]


def pair_probs(q, kk, bias):
    size = q.shape[0]
    s = dot_nt(kk, q)
    return [softmax_cols(s[h * size : (h + 1) * size] + bias) for h in range(2)]


def pair_forward(q, k, v, bias, masks):
    p = pair_probs(q * BF16(SCALE), stack_heads(k, masks), bias)
    return dot_tn(jnp.concatenate(p, axis=0).astype(BF16), stack_heads(v, masks))


def pair_backward(q, k, v, g, bias, masks, valid=None):
    size = q.shape[0]
    q = q * BF16(SCALE)
    kk, vv = stack_heads(k, masks), stack_heads(v, masks)
    p = pair_probs(q, kk, bias)
    dp = dot_nt(vv, g)
    ds = []
    for h in range(2):
        if valid is not None:
            p[h] = p[h] * valid
        d = dp[h * size : (h + 1) * size]
        ds.append(p[h] * (d - jnp.sum(p[h] * d, axis=0, keepdims=True)))
    ds = jnp.concatenate(ds, axis=0).astype(BF16)
    pp = jnp.concatenate(p, axis=0).astype(BF16)
    dq = dot_tn(ds, kk) * SCALE
    dk, dv = dot_nn(ds, q), dot_nn(pp, g)
    first = lax.broadcasted_iota(jnp.int32, (1, PAIR), 1) < HD
    return dq, jnp.where(first, dk[:size], dk[size:]), jnp.where(first, dv[:size], dv[size:])


def time_bias(scal, slots, size):
    row = lax.broadcasted_iota(jnp.int32, (size, size), 0)
    col = lax.broadcasted_iota(jnp.int32, (size, size), 1)
    frame = jnp.bitwise_xor(row % slots, scal[T_AT] * (slots // 2))
    return jnp.where((row // slots == col // slots) & (frame < scal[COUNT_AT]), 0.0, MASKED_SCORE)


def time_windows(rows, slots, scal, body):
    masks = head_masks()
    bias = time_bias(scal, slots, WINDOW)
    loop(rows // WINDOW, lambda i: body(block(i, WINDOW), bias, masks))
    left = rows % WINDOW
    if left:
        body(pl.ds(rows - left, left), time_bias(scal, slots, left), masks)


def project_qkv(h, w, par, q_row, v_row, out):
    for part, row in enumerate((q_row, None, v_row)):

        def cols(i, part=part, row=row):
            c = pl.ds(pl.multiple_of(part * D + i * NB, NB), NB)
            value = dot_nn(h[...], w[:, c])
            if row is not None:
                value = value + par[row : row + 1, block(i, NB)]
            out[:, c] = value.astype(BF16)

        loop(D // NB, cols)


def time_in_kernel(scal, own, peer, w_load, vec_load, x_out, h_out, qkv_out, par, xs):
    half, here = own.shape[0], own.shape[1]
    slots = 2 * half
    for s in range(slots):
        src = own if s < half else peer
        put_slot(xs, s, slots, src[s % half].astype(F32))
    vec = vec_load.get()
    par[...] = vec[:, :LANES].astype(F32).T[:VROWS, :]
    gain, shift = par[G_T : G_T + 1, :], par[B_T : B_T + 1, :]

    def rows(r):
        x = get_rows(xs, r)
        x_out[r, :] = x.astype(BF16)
        h_out[r, :] = (normalise(x)[0] * gain + shift).astype(BF16)

    row_blocks(xs.shape[1], rows)
    project_qkv(h_out, w_load.get(), par, C_T, E_T, qkv_out)


def time_attn_kernel(slots, scal, qkv, y_out):
    def body(r, bias, masks):
        for j in range(PAIRS):
            cq, ck, cv = pair_cols(j)
            y_out[r, cq] = pair_forward(qkv[r, cq], qkv[r, ck], qkv[r, cv], bias, masks).astype(BF16)

    time_windows(y_out.shape[0], slots, scal, body)


def time_mid_kernel(scal, y, x, par, w_load, z_out, b0, b1, b2, b3, xs):
    here, per = b0.shape[1], b0.shape[0]
    slots = 4 * per
    w = w_load.get()

    def proj(i):
        c = block(i, NB)
        z_out[:, c] = (dot_nn(y[...], w[:, c]) + par[O_T : O_T + 1, c]).astype(BF16)

    loop(D // NB, proj)

    def after(i):
        c = block(i, NB)
        fc = dot_nn(z_out[...], w[:, pl.ds(pl.multiple_of(D + i * NB, NB), NB)])
        put_cols(xs, i, x[:, c].astype(F32) + (fc + par[F_T : F_T + 1, c]))

    loop(D // NB, after)
    for r, out in enumerate((b0, b1, b2, b3)):
        first = jnp.bitwise_xor(scal[P_AT], r) * per
        for i in range(per):
            out[i] = get_slot(xs, first + i, slots, here).astype(BF16)


def fill_space(blocks, xs):
    per, here = blocks[0].shape[0], blocks[0].shape[1]
    whole = here * len(blocks)
    for f in range(per):
        for r, b in enumerate(blocks):
            xs[f * whole + r * here : f * whole + (r + 1) * here, :] = b[f].astype(F32)


def cot_kernel(scal, b0, b1, b2, b3, dy_out, xs):
    per, here = b0.shape[0], b0.shape[1]
    fill_space((b0, b1, b2, b3), xs)
    whole = 4 * here
    rows = xs.shape[0]
    row = lax.broadcasted_iota(jnp.int32, (rows, 1), 0)
    slot = scal[P_AT] * per
    weight = jnp.zeros((rows, 1), F32)
    for f in range(per):
        frame = jnp.bitwise_xor(slot + f, scal[T_AT] * (2 * per))
        live = (frame < scal[COUNT_AT]).astype(F32)
        weight = jnp.where((row >= f * whole) & (row < (f + 1) * whole), live, weight)
    dy_out[...] = (xs[...] * weight).astype(BF16)


def cut_kernel(scal, own, peer, b0, b1, b2, b3):
    half, per = own.shape[0], b0.shape[0]
    for r, out in enumerate((b0, b1, b2, b3)):
        first = jnp.bitwise_xor(scal[P_AT], r) * per
        for i in range(per):
            for src, low in ((own, 0), (peer, half)):

                @pl.when((first >= low) & (first < low + half))
                def put(src=src, low=low):
                    out[i] = src[first - low + i]


def join_kernel(scal, b0, b1, b2, b3, own, peer):
    half, per = own.shape[0], b0.shape[0]
    for r, src in enumerate((b0, b1, b2, b3)):
        first = jnp.bitwise_xor(scal[P_AT], r) * per
        for i in range(per):
            for out, low in ((own, 0), (peer, half)):

                @pl.when((first >= low) & (first < low + half))
                def put(out=out, low=low):
                    out[first - low + i] = src[i]


def space_in_kernel(scal, b0, b1, b2, b3, par, w_load, x_out, h_out, qkv_out, xs):
    fill_space((b0, b1, b2, b3), xs)
    gain, shift = par[G_S : G_S + 1, :], par[B_S : B_S + 1, :]

    def rows(r):
        x = xs[r, :]
        x_out[r, :] = x.astype(BF16)
        h_out[r, :] = (normalise(x)[0] * gain + shift).astype(BF16)

    row_blocks(xs.shape[0], rows)
    project_qkv(h_out, w_load.get(), par, C_S, E_S, qkv_out)


def space_windows(rows, per):
    whole = rows // per
    step = whole // 16 * 16
    width = rows - step * (per - 1)
    return whole, step, width


def space_frame(f, rows, per):
    whole, step, width = space_windows(rows, per)
    first = f * (whole - step)
    row = lax.broadcasted_iota(jnp.int32, (width, 1), 0)
    col = lax.broadcasted_iota(jnp.int32, (1, width), 1)
    by_row, by_col = (row >= first) & (row < first + whole), (col >= first) & (col < first + whole)
    r = pl.ds(pl.multiple_of(f * step, 16), width)
    return r, jnp.where(by_row, 0.0, MASKED_SCORE), by_col.astype(F32), by_row.astype(F32)


def space_mid_kernel(per, scal, qkv, x, par, w_load, y_out, x2_out, m_out, ys):
    rows = x.shape[0]
    masks = head_masks()
    ys[...] = jnp.zeros_like(ys)

    def frame(f):
        r, bias, _, valid = space_frame(f, rows, per)
        for j in range(PAIRS):
            cq, ck, cv = pair_cols(j)
            ys[r, cq] += pair_forward(qkv[r, cq], qkv[r, ck], qkv[r, cv], bias, masks) * valid

    loop(per, frame)
    y_out[...] = ys[...].astype(BF16)
    w = w_load.get()

    def proj(i):
        c = block(i, NB)
        x2_out[:, c] = x[:, c].astype(F32) + (dot_nn(y_out[...], w[:, c]) + par[O_S : O_S + 1, c])

    loop(D // NB, proj)
    gain, shift = par[G_M : G_M + 1, :], par[B_M : B_M + 1, :]

    def norm(r):
        m_out[r, :] = (normalise(x2_out[r, :])[0] * gain + shift).astype(BF16)

    row_blocks(rows, norm)


def mlp_kernel(
    scal, m, dy, par, weights, x3_out, dm_out, dw1, dw1_their, dw2, dw2_their, dup,
    w1, w2, w_sems, e, da, mt, up_buf, up_sems, down_buf, down_sems,
):
    rows = D // 4
    steps = FF // D

    def loads(i):
        at = pl.multiple_of(i * D, 128)
        out = [pltpu.make_async_copy(weights.at[:, pl.ds(at, D)], w1.at[i % 2], w_sems.at[i % 2, 4])]
        for j in range(4):
            src = weights.at[pl.ds(pl.multiple_of(i * rows, 16), rows), FF + j * D : FF + (j + 1) * D]
            to = w2.at[i % 2, j * rows : (j + 1) * rows, :]
            out.append(pltpu.make_async_copy(src, to, w_sems.at[i % 2, j]))
        return out

    for c in loads(0):
        c.start()
    mt[...] = m[...].T
    x3_out[...] = jnp.zeros_like(x3_out)
    dm_out[...] = jnp.zeros_like(dm_out)

    def up_copy(i, k, out):
        to = out.at[:, pl.ds(pl.multiple_of(i % 2 * D + k * NB, NB), NB)]
        return pltpu.make_async_copy(up_buf.at[k], to, up_sems.at[k])

    def down_copy(i, j, out):
        to = out.at[pl.ds(pl.multiple_of(i * rows, 16), rows), j % 2 * D : (j % 2 + 1) * D]
        return pltpu.make_async_copy(down_buf.at[j], to, down_sems.at[j])

    def step(i):
        slot = i % 2
        for c in loads(i):
            c.wait()

        @pl.when(i + 1 < steps)
        def ahead():
            for c in loads(i + 1):
                c.start()

        up_w, down_w = w1.at[slot], w2.at[slot]
        for k in range(D // NB):
            c = slice(k * NB, (k + 1) * NB)
            a = dot_nn(m[...], up_w[:, c]) + par[pl.ds(U_1 + i, 1), c]
            g = dot_nt(dy[...], down_w[c, :])
            value, slope = gelu_parts(a)
            low = (g * slope).astype(BF16)
            e[:, c] = value.astype(BF16)
            da[:, c] = low
            dup[pl.ds(i, 1), c] = jnp.sum(low.astype(F32), axis=0, keepdims=True)
        for k in range(D // NB):
            c = slice(k * NB, (k + 1) * NB)
            value = dot_nn(mt[...], da[:, c]).astype(BF16)
            pl.when(i >= 1)(lambda k=k: up_copy(i - 1, k, dw1).wait())
            up_buf[k] = value
            pl.when(scal[C_AT] == i // 2)(lambda k=k: up_copy(i, k, dw1).start())
            pl.when(scal[C_AT] != i // 2)(lambda k=k: up_copy(i, k, dw1_their).start())
        value = dot_tn(e[...], dy[...]).astype(BF16)
        for j in range(4):
            pl.when(i >= 1)(lambda j=j: down_copy(i - 1, j, dw2).wait())
            down_buf[j] = value[j * rows : (j + 1) * rows, :]
            pl.when(scal[C_AT] == j // 2)(lambda j=j: down_copy(i, j, dw2).start())
            pl.when(scal[C_AT] != j // 2)(lambda j=j: down_copy(i, j, dw2_their).start())
        for k in range(D // NB):
            c = slice(k * NB, (k + 1) * NB)
            x3_out[:, c] += dot_nn(e[...], down_w[:, c])
            dm_out[:, c] += dot_nt(da[...], up_w[c, :])

    loop(steps, step)
    for k in range(D // NB):
        up_copy(steps - 1, k, dw1).wait()
    for j in range(4):
        down_copy(steps - 1, j, dw2).wait()


def mlp_out_kernel(per, scal, x2, x3, dm, dy, y, par, w_load, dx2_out, dys_out, dw, dw_their, dvec, b0, b1, b2, b3, xs, yt):
    rows = x2.shape[0]
    here = b0.shape[1]
    gain = par[G_M : G_M + 1, :]
    dvec[...] = jnp.zeros_like(dvec)
    yt[...] = y[...].T

    def back(r):
        xs[r, :] = x2[r, :] + (x3[r, :] + par[U_2 : U_2 + 1, :])
        dz, dg, db = norm_back(x2[r, :], dm[r, :], gain)
        g = dy[r, :].astype(F32)
        dx2 = g + dz
        dx2_out[r, :] = dx2
        low = dx2.astype(BF16)
        dys_out[r, :] = low
        dvec[0:1, :] += dg
        dvec[1:2, :] += db
        dvec[2:3, :] += jnp.sum(g, axis=0, keepdims=True)
        dvec[3:4, :] += jnp.sum(low.astype(F32), axis=0, keepdims=True)

    row_blocks(rows, back)
    for f in range(per):
        for r, out in enumerate((b0, b1, b2, b3)):
            first = f * 4 * here + r * here
            out[f] = xs[first : first + here, :].astype(BF16)

    weight_grad(yt, dys_out, scal, dw, dw_their)
    w = w_load.get()

    def proj(i):
        c = block(i, NB)
        xs[:, c] = dot_nt(dys_out[...], w[c, :])

    loop(D // NB, proj)
    dys_out[...] = xs[...].astype(BF16)


def space_back_kernel(per, scal, qkv, dy, dqkv_out, dvec, acc):
    rows = dy.shape[0]
    masks = head_masks()
    acc[...] = jnp.zeros_like(acc)

    def frame(f):
        r, bias, valid, _ = space_frame(f, rows, per)
        for j in range(PAIRS):
            cq, ck, cv = pair_cols(j)
            dq, dk, dv = pair_backward(qkv[r, cq], qkv[r, ck], qkv[r, cv], dy[r, cq], bias, masks, valid)
            acc[r, cq] += dq
            acc[r, ck] += dk
            acc[r, cv] += dv

    loop(per, frame)
    low = acc[...].astype(BF16)
    dqkv_out[...] = low
    dvec[...] = jnp.zeros_like(dvec)
    dvec[0:1, :] = jnp.sum(dqkv_out[:, :D].astype(F32), axis=0, keepdims=True)
    dvec[1:2, :] = jnp.sum(dqkv_out[:, 2 * D :].astype(F32), axis=0, keepdims=True)


def space_out_kernel(per, scal, dqkv, h, x, dx2, par, w_load, dw, dw_their, dvec, b0, b1, b2, b3, xs, ht):
    rows = x.shape[0]
    here = b0.shape[1]
    ht[...] = h[...].T
    weight_grad(ht, dqkv, scal, dw, dw_their)
    w = w_load.get()

    def proj(c):
        xs[:, c] = dot_nt(dqkv[...], w[c, :])

    col_blocks(D, proj)
    gain = par[G_S : G_S + 1, :]
    dvec[...] = jnp.zeros_like(dvec)

    def back(r):
        dz, dg, db = norm_back(x[r, :].astype(F32), xs[r, :], gain)
        xs[r, :] = dx2[r, :] + dz
        dvec[0:1, :] += dg
        dvec[1:2, :] += db

    row_blocks(rows, back)
    for f in range(per):
        for r, out in enumerate((b0, b1, b2, b3)):
            first = f * 4 * here + r * here
            out[f] = xs[first : first + here, :].astype(BF16)


def time_proj_kernel(scal, b0, b1, b2, b3, y, z, w_load, dx1_out, dy_out, dw, dw_their, dvec, xs, zt, dz):
    per, here = b0.shape[0], b0.shape[1]
    slots = 4 * per
    for r, src in enumerate((b0, b1, b2, b3)):
        first = jnp.bitwise_xor(scal[P_AT], r) * per
        for i in range(per):
            put_slot(xs, first + i, slots, src[i].astype(F32))
    dvec[...] = jnp.zeros_like(dvec)

    def gather_rows(r):
        value = get_rows(xs, r)
        dx1_out[r, :] = value.astype(BF16)
        dvec[0:1, :] += jnp.sum(value, axis=0, keepdims=True)

    row_blocks(xs.shape[1], gather_rows)
    w = w_load.get()

    def proj_f(i):
        c = block(i, NB)
        dz[:, c] = dot_nt(dx1_out[...], w[c, D:]).astype(BF16)

    loop(D // NB, proj_f)

    def proj_o(i):
        c = block(i, NB)
        dy_out[:, c] = dot_nt(dz[...], w[c, :D]).astype(BF16)

    loop(D // NB, proj_o)
    dvec[1:2, :] = jnp.sum(dz[...].astype(F32), axis=0, keepdims=True)

    def put_grad(half, left, right):
        zt[...] = left[...].T

        def cols(out):
            def body(i):
                out[:, block(i, NB)] = dot_nn(zt[...], right[:, block(i, NB)]).astype(BF16)

            loop(D // NB, body)

        pl.when(scal[C_AT] == half)(lambda: cols(dw))
        pl.when(scal[C_AT] != half)(lambda: cols(dw_their))

    put_grad(1, z, dx1_out)
    put_grad(0, y, dz)


def time_attn_back_kernel(slots, scal, qkv, dys, dqkv_out, dvec):
    def body(r, bias, masks):
        for j in range(PAIRS):
            cq, ck, cv = pair_cols(j)
            dq, dk, dv = pair_backward(qkv[r, cq], qkv[r, ck], qkv[r, cv], dys[r, cq], bias, masks)
            dqkv_out[r, cq] = dq.astype(BF16)
            dqkv_out[r, ck] = dk.astype(BF16)
            dqkv_out[r, cv] = dv.astype(BF16)

    time_windows(dys.shape[0], slots, scal, body)
    dvec[...] = jnp.zeros_like(dvec)
    dvec[0:1, :] = jnp.sum(dqkv_out[:, :D].astype(F32), axis=0, keepdims=True)
    dvec[1:2, :] = jnp.sum(dqkv_out[:, 2 * D :].astype(F32), axis=0, keepdims=True)


def time_out_kernel(
    scal, dqkv, h, x, dx1, par, v_t, v_a, v_n, v_s, v_m, v_u, w_load, own, peer, dw, dw_their, vec, dvec, xs, ht, vs
):
    half, here = own.shape[0], own.shape[1]
    slots = 2 * half
    w = w_load.get()

    def proj(i):
        put_cols(xs, i, dot_nt(dqkv[...], w[block(i, NB), :]))

    loop(D // NB, proj)
    gain = par[G_T : G_T + 1, :]
    dvec[...] = jnp.zeros_like(dvec)

    def back(r):
        dz, dg, db = norm_back(x[r, :].astype(F32), get_rows(xs, r), gain)
        put_rows(xs, r, dx1[r, :].astype(F32) + dz)
        dvec[0:1, :] += dg
        dvec[1:2, :] += db

    row_blocks(xs.shape[1], back)
    for s in range(slots):
        v = get_slot(xs, s, slots, here)
        if s < half:
            own[s] = v
        else:
            peer[s - half] = v.astype(BF16)
    vs[...] = jnp.zeros_like(vs)
    for at, (src, row, count) in enumerate(
        (
            (dvec, 0, 2), (None, 0, 0), (v_a, 0, 2), (None, 0, 0), (v_t, 1, 1), (v_t, 0, 1), (v_n, 0, 2), (None, 0, 0),
            (v_s, 0, 2), (None, 0, 0), (v_m, 3, 1), (v_m, 0, 2), (None, 0, 0), (None, 0, 0), (None, 0, 0), (None, 0, 0),
            (None, 0, 0), (v_m, 2, 1),
        )
    ):
        if src is not None:
            vs[at : at + count, :] = src[row : row + count, :]
    vs[U_1 : U_1 + FF // D, :] = v_u[: FF // D, :]
    vec[...] = vs[...].T.astype(BF16)
    ht[...] = h[...].T
    weight_grad(ht, dqkv, scal, dw, dw_their)


def add_split_kernel(packs, n_after, sel_at, scal, *refs):
    n = len(packs)
    send, keep = refs[2 * n + n_after], refs[2 * n + n_after + 1]
    sel = scal[sel_at]
    for i, (offset, width) in enumerate(packs):
        mine, other = refs[i], refs[n + i]
        for out, which in ((send, 1 - sel), (keep, sel)):
            value = mine[0, which].astype(F32) + other[0, which].astype(F32)
            out[0, :, offset : offset + width] = value.astype(BF16)


def add_split(scal, sel_at, mine, other, packs, rows, after=()):
    n = mine[0].shape[0]
    out = sds((n, rows, sum(w for _, w in packs)), BF16)

    def spec(a):
        return pl.BlockSpec((1,) + a.shape[1:], lambda i: (i, 0, 0, 0))

    return pl.pallas_call(
        functools.partial(add_split_kernel, packs, len(after), sel_at),
        grid=(n,),
        out_shape=(out, out),
        in_specs=[pl.BlockSpec(memory_space=pltpu.SMEM)]
        + [spec(a) for a in [*mine, *other]]
        + [pl.BlockSpec(memory_space=pl.ANY)] * len(after),
        out_specs=tuple(pl.BlockSpec((1, *out.shape[1:]), lambda i: (i, 0, 0)) for _ in range(2)),
        compiler_params=pltpu.CompilerParams(vmem_limit_bytes=SMALL_VMEM),
        cost_estimate=cost(20),
    )(scal, *mine, *other, *after)


def adam_update(weight, grad, moment, square, decay, factor, rate):
    grad = grad * factor
    moment = BETA_FIRST * moment + (1.0 - BETA_FIRST) * grad
    square = BETA_SECOND * square + (1.0 - BETA_SECOND) * grad * grad
    moment_hat = moment * (1.0 / (1.0 - BETA_FIRST**STEP))
    square_hat = square * (1.0 / (1.0 - BETA_SECOND**STEP))
    fresh = weight * (1.0 - rate * decay) - (rate * moment_hat) * (1.0 / (jnp.sqrt(square_hat) + ADAM_EPSILON))
    return (fresh, moment, square)


PLANE = ("tm", "pos")
EVERY = ("dp", "tm", "pos")


def pos_permute(a, r):
    n = lax.axis_size("pos")
    return lax.ppermute(a, "pos", [(i, i ^ r) for i in range(n)]) if r else a


def tm_permute(a):
    n = lax.axis_size("tm")
    return lax.ppermute(a, "tm", [(i, n - 1 - i) for i in range(n)])


def grid_permute(a, move):
    pairs = []
    for z in range(4):
        for x in range(2):
            for p in range(4):
                zz, xx, pp = move(z, x, p)
                pairs.append(((z * 2 + x) * 4 + p, (zz * 2 + xx) * 4 + pp))
    return lax.ppermute(a, EVERY, pairs)


def next_plane(a):
    return grid_permute(a, lambda z, x, p: (z ^ 1, x, p))


def far_plane(a):
    return grid_permute(a, lambda z, x, p: (z ^ 3, x, p))


def first_side(a):
    return grid_permute(a, lambda z, x, p: (z, x, p ^ 2) if p & 1 else (z, x ^ 1, p))


def second_side(a):
    return grid_permute(a, lambda z, x, p: (z, x ^ 1, p) if p & 1 else (z, x, p ^ 2))


def other_core(a):
    return grid_permute(a, lambda z, x, p: (z, x, p ^ 1))


def spread_plane(part):
    side = first_side(part)
    far, both = second_side(part), second_side(side)
    own = [part, side, far, both]
    return own + [other_core(a) for a in own]


def once(value, *others):
    return lax.optimization_barrier((value, *others))[0]


def pack_kernel(n, *refs):
    out, at = refs[-1], 0
    for src in refs[:n]:
        for part in range(src.shape[0] if len(src.shape) == 3 else 1):
            out[at] = src[part] if len(src.shape) == 3 else src[...]
            at += 1


def pack(arrays, *after):
    vmem = pl.BlockSpec(memory_space=pltpu.VMEM)
    return pl.pallas_call(
        functools.partial(pack_kernel, len(arrays)),
        out_shape=sds((sum(v.shape[0] if v.ndim == 3 else 1 for v in arrays), *arrays[0].shape[-2:]), BF16),
        in_specs=[vmem] * len(arrays) + [pl.BlockSpec(memory_space=pl.ANY)] * len(after),
        out_specs=vmem,
        compiler_params=pltpu.CompilerParams(vmem_limit_bytes=SMALL_VMEM),
        cost_estimate=cost(20),
        name="pack",
    )(*arrays, *after)


def gather_lines(piece):
    near = next_plane(piece)
    return [near, far_plane(piece), far_plane(near)]


class Group:
    def __init__(self, scal, members):
        self.scal, self.members, self.packs, at = scal, members, [], 0
        for mine, _ in members:
            self.packs.append((at, mine.shape[1]))
            at += mine.shape[1]
        self.width = at
        self.received = [other_core(t) for _, t in members]

    def add(self, mine, theirs):
        self.members = self.members + [(mine, theirs)]
        self.packs.append((self.width, mine.shape[1]))
        self.width += mine.shape[1]
        self.received = self.received + [other_core(theirs)]

    def chip(self, *after):
        mine = [m.reshape(4, 2, -1, m.shape[1]) for m, _ in self.members]
        other = [r.reshape(4, 2, -1, r.shape[1]) for r in self.received]
        self.send, self.keep = add_split(self.scal, A_AT, mine, other, self.packs, 2 * PIECE, after)
        self.received = first_side(self.send)

    def step(self, sel, shape, rows, move, after, gate=()):
        shape = (*shape, self.width)
        self.send, self.keep = add_split(
            self.scal, sel, [self.keep.reshape(shape)], [self.received.reshape(shape)], [(0, self.width)], rows, after
        )
        self.received = move(once(self.send, *gate) if gate else self.send)

    def side(self, *after, gate=()):
        self.step(B_AT, (4, 2, PIECE), PIECE, second_side, after, gate)

    def plane(self, *after):
        self.step(PAIR_AT, (1, 2, 2 * PIECE), 2 * PIECE, far_plane, after)

    def pair(self, *after):
        self.step(ODD_AT, (1, 2, PIECE), PIECE, next_plane, after)

    def total(self, square, alone=0, *after):
        vmem = pl.BlockSpec(memory_space=pltpu.VMEM)
        return pl.pallas_call(
            functools.partial(total_kernel, self.width - alone),
            out_shape=(sds((PIECE, self.width), BF16), sds(square.shape, F32)),
            in_specs=[pl.BlockSpec(memory_space=pltpu.SMEM), vmem, vmem, vmem]
            + [pl.BlockSpec(memory_space=pl.ANY)] * len(after),
            out_specs=(vmem, vmem),
            compiler_params=pltpu.CompilerParams(vmem_limit_bytes=SMALL_VMEM),
            cost_estimate=cost(20),
        )(self.scal, self.keep.reshape(PIECE, -1), self.received.reshape(PIECE, -1), square, *after)


def total_kernel(alone, scal, keep, received, before, *refs):
    out, square = refs[-2:]
    total = (keep[...].astype(F32) + received[...].astype(F32)).astype(BF16)
    out[...] = total
    total = total.astype(F32)
    found = jnp.sum(total[:, :alone] * total[:, :alone])
    if alone < total.shape[1]:
        found += jnp.where(scal[C_AT] == 0, jnp.sum(total[:, alone:] * total[:, alone:]), 0.0)
    square[...] = before[...] + found


def adam_kernel(jobs, n_arrays, steps, scal, total_square, *refs):
    ins, refs = refs[:9], refs[9:]
    arrays, refs = refs[:n_arrays], refs[n_arrays:]
    outs, grads, sems, buffers, out_sems = refs[:10], refs[10:13], refs[13], refs[14:16], refs[16]
    scale = CLIP_NORM / jnp.maximum(jnp.sqrt(total_square[0:1, 0:1]), CLIP_NORM)
    copies = []
    for start, offset, width, to_grad, firsts in jobs:
        for k in range(8):
            half = scal[C_AT] if k < 4 else 1 - scal[C_AT]
            quarter = scal[Q_AT + k] * PIECE
            each = width // len(firsts)
            for j, (low, high) in enumerate(firsts):
                src = arrays[start + k].at[:, offset + j * each : offset + (j + 1) * each]
                if to_grad == 1:
                    rows = pl.ds(pl.multiple_of(low + half * (high - low) + quarter, 16), PIECE)
                    to = grads[1].at[rows, :]
                else:
                    rows = pl.ds(pl.multiple_of(quarter, 16), PIECE)
                    to = grads[to_grad].at[rows, pl.ds(pl.multiple_of(low + half * (high - low), 128), each)]
                copies.append(pltpu.make_async_copy(src, to, sems.at[len(copies)]))
    for c in copies:
        c.start()
    for c in copies:
        c.wait()

    def rows_of(i, which):
        size = buffers[which].shape[2]
        return pl.ds(pl.multiple_of(i * size, 16), size)

    def copy_out(i, which, j):
        to = outs[3 * which + j].at[rows_of(i, which), :]
        return pltpu.make_async_copy(buffers[which].at[i % 2, j], to, out_sems.at[i % 2, which, j])

    def step(i):
        for which in range(2):
            r = rows_of(i, which)
            weight, moment, square = (v[r, :] for v in ins[3 * which : 3 * which + 3])
            g = grads[which][r, :].astype(F32)
            fresh = adam_update(weight, g, moment, square, WEIGHT_DECAY, scale, LEARN_RATE)
            for j, value in enumerate(fresh):
                pl.when(i >= 2)(lambda j=j: copy_out(i - 2, which, j).wait())
                buffers[which][i % 2, j] = value
                copy_out(i, which, j).start()

    loop(steps, step)
    g = grads[2][:, :LANES].astype(F32).T[: ins[6].shape[0], :]
    fresh = adam_update(ins[6][...], g, ins[7][...], ins[8][...], 0.0, scale, LEARN_RATE_VEC)
    for out, value in zip(outs[6:9], fresh):
        out[...] = value
    outs[9][...] = g[U_2 : U_2 + 1, :] * scale
    for i in (steps - 2, steps - 1):
        for which in range(2):
            for j in range(3):
                copy_out(i, which, j).wait()


def adam_all(scal, total_square, arrays, jobs, steps, wide, tall, vec):
    anywhere, vmem = pl.BlockSpec(memory_space=pl.ANY), pl.BlockSpec(memory_space=pltpu.VMEM)
    both = [*wide, *tall, *vec]
    shard = vec[0].shape[1]
    return pl.pallas_call(
        functools.partial(adam_kernel, jobs, len(arrays), steps),
        out_shape=tuple(sds(v.shape, F32) for v in both) + (sds((1, shard), F32),),
        in_specs=[pl.BlockSpec(memory_space=pltpu.SMEM)] + [vmem] * (1 + len(both)) + [anywhere] * len(arrays),
        out_specs=tuple([pl.BlockSpec(memory_space=pltpu.HBM)] * 6 + [vmem] * 4),
        scratch_shapes=[
            pltpu.VMEM(wide[0].shape, BF16),
            pltpu.VMEM(tall[0].shape, BF16),
            pltpu.VMEM((shard, 2 * LANES), BF16),
            pltpu.SemaphoreType.DMA((sum(8 * len(j[4]) for j in jobs),)),
            pltpu.VMEM((2, 3, wide[0].shape[0] // steps, wide[0].shape[1]), F32),
            pltpu.VMEM((2, 3, tall[0].shape[0] // steps, tall[0].shape[1]), F32),
            pltpu.SemaphoreType.DMA((2, 2, 3)),
        ],
        compiler_params=pltpu.CompilerParams(vmem_limit_bytes=ADAM_VMEM),
        cost_estimate=cost(25),
    )(scal, total_square, *both, *arrays)


def shards(
    tokens,
    cotangent,
    frame_counts,
    weight_in,
    weight_out,
    vectors,
    moment_in,
    moment_out,
    moment_vec,
    square_in,
    square_out,
    square_vec,
):
    clips, half, here, _ = tokens.shape
    tm, n_pos, n_dp = lax.axis_size("tm"), lax.axis_size("pos"), lax.axis_size("dp")
    slots = half * tm
    per = slots // n_pos
    rows = slots * here
    t, p, z = lax.axis_index("tm"), lax.axis_index("pos"), lax.axis_index("dp")
    count = lax.dynamic_index_in_dim(frame_counts, t, keepdims=False)
    line = n_dp == 4
    core = p % 2 if line else 0
    a = jnp.where(core == 0, t, p // 2)
    b = jnp.where(core == 0, p // 2, t)
    quarters = [2 * a + b, 2 * (1 - a) + b, 2 * a + 1 - b, 2 * (1 - a) + 1 - b]
    quarters += [2 * b + a, 2 * (1 - b) + a, 2 * b + 1 - a, 2 * (1 - b) + 1 - a]
    scal = jnp.stack([count, t, p, z, core, *quarters, a, b, z // 2, z % 2]).astype(jnp.int32)

    own_tokens, peer_tokens, own_cot, peer_cot = (
        lax.dynamic_index_in_dim(v, at, keepdims=False) for v in (tokens, cotangent) for at in (t, 1 - t)
    )
    low_in, low_out = weight_in.astype(BF16), weight_out.astype(BF16)
    vec_low = jnp.pad(vectors.astype(BF16), ((0, 0), (0, LANES - vectors.shape[1])))
    vec_low = jnp.concatenate([vec_low, vec_low], axis=1)

    spans = {"at": (0, 3 * D), "ot": (3 * D, 2 * D), "as": (5 * D, 3 * D), "os": (8 * D, D)}

    def whole(low, *after):
        part = low.shape[0] // (tm * n_pos)
        mine = once(lax.dynamic_slice_in_dim(low, (t * n_pos + p) * part, part, axis=0), *after)
        return lax.all_gather(mine, EVERY, axis=0, tiled=True)

    blk = sds((per, here, D), BF16)
    act = sds((rows, D), BF16)
    wide = sds((rows, 3 * D), BF16)
    full = sds((rows, D), F32)
    par_out = sds((VROWS, D), F32)
    vec_out = sds((8, D), F32)
    scr = pltpu.VMEM((rows, D), F32)
    scr_tiled = pltpu.VMEM((TILES, rows, LANES), F32)
    scr_low = pltpu.VMEM((rows, D), BF16)
    scr_hidden = pltpu.VMEM((rows, FF), BF16)
    scr_t = pltpu.VMEM((D, rows), BF16)

    def halves(cols, height=D):
        return [sds((height, cols), BF16)] * 2

    after_in = after_attn = after_mid = after_space = ()
    if line:
        quarter = lax.dynamic_slice_in_dim(weight_in, quarters[0] * PIECE, PIECE, axis=0)
        vec_quarter = lax.dynamic_slice_in_dim(vec_low[:, :LANES], quarters[0] * PIECE, PIECE, axis=0)

        def half_of(first, width):
            return lax.dynamic_slice_in_dim(quarter, first + core * (width // 2), width // 2, axis=1).astype(BF16)

        def lines(piece, near):
            return [near, far_plane(piece), far_plane(near)]

        def sides(first):
            return first_side(first), second_side(first)

        def cores(group):
            return group + [other_core(v) for v in group]

        piece_0 = jnp.concatenate([half_of(*spans["at"]), vec_quarter], axis=1)
        near_0 = next_plane(piece_0)
        lines_0 = lines(piece_0, near_0)
        part = D // 4 // (tm * n_pos)
        up_rows = lax.dynamic_slice(weight_in, ((t * n_pos + p) * part, 9 * D), (part, FF))
        down_rows = lax.dynamic_slice(
            weight_out.reshape(4, D // 4, D), (0, (t * n_pos + p) * part, 0), (4, part, D)
        )
        hidden = jnp.concatenate([up_rows, *down_rows], axis=1).astype(BF16)
        hidden = lax.all_gather(once(hidden, near_0), EVERY, axis=0, tiled=True)
        peer_tokens = tm_permute(peer_tokens)
        piece_1 = half_of(*spans["ot"])
        piece_2 = jnp.concatenate([half_of(*spans[name]) for name in ("as", "os")], axis=1)
        first_0 = pack(lines_0, piece_1, peer_tokens)
        side_0, far_0 = sides(first_0)
        piece_1 = once(piece_1, first_0)
        near_1 = next_plane(piece_1)
        pair_1 = pack([piece_1, near_1])
        far_pair_1 = far_plane(pair_1)
        both_0 = second_side(once(side_0, own_tokens, scal, vec_low, piece_2, pair_1))
        group_0 = cores([first_0, side_0, far_0, both_0])
        first_1 = pack([near_1, far_pair_1], both_0)
        side_1, far_1 = sides(first_1)
        piece_2 = once(piece_2, first_1)
        near_2 = next_plane(piece_2)
        pair_2 = pack([piece_2, near_2], first_1)
        far_pair_2 = far_plane(pair_2)
        after_in = (first_1, pair_2)
        w_at = Weight(3 * D, shard=low_in, blocks=[spans["at"]], pieces=group_0)
        w_vec = Weight(2 * LANES, shard=vec_low, blocks=[(0, 2 * LANES)], pieces=group_0, offset=3 * D // 2)
    else:
        peer_tokens, peer_cot = tm_permute(peer_tokens), tm_permute(peer_cot)

        w_at, w_ot, w_as, w_os = (
            Weight(width, whole=whole(low_in[:, first : first + width])) for first, width in spans.values()
        )
        up_all, down_all = whole(low_in[:, 9 * D :]), whole(low_out)
        w_vec = Weight(2 * LANES, whole=lax.all_gather(vec_low, "dp", axis=0, tiled=True))

    x, h_t, qkv_t, par = call(
        time_in_kernel, scal, [own_tokens, peer_tokens], [w_at, w_vec], [act, act, wide, par_out], [scr_tiled], after_in
    )
    if line:
        first_2 = pack([near_2, far_pair_2], h_t)
        both_1 = second_side(once(side_1, h_t))
        side_2, far_2 = sides(first_2)
        after_attn = (first_2, side_1)
    (y_t,) = call(functools.partial(time_attn_kernel, slots), scal, [qkv_t], [], [act], [], after_attn)
    if line:
        group_1 = cores(once([first_1, side_1, far_1, both_1], y_t))
        w_ot = Weight(2 * D, shard=low_in, blocks=[spans["ot"]], pieces=group_1)
        both_2 = second_side(once(side_2, y_t))
        after_mid = (side_2,)
    z_t, *x1 = call(time_mid_kernel, scal, [y_t, x, par], [w_ot], [act, blk, blk, blk, blk], [scr_tiled], after_mid)
    x1 = [pos_permute(v, r) for r, v in enumerate(x1)]
    if line:
        peer_cot = tm_permute(once(peer_cot, z_t))
        group_2 = cores(once([first_2, side_2, far_2, both_2], *x1[1:]))
        w_as = Weight(3 * D, shard=low_in, blocks=[spans["as"]], pieces=group_2)
        w_os = Weight(D, shard=low_in, blocks=[spans["os"]], pieces=group_2, offset=3 * D // 2)
        after_space = (peer_cot,)

    x1, h_s, qkv_s = call(space_in_kernel, scal, [*x1, par], [w_as], [act, act, wide], [scr], after_space)
    cot = call(cut_kernel, scal, [own_cot, peer_cot], [], [blk] * 4, [], (h_s,))
    cot = [pos_permute(v, r) for r, v in enumerate(cot)]
    y_s, x2, m = call(
        functools.partial(space_mid_kernel, per), scal, [qkv_s, x1, par], [w_os], [act, full, act], [scr], (cot[0],)
    )
    (dy,) = call(cot_kernel, scal, cot, [], [act], [scr], (m,))

    if not line:
        down_all = down_all.reshape(4, 4, D // 4, D).transpose(0, 2, 1, 3).reshape(D, FF)
        hidden = jnp.concatenate([up_all, down_all], axis=1)
    buffers = [
        pltpu.VMEM((2, D, D), BF16),
        pltpu.VMEM((2, D, D), BF16),
        pltpu.SemaphoreType.DMA((2, 5)),
        scr_low,
        scr_low,
        scr_t,
        pltpu.VMEM((D // NB, D, NB), BF16),
        pltpu.SemaphoreType.DMA((D // NB,)),
        pltpu.VMEM((4, D // 4, D), BF16),
        pltpu.SemaphoreType.DMA((4,)),
    ]
    x3, dm, g_1, g_1t, g_2, g_2t, v_u = call(
        mlp_kernel,
        scal,
        [m, dy, par],
        [],
        [full, full, *halves(FF // 2), *halves(FF // 2), vec_out],
        buffers,
        anywhere=(2, 3, 4, 5),
        left=(hidden,),
    )
    if line:
        group_a = Group(scal, [(g_1, g_1t), (g_2, g_2t)])
    dx2, dys, g_os, g_ost, v_m, *out = call(
        functools.partial(mlp_out_kernel, per),
        scal,
        [x2, x3, dm, dy, y_s, par],
        [w_os],
        [full, act, *halves(D // 2), vec_out, blk, blk, blk, blk],
        [scr, scr_t],
    )
    mine = (jnp.arange(clips, dtype=jnp.int32) == t)[:, None, None, None]

    wait = ()
    if line:
        group_a.chip(v_m)
        wait = (group_a.send,)
    dqkv_s, v_s = call(
        functools.partial(space_back_kernel, per),
        scal,
        [qkv_s, dys],
        [],
        [wide, vec_out],
        [pltpu.VMEM((rows, 3 * D), F32)],
        wait,
    )
    g_as, g_ast, v_n, *dx1 = call(
        functools.partial(space_out_kernel, per),
        scal,
        [dqkv_s, h_s, x1, dx2, par],
        [w_as],
        [*halves(3 * D // 2), vec_out, blk, blk, blk, blk],
        [scr, scr_t],
    )
    dx1 = [pos_permute(v, r) for r, v in enumerate(dx1)]

    if line:
        group_s = Group(scal, [(g_os, g_ost), (g_as, g_ast)])
        group_a.side(v_n, gate=dx1[1:])
        wait = (group_a.send,)
    dx1, dy_t, g_ot, g_ott, v_t = call(
        time_proj_kernel,
        scal,
        [*dx1, y_t, z_t],
        [w_ot],
        [act, act, *halves(D), vec_out],
        [scr_tiled, scr_t, scr_low],
        wait,
    )
    if line:
        group_s.add(g_ot, g_ott)
        group_a.plane(v_t)
        group_s.chip(group_a.send)
        wait = (group_s.send,)
    out = [pos_permute(once(v, v_t), r) for r, v in enumerate(out)]
    dqkv_t, v_a = call(
        functools.partial(time_attn_back_kernel, slots), scal, [qkv_t, dy_t], [], [wide, vec_out], [], wait
    )
    if line:
        group_s.side(v_a)
    out_own, out_peer = call(join_kernel, scal, out, [], [sds((half, here, D), BF16)] * 2, [], (v_a,))
    wait = (group_s.send, out_own) if line else ()
    grad_own, grad_peer, g_at, g_att, g_vec, _ = call(
        time_out_kernel,
        scal,
        [dqkv_t, h_t, x, dx1, par, v_t, v_a, v_n, v_s, v_m, v_u],
        [w_at],
        [
            sds((half, here, D), F32),
            sds((half, here, D), BF16),
            *halves(3 * D // 2),
            sds((D, LANES), BF16),
            vec_out,
        ],
        [scr_tiled, scr_t, pltpu.VMEM((LANES, D), F32)],
        wait,
    )
    if line:
        group_t = Group(scal, [(g_at, g_att), (g_vec, g_vec)])
        square = jnp.zeros((8, LANES), F32)
        group_a.pair(g_vec)
        group_s.plane(group_a.send)
        group_t.chip(group_s.send)
        group_t.side()
        sum_a, square = group_a.total(square, 0, group_t.send)
        sides_a = sides(sum_a)
        group_s.pair(sum_a)
        group_t.plane(group_s.send)
        sum_s, square = group_s.total(square, 0, group_t.send)
        parts_a = [sum_a, *sides_a, second_side(once(sides_a[0], group_t.send))]
        group_t.pair(sum_s)
        sides_s = sides(sum_s)
        parts_s = [sum_s, *sides_s, second_side(once(sides_s[0], group_t.send))]
        sum_t, square = group_t.total(square, LANES, *parts_a, *sides_s)
        parts_t = spread_plane(sum_t)
        parts = [*cores(parts_a), *cores(parts_s), *parts_t]
        out_peer, grad_peer = once(out_peer, parts_t[3]), once(grad_peer, parts_t[3])
    out_peer = tm_permute(out_peer)
    block_out = jnp.where(mine, out_own[None], out_peer[None])
    grad_peer = tm_permute(grad_peer).astype(F32)
    input_grad = jnp.where(mine, grad_own[None], grad_peer[None])

    if line:
        square = square + next_plane(square)
        square = square + far_plane(once(square, *parts_t[1:3]))
        square = square + first_side(square)
        square = square + second_side(once(square, parts_t[3]))
        square = square + other_core(square)
        total_square = square[0, 0]
    else:
        g_in = jnp.concatenate([g_at, g_att, g_ot, g_ott, g_as, g_ast, g_os, g_ost, g_1, g_1t], axis=1)
        g_out = jnp.concatenate([g_2, g_2t], axis=1).reshape(4, D // 4, 4, D).transpose(0, 2, 1, 3).reshape(FF, D)
        g_vec = g_vec[:, : vectors.shape[1]]

        def reduced(grad):
            mine_rows = lax.psum_scatter(grad, "dp", scatter_dimension=0, tiled=True)
            return lax.psum(mine_rows, PLANE).astype(F32)

        g_in, g_out, g_vec = reduced(g_in), reduced(g_out), reduced(g_vec)
        local_square = jnp.sum(g_in * g_in) + jnp.sum(g_out * g_out) + jnp.sum(g_vec * g_vec)
        total_square = lax.psum(local_square, "dp")

    grad_norm = jnp.sqrt(total_square)
    factor = CLIP_NORM / jnp.maximum(grad_norm, CLIP_NORM)
    wide_in, tall_in = (weight_in, moment_in, square_in), (weight_out, moment_out, square_out)
    vec_in = (vectors, moment_vec, square_vec)
    if line:

        def span(name):
            first, width = spans[name]
            return ((first, first + width // 2),)

        shard = weight_out.shape[0]
        jobs = [
            (0, *group_a.packs[0], 0, ((9 * D, 9 * D + FF // 2),)),
            (0, *group_a.packs[1], 1, ((0, shard // 2), (shard // 4, shard // 4 * 3))),
        ]
        for name, (offset, width) in zip(("os", "as", "ot"), group_s.packs):
            jobs.append((8, offset, width, 0, span(name)))
        jobs.append((16, *group_t.packs[0], 0, span("at")))
        jobs.append((16, *group_t.packs[1], 2, ((0, LANES),)))
        fresh = adam_all(scal, square, parts, jobs, 12, wide_in, tall_in, [v.T for v in vec_in])
        *fresh, new_v, first_v, second_v, bias_down = fresh
        fresh += [new_v.T, first_v.T, second_v.T]
        bias_down_grad = bias_down.reshape(-1)
    else:
        fresh = [
            *adam_update(weight_in, g_in, moment_in, square_in, WEIGHT_DECAY, factor, LEARN_RATE),
            *adam_update(weight_out, g_out, moment_out, square_out, WEIGHT_DECAY, factor, LEARN_RATE),
            *adam_update(vectors, g_vec, moment_vec, square_vec, 0.0, factor, LEARN_RATE_VEC),
        ]
        bias_down_grad = g_vec[:, U_2] * factor
    new_in, first_in, second_in, new_out, first_out, second_out, new_vec, first_vec, second_vec = fresh
    return (
        block_out,
        input_grad,
        grad_norm,
        new_in,
        new_out,
        new_vec,
        first_in,
        first_out,
        first_vec,
        second_in,
        second_out,
        second_vec,
        bias_down_grad,
    )


def solution(mesh):
    acts, rows = P("dp", "tm", "pos", None), P("dp", None)
    return jax.shard_map(
        shards,
        mesh=mesh,
        in_specs=(acts, acts, P("dp"), *[rows] * 9),
        out_specs=(acts, acts, P(), *[rows] * 9, P("dp")),
        check_vma=False,
    )
```

```python
import functools

import jax
import jax.numpy as jnp
from jax import lax
from jax.experimental import pallas as pl
from jax.experimental.pallas import tpu as pltpu
from jax.sharding import PartitionSpec as P

HEADS = 12
HD = 64
D = 768
FF = 3072
STEP = 10

NORM_EPSILON = 1e-06
CLIP_NORM = 1.0
LEARN_RATE = 0.03
LEARN_RATE_VEC = 0.25
BETA_FIRST = 0.9
BETA_SECOND = 0.999
ADAM_EPSILON = 1e-08
WEIGHT_DECAY = 0.05
MASKED_SCORE = -1e30
SCALE = HD ** (-0.5)

F32 = jnp.float32
BF16 = jnp.bfloat16
PAIR = 2 * HD
PAIRS = D // PAIR
NB = 256
ROWB = 112
WINDOW = 128
VMEM_LIMIT = 56 * 1024 * 1024
SMALL_VMEM = 16 * 1024 * 1024
SPARE_VMEM = 4 * 1024 * 1024
ADAM_VMEM = 20 * 1024 * 1024

G_T, B_T, C_T, E_T, O_T, F_T, G_S, B_S, C_S, E_S, O_S, G_M, B_M, U_1, U_2 = (
    0, 1, 2, 3, 4, 5, 6, 7, 8, 9, 10, 11, 12, 13, 17,
)


COUNT_AT, T_AT, P_AT, Z_AT, C_AT, Q_AT = 0, 1, 2, 3, 4, 5
A_AT, B_AT, PAIR_AT, ODD_AT = 13, 14, 15, 16
OTHERS = (1, 3, 2)
PIECE = 48
VROWS = 24


def dot_nn(a, b):
    return lax.dot_general(a, b, (((1,), (0,)), ((), ())), preferred_element_type=F32)


def dot_nt(a, b):
    return lax.dot_general(a, b, (((1,), (1,)), ((), ())), preferred_element_type=F32)


def dot_tn(a, b):
    return lax.dot_general(a, b, (((0,), (0,)), ((), ())), preferred_element_type=F32)


def loop(count, body, unroll=1):
    def step(i, carry):
        body(i)
        return carry

    lax.fori_loop(0, count, step, 0, unroll=unroll)


def block(i, size):
    return pl.ds(pl.multiple_of(i * size, size), size)


def row_blocks(rows, body):
    loop(rows // ROWB, lambda i: body(pl.ds(pl.multiple_of(i * ROWB, 16), ROWB)))


def col_blocks(cols, body):
    loop(cols // NB, lambda i: body(block(i, NB)))


LANES = 128
TILES = D // LANES


def put_slot(xs, s, slots, value):
    for j in range(TILES):
        xs[j, pl.ds(s, value.shape[0], stride=slots), :] = value[:, j * LANES : (j + 1) * LANES]


def get_slot(xs, s, slots, count):
    return jnp.concatenate([xs[j, pl.ds(s, count, stride=slots), :] for j in range(TILES)], axis=1)


def get_rows(xs, r):
    return jnp.concatenate([xs[j, r, :] for j in range(TILES)], axis=1)


def put_rows(xs, r, value):
    for j in range(TILES):
        xs[j, r, :] = value[:, j * LANES : (j + 1) * LANES]


def put_cols(xs, i, value):
    per = NB // LANES
    for j in range(per):
        xs[i * per + j] = value[:, j * LANES : (j + 1) * LANES]


def normalise(x):
    centred = x - jnp.mean(x, axis=-1, keepdims=True)
    variance = jnp.mean(centred * centred, axis=-1, keepdims=True)
    inverse = lax.rsqrt(variance + NORM_EPSILON)
    return centred * inverse, inverse


def norm_back(x, grad, gain):
    z_hat, inverse = normalise(x)
    h = grad * gain
    first = jnp.mean(h, axis=-1, keepdims=True)
    second = jnp.mean(h * z_hat, axis=-1, keepdims=True)
    dz = inverse * (h - first - z_hat * second)
    return dz, jnp.sum(grad * z_hat, axis=0, keepdims=True), jnp.sum(grad, axis=0, keepdims=True)


def head_masks():
    lane = lax.broadcasted_iota(jnp.int32, (1, PAIR), 1)
    return [(lane < HD).astype(BF16), (lane >= HD).astype(BF16)]


def gelu_parts(a):
    z = jnp.abs(a) * 0.7071067811865476
    t = 1.0 / (1.0 + 0.3275911 * z)
    e = jnp.exp(-z * z)
    poly = t * (0.254829592 + t * (-0.284496736 + t * (1.421413741 + t * (-1.453152027 + t * 1.061405429))))
    tail = 0.5 * poly * e
    phi_low = jnp.where(a < 0.0, tail, 1.0 - tail)
    return a * phi_low, phi_low + a * (0.3989422804014327 * e)


class Weight:
    def __init__(self, cols, rows=D, whole=None, shard=None, blocks=None, pieces=(), offset=0):
        self.rows, self.cols, self.whole, self.offset = rows, cols, whole, offset
        self.blocks = blocks
        self.arrays = [whole] if whole is not None else [shard, *pieces]

    def scratch(self):
        count = 1 if self.whole is not None else len(self.blocks) + 8 * len(OTHERS)
        return [pltpu.VMEM((self.rows, self.cols), BF16), pltpu.SemaphoreType.DMA((count,))]

    def copies(self, refs, scal, dst, sems):
        if self.whole is not None:
            return [pltpu.make_async_copy(refs[0].at[:, self.offset : self.offset + self.cols], dst, sems.at[0])]
        shard = self.rows // 4
        z, c = scal[Z_AT], scal[C_AT]
        own_rows = pl.ds(pl.multiple_of(z * shard, 16), shard)
        out, at = [], 0
        for first, size in self.blocks:
            src, to = refs[0].at[:, first : first + size], dst.at[own_rows, at : at + size]
            at += size
            out.append(pltpu.make_async_copy(src, to, sems.at[len(out)]))
        width = self.cols // 2
        for k in range(8):
            half = c if k < 4 else 1 - c
            quarter = scal[Q_AT + k]
            for j, m in enumerate(OTHERS):
                row = jnp.bitwise_xor(z, m) * shard + quarter * PIECE
                col = pl.multiple_of(half * width, 128)
                src = refs[1 + k].at[j, :, self.offset : self.offset + width]
                to = dst.at[pl.ds(pl.multiple_of(row, 16), PIECE), pl.ds(col, width)]
                out.append(pltpu.make_async_copy(src, to, sems.at[len(out)]))
        return out


class Loaded:
    def __init__(self, ref, copies):
        self.ref, self.copies, self.waited = ref, copies, False

    def get(self):
        if not self.waited:
            for c in self.copies:
                c.wait()
            self.waited = True
        return self.ref


def sds(shape, dtype):
    return jax.ShapeDtypeStruct(shape, dtype)


def cost(microseconds):
    return pl.CostEstimate(flops=int(microseconds * 1e9), bytes_accessed=0, transcendentals=0)


COSTS = {"join": 20, "cut": 20, "cot": 20}


def call(kernel, scal, ins, weights, outs, scratch=(), after=(), anywhere=(), left=()):
    n_in, n_out, n_scr = len(ins), len(outs), len(scratch)
    arrays = [a for w in weights for a in w.arrays]
    n_left = len(left)

    def body(scal_ref, *refs):
        in_refs, refs = refs[: n_in + n_left], refs[n_in + n_left :]
        array_refs, refs = refs[: len(arrays)], refs[len(arrays) + len(after) :]
        out_refs, refs = refs[:n_out], refs[n_out:]
        own, refs = refs[:n_scr], refs[n_scr:]
        loaded, at = [], 0
        for i, w in enumerate(weights):
            dst, sems = refs[2 * i : 2 * i + 2]
            copies = w.copies(array_refs[at : at + len(w.arrays)], scal_ref, dst, sems)
            at += len(w.arrays)
            for c in copies:
                c.start()
            loaded.append(Loaded(dst, copies))
        kernel(scal_ref, *in_refs, *loaded, *out_refs, *own)
        for w in loaded:
            w.get()

    in_vmem = pl.BlockSpec(memory_space=pltpu.VMEM)
    def padded(v):
        lead = 1
        for n in v.shape[:-2]:
            lead *= n
        return lead * (-(-v.shape[-2] // 16) * 16) * (-(-v.shape[-1] // LANES) * LANES) * jnp.dtype(v.dtype).itemsize

    held = [v for v in scratch if v.dtype in (BF16, F32)]
    used = sum(padded(v) for v in held) + sum(w.rows * w.cols * 2 for w in weights)
    limit = used + SPARE_VMEM
    name = getattr(kernel, "func", kernel).__name__.removesuffix("_kernel")
    return pl.pallas_call(
        body,
        name=name,
        out_shape=tuple(outs),
        in_specs=[pl.BlockSpec(memory_space=pltpu.SMEM)]
        + [in_vmem] * n_in
        + [pl.BlockSpec(memory_space=pltpu.HBM)] * n_left
        + [pl.BlockSpec(memory_space=pl.ANY)] * (len(arrays) + len(after)),
        out_specs=tuple(pl.BlockSpec(memory_space=pltpu.HBM) if i in anywhere else in_vmem for i in range(n_out)),
        scratch_shapes=list(scratch) + [x for w in weights for x in w.scratch()],
        compiler_params=pltpu.CompilerParams(vmem_limit_bytes=limit),
        cost_estimate=cost(COSTS.get(name, 0)),
    )(scal, *ins, *left, *arrays, *after)


def grad_cols(width, body):
    loop(width // NB, lambda i: body(pl.multiple_of(i * NB, NB), NB))
    if width % NB:
        body(width - width % NB, width % NB)


def weight_grad(left_t, right, scal, mine, theirs):
    width = mine.shape[1]
    for out, half in ((theirs, 1 - scal[C_AT]), (mine, scal[C_AT])):

        def body(at, size, out=out, half=half):
            c = pl.ds(pl.multiple_of(half * width + at, 128), size)
            out[:, pl.ds(at, size)] = dot_nn(left_t[...], right[:, c]).astype(BF16)

        grad_cols(width, body)


def stack_heads(a, masks):
    return jnp.concatenate([a * masks[0], a * masks[1]], axis=0)


def softmax_cols(scores):
    e = jnp.exp(scores - jnp.max(scores, axis=0, keepdims=True))
    return e * (1.0 / jnp.sum(e, axis=0, keepdims=True))


def pair_cols(j):
    return [slice(part * D + j * PAIR, part * D + (j + 1) * PAIR) for part in range(3)]


def pair_probs(q, kk, bias):
    size = q.shape[0]
    s = dot_nt(kk, q)
    return [softmax_cols(s[h * size : (h + 1) * size] + bias) for h in range(2)]


def pair_forward(q, k, v, bias, masks):
    p = pair_probs(q * BF16(SCALE), stack_heads(k, masks), bias)
    return dot_tn(jnp.concatenate(p, axis=0).astype(BF16), stack_heads(v, masks))


def pair_backward(q, k, v, g, bias, masks, valid=None):
    size = q.shape[0]
    q = q * BF16(SCALE)
    kk, vv = stack_heads(k, masks), stack_heads(v, masks)
    p = pair_probs(q, kk, bias)
    dp = dot_nt(vv, g)
    ds = []
    for h in range(2):
        if valid is not None:
            p[h] = p[h] * valid
        d = dp[h * size : (h + 1) * size]
        ds.append(p[h] * (d - jnp.sum(p[h] * d, axis=0, keepdims=True)))
    ds = jnp.concatenate(ds, axis=0).astype(BF16)
    pp = jnp.concatenate(p, axis=0).astype(BF16)
    dq = dot_tn(ds, kk) * SCALE
    dk, dv = dot_nn(ds, q), dot_nn(pp, g)
    first = lax.broadcasted_iota(jnp.int32, (1, PAIR), 1) < HD
    return dq, jnp.where(first, dk[:size], dk[size:]), jnp.where(first, dv[:size], dv[size:])


def time_bias(scal, slots, size):
    row = lax.broadcasted_iota(jnp.int32, (size, size), 0)
    col = lax.broadcasted_iota(jnp.int32, (size, size), 1)
    frame = jnp.bitwise_xor(row % slots, scal[T_AT] * (slots // 2))
    return jnp.where((row // slots == col // slots) & (frame < scal[COUNT_AT]), 0.0, MASKED_SCORE)


def time_windows(rows, slots, scal, body):
    masks = head_masks()
    bias = time_bias(scal, slots, WINDOW)
    loop(rows // WINDOW, lambda i: body(block(i, WINDOW), bias, masks))
    left = rows % WINDOW
    if left:
        body(pl.ds(rows - left, left), time_bias(scal, slots, left), masks)


def project_qkv(h, w, par, q_row, v_row, out):
    for part, row in enumerate((q_row, None, v_row)):

        def cols(i, part=part, row=row):
            c = pl.ds(pl.multiple_of(part * D + i * NB, NB), NB)
            value = dot_nn(h[...], w[:, c])
            if row is not None:
                value = value + par[row : row + 1, block(i, NB)]
            out[:, c] = value.astype(BF16)

        loop(D // NB, cols)


def time_in_kernel(scal, own, peer, w_load, vec_load, x_out, h_out, qkv_out, par, xs):
    half, here = own.shape[0], own.shape[1]
    slots = 2 * half
    for s in range(slots):
        src = own if s < half else peer
        put_slot(xs, s, slots, src[s % half].astype(F32))
    vec = vec_load.get()
    par[...] = vec[:, :LANES].astype(F32).T[:VROWS, :]
    gain, shift = par[G_T : G_T + 1, :], par[B_T : B_T + 1, :]

    def rows(r):
        x = get_rows(xs, r)
        x_out[r, :] = x.astype(BF16)
        h_out[r, :] = (normalise(x)[0] * gain + shift).astype(BF16)

    row_blocks(xs.shape[1], rows)
    project_qkv(h_out, w_load.get(), par, C_T, E_T, qkv_out)


def time_attn_kernel(slots, scal, qkv, y_out):
    def body(r, bias, masks):
        for j in range(PAIRS):
            cq, ck, cv = pair_cols(j)
            y_out[r, cq] = pair_forward(qkv[r, cq], qkv[r, ck], qkv[r, cv], bias, masks).astype(BF16)

    time_windows(y_out.shape[0], slots, scal, body)


def time_mid_kernel(scal, y, x, par, w_load, z_out, b0, b1, b2, b3, xs):
    here, per = b0.shape[1], b0.shape[0]
    slots = 4 * per
    w = w_load.get()

    def proj(i):
        c = block(i, NB)
        z_out[:, c] = (dot_nn(y[...], w[:, c]) + par[O_T : O_T + 1, c]).astype(BF16)

    loop(D // NB, proj)

    def after(i):
        c = block(i, NB)
        fc = dot_nn(z_out[...], w[:, pl.ds(pl.multiple_of(D + i * NB, NB), NB)])
        put_cols(xs, i, x[:, c].astype(F32) + (fc + par[F_T : F_T + 1, c]))

    loop(D // NB, after)
    for r, out in enumerate((b0, b1, b2, b3)):
        first = jnp.bitwise_xor(scal[P_AT], r) * per
        for i in range(per):
            out[i] = get_slot(xs, first + i, slots, here).astype(BF16)


def fill_space(blocks, xs):
    per, here = blocks[0].shape[0], blocks[0].shape[1]
    whole = here * len(blocks)
    for f in range(per):
        for r, b in enumerate(blocks):
            xs[f * whole + r * here : f * whole + (r + 1) * here, :] = b[f].astype(F32)


def cot_kernel(scal, b0, b1, b2, b3, dy_out, xs):
    per, here = b0.shape[0], b0.shape[1]
    fill_space((b0, b1, b2, b3), xs)
    whole = 4 * here
    rows = xs.shape[0]
    row = lax.broadcasted_iota(jnp.int32, (rows, 1), 0)
    slot = scal[P_AT] * per
    weight = jnp.zeros((rows, 1), F32)
    for f in range(per):
        frame = jnp.bitwise_xor(slot + f, scal[T_AT] * (2 * per))
        live = (frame < scal[COUNT_AT]).astype(F32)
        weight = jnp.where((row >= f * whole) & (row < (f + 1) * whole), live, weight)
    dy_out[...] = (xs[...] * weight).astype(BF16)


def cut_kernel(scal, own, peer, b0, b1, b2, b3):
    half, per = own.shape[0], b0.shape[0]
    for r, out in enumerate((b0, b1, b2, b3)):
        first = jnp.bitwise_xor(scal[P_AT], r) * per
        for i in range(per):
            for src, low in ((own, 0), (peer, half)):

                @pl.when((first >= low) & (first < low + half))
                def put(src=src, low=low):
                    out[i] = src[first - low + i]


def join_kernel(scal, b0, b1, b2, b3, own, peer):
    half, per = own.shape[0], b0.shape[0]
    for r, src in enumerate((b0, b1, b2, b3)):
        first = jnp.bitwise_xor(scal[P_AT], r) * per
        for i in range(per):
            for out, low in ((own, 0), (peer, half)):

                @pl.when((first >= low) & (first < low + half))
                def put(out=out, low=low):
                    out[first - low + i] = src[i]


def space_in_kernel(scal, b0, b1, b2, b3, par, w_load, x_out, h_out, qkv_out, xs):
    fill_space((b0, b1, b2, b3), xs)
    gain, shift = par[G_S : G_S + 1, :], par[B_S : B_S + 1, :]

    def rows(r):
        x = xs[r, :]
        x_out[r, :] = x.astype(BF16)
        h_out[r, :] = (normalise(x)[0] * gain + shift).astype(BF16)

    row_blocks(xs.shape[0], rows)
    project_qkv(h_out, w_load.get(), par, C_S, E_S, qkv_out)


def space_windows(rows, per):
    whole = rows // per
    step = whole // 16 * 16
    width = rows - step * (per - 1)
    return whole, step, width


def space_frame(f, rows, per):
    whole, step, width = space_windows(rows, per)
    first = f * (whole - step)
    row = lax.broadcasted_iota(jnp.int32, (width, 1), 0)
    col = lax.broadcasted_iota(jnp.int32, (1, width), 1)
    by_row, by_col = (row >= first) & (row < first + whole), (col >= first) & (col < first + whole)
    r = pl.ds(pl.multiple_of(f * step, 16), width)
    return r, jnp.where(by_row, 0.0, MASKED_SCORE), by_col.astype(F32), by_row.astype(F32)


def space_mid_kernel(per, scal, qkv, x, par, w_load, y_out, x2_out, m_out, ys):
    rows = x.shape[0]
    masks = head_masks()
    ys[...] = jnp.zeros_like(ys)

    def frame(f):
        r, bias, _, valid = space_frame(f, rows, per)
        for j in range(PAIRS):
            cq, ck, cv = pair_cols(j)
            ys[r, cq] += pair_forward(qkv[r, cq], qkv[r, ck], qkv[r, cv], bias, masks) * valid

    loop(per, frame)
    y_out[...] = ys[...].astype(BF16)
    w = w_load.get()

    def proj(i):
        c = block(i, NB)
        x2_out[:, c] = x[:, c].astype(F32) + (dot_nn(y_out[...], w[:, c]) + par[O_S : O_S + 1, c])

    loop(D // NB, proj)
    gain, shift = par[G_M : G_M + 1, :], par[B_M : B_M + 1, :]

    def norm(r):
        m_out[r, :] = (normalise(x2_out[r, :])[0] * gain + shift).astype(BF16)

    row_blocks(rows, norm)


def mlp_kernel(
    scal, m, dy, par, weights, x3_out, dm_out, dw1, dw1_their, dw2, dw2_their, dup,
    w1, w2, w_sems, e, da, mt, up_buf, up_sems, down_buf, down_sems,
):
    rows = D // 4
    steps = FF // D

    def loads(i):
        at = pl.multiple_of(i * D, 128)
        out = [pltpu.make_async_copy(weights.at[:, pl.ds(at, D)], w1.at[i % 2], w_sems.at[i % 2, 4])]
        for j in range(4):
            src = weights.at[pl.ds(pl.multiple_of(i * rows, 16), rows), FF + j * D : FF + (j + 1) * D]
            to = w2.at[i % 2, j * rows : (j + 1) * rows, :]
            out.append(pltpu.make_async_copy(src, to, w_sems.at[i % 2, j]))
        return out

    for c in loads(0):
        c.start()
    mt[...] = m[...].T
    x3_out[...] = jnp.zeros_like(x3_out)
    dm_out[...] = jnp.zeros_like(dm_out)

    def up_copy(i, k, out):
        to = out.at[:, pl.ds(pl.multiple_of(i % 2 * D + k * NB, NB), NB)]
        return pltpu.make_async_copy(up_buf.at[k], to, up_sems.at[k])

    def down_copy(i, j, out):
        to = out.at[pl.ds(pl.multiple_of(i * rows, 16), rows), j % 2 * D : (j % 2 + 1) * D]
        return pltpu.make_async_copy(down_buf.at[j], to, down_sems.at[j])

    def step(i):
        slot = i % 2
        for c in loads(i):
            c.wait()

        @pl.when(i + 1 < steps)
        def ahead():
            for c in loads(i + 1):
                c.start()

        up_w, down_w = w1.at[slot], w2.at[slot]
        for k in range(D // NB):
            c = slice(k * NB, (k + 1) * NB)
            a = dot_nn(m[...], up_w[:, c]) + par[pl.ds(U_1 + i, 1), c]
            g = dot_nt(dy[...], down_w[c, :])
            value, slope = gelu_parts(a)
            low = (g * slope).astype(BF16)
            e[:, c] = value.astype(BF16)
            da[:, c] = low
            dup[pl.ds(i, 1), c] = jnp.sum(low.astype(F32), axis=0, keepdims=True)
        for k in range(D // NB):
            c = slice(k * NB, (k + 1) * NB)
            value = dot_nn(mt[...], da[:, c]).astype(BF16)
            pl.when(i >= 1)(lambda k=k: up_copy(i - 1, k, dw1).wait())
            up_buf[k] = value
            pl.when(scal[C_AT] == i // 2)(lambda k=k: up_copy(i, k, dw1).start())
            pl.when(scal[C_AT] != i // 2)(lambda k=k: up_copy(i, k, dw1_their).start())
        value = dot_tn(e[...], dy[...]).astype(BF16)
        for j in range(4):
            pl.when(i >= 1)(lambda j=j: down_copy(i - 1, j, dw2).wait())
            down_buf[j] = value[j * rows : (j + 1) * rows, :]
            pl.when(scal[C_AT] == j // 2)(lambda j=j: down_copy(i, j, dw2).start())
            pl.when(scal[C_AT] != j // 2)(lambda j=j: down_copy(i, j, dw2_their).start())
        for k in range(D // NB):
            c = slice(k * NB, (k + 1) * NB)
            x3_out[:, c] += dot_nn(e[...], down_w[:, c])
            dm_out[:, c] += dot_nt(da[...], up_w[c, :])

    loop(steps, step)
    for k in range(D // NB):
        up_copy(steps - 1, k, dw1).wait()
    for j in range(4):
        down_copy(steps - 1, j, dw2).wait()


def mlp_out_kernel(per, scal, x2, x3, dm, dy, y, par, w_load, dx2_out, dys_out, dw, dw_their, dvec, b0, b1, b2, b3, xs, yt):
    rows = x2.shape[0]
    here = b0.shape[1]
    gain = par[G_M : G_M + 1, :]
    dvec[...] = jnp.zeros_like(dvec)
    yt[...] = y[...].T

    def back(r):
        xs[r, :] = x2[r, :] + (x3[r, :] + par[U_2 : U_2 + 1, :])
        dz, dg, db = norm_back(x2[r, :], dm[r, :], gain)
        g = dy[r, :].astype(F32)
        dx2 = g + dz
        dx2_out[r, :] = dx2
        low = dx2.astype(BF16)
        dys_out[r, :] = low
        dvec[0:1, :] += dg
        dvec[1:2, :] += db
        dvec[2:3, :] += jnp.sum(g, axis=0, keepdims=True)
        dvec[3:4, :] += jnp.sum(low.astype(F32), axis=0, keepdims=True)

    row_blocks(rows, back)
    for f in range(per):
        for r, out in enumerate((b0, b1, b2, b3)):
            first = f * 4 * here + r * here
            out[f] = xs[first : first + here, :].astype(BF16)

    weight_grad(yt, dys_out, scal, dw, dw_their)
    w = w_load.get()

    def proj(i):
        c = block(i, NB)
        xs[:, c] = dot_nt(dys_out[...], w[c, :])

    loop(D // NB, proj)
    dys_out[...] = xs[...].astype(BF16)


def space_back_kernel(per, scal, qkv, dy, dqkv_out, dvec, acc):
    rows = dy.shape[0]
    masks = head_masks()
    acc[...] = jnp.zeros_like(acc)

    def frame(f):
        r, bias, valid, _ = space_frame(f, rows, per)
        for j in range(PAIRS):
            cq, ck, cv = pair_cols(j)
            dq, dk, dv = pair_backward(qkv[r, cq], qkv[r, ck], qkv[r, cv], dy[r, cq], bias, masks, valid)
            acc[r, cq] += dq
            acc[r, ck] += dk
            acc[r, cv] += dv

    loop(per, frame)
    low = acc[...].astype(BF16)
    dqkv_out[...] = low
    dvec[...] = jnp.zeros_like(dvec)
    dvec[0:1, :] = jnp.sum(dqkv_out[:, :D].astype(F32), axis=0, keepdims=True)
    dvec[1:2, :] = jnp.sum(dqkv_out[:, 2 * D :].astype(F32), axis=0, keepdims=True)


def space_out_kernel(per, scal, dqkv, h, x, dx2, par, w_load, dw, dw_their, dvec, b0, b1, b2, b3, xs, ht):
    rows = x.shape[0]
    here = b0.shape[1]
    ht[...] = h[...].T
    weight_grad(ht, dqkv, scal, dw, dw_their)
    w = w_load.get()

    def proj(c):
        xs[:, c] = dot_nt(dqkv[...], w[c, :])

    col_blocks(D, proj)
    gain = par[G_S : G_S + 1, :]
    dvec[...] = jnp.zeros_like(dvec)

    def back(r):
        dz, dg, db = norm_back(x[r, :].astype(F32), xs[r, :], gain)
        xs[r, :] = dx2[r, :] + dz
        dvec[0:1, :] += dg
        dvec[1:2, :] += db

    row_blocks(rows, back)
    for f in range(per):
        for r, out in enumerate((b0, b1, b2, b3)):
            first = f * 4 * here + r * here
            out[f] = xs[first : first + here, :].astype(BF16)


def time_proj_kernel(scal, b0, b1, b2, b3, y, z, w_load, dx1_out, dy_out, dw, dw_their, dvec, xs, zt, dz):
    per, here = b0.shape[0], b0.shape[1]
    slots = 4 * per
    for r, src in enumerate((b0, b1, b2, b3)):
        first = jnp.bitwise_xor(scal[P_AT], r) * per
        for i in range(per):
            put_slot(xs, first + i, slots, src[i].astype(F32))
    dvec[...] = jnp.zeros_like(dvec)

    def gather_rows(r):
        value = get_rows(xs, r)
        dx1_out[r, :] = value.astype(BF16)
        dvec[0:1, :] += jnp.sum(value, axis=0, keepdims=True)

    row_blocks(xs.shape[1], gather_rows)
    w = w_load.get()

    def proj_f(i):
        c = block(i, NB)
        dz[:, c] = dot_nt(dx1_out[...], w[c, D:]).astype(BF16)

    loop(D // NB, proj_f)

    def proj_o(i):
        c = block(i, NB)
        dy_out[:, c] = dot_nt(dz[...], w[c, :D]).astype(BF16)

    loop(D // NB, proj_o)
    dvec[1:2, :] = jnp.sum(dz[...].astype(F32), axis=0, keepdims=True)

    def put_grad(half, left, right):
        zt[...] = left[...].T

        def cols(out):
            def body(i):
                out[:, block(i, NB)] = dot_nn(zt[...], right[:, block(i, NB)]).astype(BF16)

            loop(D // NB, body)

        pl.when(scal[C_AT] == half)(lambda: cols(dw))
        pl.when(scal[C_AT] != half)(lambda: cols(dw_their))

    put_grad(1, z, dx1_out)
    put_grad(0, y, dz)


def time_attn_back_kernel(slots, scal, qkv, dys, dqkv_out, dvec):
    def body(r, bias, masks):
        for j in range(PAIRS):
            cq, ck, cv = pair_cols(j)
            dq, dk, dv = pair_backward(qkv[r, cq], qkv[r, ck], qkv[r, cv], dys[r, cq], bias, masks)
            dqkv_out[r, cq] = dq.astype(BF16)
            dqkv_out[r, ck] = dk.astype(BF16)
            dqkv_out[r, cv] = dv.astype(BF16)

    time_windows(dys.shape[0], slots, scal, body)
    dvec[...] = jnp.zeros_like(dvec)
    dvec[0:1, :] = jnp.sum(dqkv_out[:, :D].astype(F32), axis=0, keepdims=True)
    dvec[1:2, :] = jnp.sum(dqkv_out[:, 2 * D :].astype(F32), axis=0, keepdims=True)


def time_out_kernel(
    scal, dqkv, h, x, dx1, par, v_t, v_a, v_n, v_s, v_m, v_u, w_load, own, peer, dw, dw_their, vec, dvec, xs, ht, vs
):
    half, here = own.shape[0], own.shape[1]
    slots = 2 * half
    w = w_load.get()

    def proj(i):
        put_cols(xs, i, dot_nt(dqkv[...], w[block(i, NB), :]))

    loop(D // NB, proj)
    gain = par[G_T : G_T + 1, :]
    dvec[...] = jnp.zeros_like(dvec)

    def back(r):
        dz, dg, db = norm_back(x[r, :].astype(F32), get_rows(xs, r), gain)
        put_rows(xs, r, dx1[r, :].astype(F32) + dz)
        dvec[0:1, :] += dg
        dvec[1:2, :] += db

    row_blocks(xs.shape[1], back)
    for s in range(slots):
        v = get_slot(xs, s, slots, here)
        if s < half:
            own[s] = v
        else:
            peer[s - half] = v.astype(BF16)
    vs[...] = jnp.zeros_like(vs)
    for at, (src, row, count) in enumerate(
        (
            (dvec, 0, 2), (None, 0, 0), (v_a, 0, 2), (None, 0, 0), (v_t, 1, 1), (v_t, 0, 1), (v_n, 0, 2), (None, 0, 0),
            (v_s, 0, 2), (None, 0, 0), (v_m, 3, 1), (v_m, 0, 2), (None, 0, 0), (None, 0, 0), (None, 0, 0), (None, 0, 0),
            (None, 0, 0), (v_m, 2, 1),
        )
    ):
        if src is not None:
            vs[at : at + count, :] = src[row : row + count, :]
    vs[U_1 : U_1 + FF // D, :] = v_u[: FF // D, :]
    vec[...] = vs[...].T.astype(BF16)
    ht[...] = h[...].T
    weight_grad(ht, dqkv, scal, dw, dw_their)


def add_split_kernel(packs, n_after, sel_at, scal, *refs):
    n = len(packs)
    send, keep = refs[2 * n + n_after], refs[2 * n + n_after + 1]
    sel = scal[sel_at]
    for i, (offset, width) in enumerate(packs):
        mine, other = refs[i], refs[n + i]
        for out, which in ((send, 1 - sel), (keep, sel)):
            value = mine[0, which].astype(F32) + other[0, which].astype(F32)
            out[0, :, offset : offset + width] = value.astype(BF16)


def add_split(scal, sel_at, mine, other, packs, rows, after=()):
    n = mine[0].shape[0]
    out = sds((n, rows, sum(w for _, w in packs)), BF16)

    def spec(a):
        return pl.BlockSpec((1,) + a.shape[1:], lambda i: (i, 0, 0, 0))

    return pl.pallas_call(
        functools.partial(add_split_kernel, packs, len(after), sel_at),
        grid=(n,),
        out_shape=(out, out),
        in_specs=[pl.BlockSpec(memory_space=pltpu.SMEM)]
        + [spec(a) for a in [*mine, *other]]
        + [pl.BlockSpec(memory_space=pl.ANY)] * len(after),
        out_specs=tuple(pl.BlockSpec((1, *out.shape[1:]), lambda i: (i, 0, 0)) for _ in range(2)),
        compiler_params=pltpu.CompilerParams(vmem_limit_bytes=SMALL_VMEM),
        cost_estimate=cost(20),
    )(scal, *mine, *other, *after)


def adam_update(weight, grad, moment, square, decay, factor, rate):
    grad = grad * factor
    moment = BETA_FIRST * moment + (1.0 - BETA_FIRST) * grad
    square = BETA_SECOND * square + (1.0 - BETA_SECOND) * grad * grad
    moment_hat = moment * (1.0 / (1.0 - BETA_FIRST**STEP))
    square_hat = square * (1.0 / (1.0 - BETA_SECOND**STEP))
    fresh = weight * (1.0 - rate * decay) - (rate * moment_hat) * (1.0 / (jnp.sqrt(square_hat) + ADAM_EPSILON))
    return (fresh, moment, square)


PLANE = ("tm", "pos")
EVERY = ("dp", "tm", "pos")


def pos_permute(a, r):
    n = lax.axis_size("pos")
    return lax.ppermute(a, "pos", [(i, i ^ r) for i in range(n)]) if r else a


def tm_permute(a):
    n = lax.axis_size("tm")
    return lax.ppermute(a, "tm", [(i, n - 1 - i) for i in range(n)])


def grid_permute(a, move):
    pairs = []
    for z in range(4):
        for x in range(2):
            for p in range(4):
                zz, xx, pp = move(z, x, p)
                pairs.append(((z * 2 + x) * 4 + p, (zz * 2 + xx) * 4 + pp))
    return lax.ppermute(a, EVERY, pairs)


def next_plane(a):
    return grid_permute(a, lambda z, x, p: (z ^ 1, x, p))


def far_plane(a):
    return grid_permute(a, lambda z, x, p: (z ^ 3, x, p))


def first_side(a):
    return grid_permute(a, lambda z, x, p: (z, x, p ^ 2) if p & 1 else (z, x ^ 1, p))


def second_side(a):
    return grid_permute(a, lambda z, x, p: (z, x ^ 1, p) if p & 1 else (z, x, p ^ 2))


def other_core(a):
    return grid_permute(a, lambda z, x, p: (z, x, p ^ 1))


def spread_plane(part):
    side = first_side(part)
    far, both = second_side(part), second_side(side)
    own = [part, side, far, both]
    return own + [other_core(a) for a in own]


def once(value, *others):
    return lax.optimization_barrier((value, *others))[0]


def pack_kernel(n, *refs):
    out, at = refs[-1], 0
    for src in refs[:n]:
        for part in range(src.shape[0] if len(src.shape) == 3 else 1):
            out[at] = src[part] if len(src.shape) == 3 else src[...]
            at += 1


def pack(arrays, *after):
    vmem = pl.BlockSpec(memory_space=pltpu.VMEM)
    return pl.pallas_call(
        functools.partial(pack_kernel, len(arrays)),
        out_shape=sds((sum(v.shape[0] if v.ndim == 3 else 1 for v in arrays), *arrays[0].shape[-2:]), BF16),
        in_specs=[vmem] * len(arrays) + [pl.BlockSpec(memory_space=pl.ANY)] * len(after),
        out_specs=vmem,
        compiler_params=pltpu.CompilerParams(vmem_limit_bytes=SMALL_VMEM),
        cost_estimate=cost(20),
        name="pack",
    )(*arrays, *after)


def gather_lines(piece):
    near = next_plane(piece)
    return [near, far_plane(piece), far_plane(near)]


class Group:
    def __init__(self, scal, members):
        self.scal, self.members, self.packs, at = scal, members, [], 0
        for mine, _ in members:
            self.packs.append((at, mine.shape[1]))
            at += mine.shape[1]
        self.width = at
        self.received = [other_core(t) for _, t in members]

    def add(self, mine, theirs):
        self.members = self.members + [(mine, theirs)]
        self.packs.append((self.width, mine.shape[1]))
        self.width += mine.shape[1]
        self.received = self.received + [other_core(theirs)]

    def chip(self, *after):
        mine = [m.reshape(4, 2, -1, m.shape[1]) for m, _ in self.members]
        other = [r.reshape(4, 2, -1, r.shape[1]) for r in self.received]
        self.send, self.keep = add_split(self.scal, A_AT, mine, other, self.packs, 2 * PIECE, after)
        self.received = first_side(self.send)

    def step(self, sel, shape, rows, move, after, gate=()):
        shape = (*shape, self.width)
        self.send, self.keep = add_split(
            self.scal, sel, [self.keep.reshape(shape)], [self.received.reshape(shape)], [(0, self.width)], rows, after
        )
        self.received = move(once(self.send, *gate) if gate else self.send)

    def side(self, *after, gate=()):
        self.step(B_AT, (4, 2, PIECE), PIECE, second_side, after, gate)

    def plane(self, *after):
        self.step(PAIR_AT, (1, 2, 2 * PIECE), 2 * PIECE, far_plane, after)

    def pair(self, *after):
        self.step(ODD_AT, (1, 2, PIECE), PIECE, next_plane, after)

    def total(self, square, alone=0, *after):
        vmem = pl.BlockSpec(memory_space=pltpu.VMEM)
        return pl.pallas_call(
            functools.partial(total_kernel, self.width - alone),
            out_shape=(sds((PIECE, self.width), BF16), sds(square.shape, F32)),
            in_specs=[pl.BlockSpec(memory_space=pltpu.SMEM), vmem, vmem, vmem]
            + [pl.BlockSpec(memory_space=pl.ANY)] * len(after),
            out_specs=(vmem, vmem),
            compiler_params=pltpu.CompilerParams(vmem_limit_bytes=SMALL_VMEM),
            cost_estimate=cost(20),
        )(self.scal, self.keep.reshape(PIECE, -1), self.received.reshape(PIECE, -1), square, *after)


def total_kernel(alone, scal, keep, received, before, *refs):
    out, square = refs[-2:]
    total = (keep[...].astype(F32) + received[...].astype(F32)).astype(BF16)
    out[...] = total
    total = total.astype(F32)
    found = jnp.sum(total[:, :alone] * total[:, :alone])
    if alone < total.shape[1]:
        found += jnp.where(scal[C_AT] == 0, jnp.sum(total[:, alone:] * total[:, alone:]), 0.0)
    square[...] = before[...] + found


def adam_kernel(jobs, n_arrays, steps, scal, total_square, *refs):
    ins, refs = refs[:9], refs[9:]
    arrays, refs = refs[:n_arrays], refs[n_arrays:]
    outs, grads, sems, buffers, out_sems = refs[:10], refs[10:13], refs[13], refs[14:16], refs[16]
    scale = CLIP_NORM / jnp.maximum(jnp.sqrt(total_square[0:1, 0:1]), CLIP_NORM)
    copies = []
    for start, offset, width, to_grad, firsts in jobs:
        for k in range(8):
            half = scal[C_AT] if k < 4 else 1 - scal[C_AT]
            quarter = scal[Q_AT + k] * PIECE
            each = width // len(firsts)
            for j, (low, high) in enumerate(firsts):
                src = arrays[start + k].at[:, offset + j * each : offset + (j + 1) * each]
                if to_grad == 1:
                    rows = pl.ds(pl.multiple_of(low + half * (high - low) + quarter, 16), PIECE)
                    to = grads[1].at[rows, :]
                else:
                    rows = pl.ds(pl.multiple_of(quarter, 16), PIECE)
                    to = grads[to_grad].at[rows, pl.ds(pl.multiple_of(low + half * (high - low), 128), each)]
                copies.append(pltpu.make_async_copy(src, to, sems.at[len(copies)]))
    for c in copies:
        c.start()
    for c in copies:
        c.wait()

    def rows_of(i, which):
        size = buffers[which].shape[2]
        return pl.ds(pl.multiple_of(i * size, 16), size)

    def copy_out(i, which, j):
        to = outs[3 * which + j].at[rows_of(i, which), :]
        return pltpu.make_async_copy(buffers[which].at[i % 2, j], to, out_sems.at[i % 2, which, j])

    def step(i):
        for which in range(2):
            r = rows_of(i, which)
            weight, moment, square = (v[r, :] for v in ins[3 * which : 3 * which + 3])
            g = grads[which][r, :].astype(F32)
            fresh = adam_update(weight, g, moment, square, WEIGHT_DECAY, scale, LEARN_RATE)
            for j, value in enumerate(fresh):
                pl.when(i >= 2)(lambda j=j: copy_out(i - 2, which, j).wait())
                buffers[which][i % 2, j] = value
                copy_out(i, which, j).start()

    loop(steps, step)
    g = grads[2][:, :LANES].astype(F32).T[: ins[6].shape[0], :]
    fresh = adam_update(ins[6][...], g, ins[7][...], ins[8][...], 0.0, scale, LEARN_RATE_VEC)
    for out, value in zip(outs[6:9], fresh):
        out[...] = value
    outs[9][...] = g[U_2 : U_2 + 1, :] * scale
    for i in (steps - 2, steps - 1):
        for which in range(2):
            for j in range(3):
                copy_out(i, which, j).wait()


def adam_all(scal, total_square, arrays, jobs, steps, wide, tall, vec):
    anywhere, vmem = pl.BlockSpec(memory_space=pl.ANY), pl.BlockSpec(memory_space=pltpu.VMEM)
    both = [*wide, *tall, *vec]
    shard = vec[0].shape[1]
    return pl.pallas_call(
        functools.partial(adam_kernel, jobs, len(arrays), steps),
        out_shape=tuple(sds(v.shape, F32) for v in both) + (sds((1, shard), F32),),
        in_specs=[pl.BlockSpec(memory_space=pltpu.SMEM)] + [vmem] * (1 + len(both)) + [anywhere] * len(arrays),
        out_specs=tuple([pl.BlockSpec(memory_space=pltpu.HBM)] * 6 + [vmem] * 4),
        scratch_shapes=[
            pltpu.VMEM(wide[0].shape, BF16),
            pltpu.VMEM(tall[0].shape, BF16),
            pltpu.VMEM((shard, 2 * LANES), BF16),
            pltpu.SemaphoreType.DMA((sum(8 * len(j[4]) for j in jobs),)),
            pltpu.VMEM((2, 3, wide[0].shape[0] // steps, wide[0].shape[1]), F32),
            pltpu.VMEM((2, 3, tall[0].shape[0] // steps, tall[0].shape[1]), F32),
            pltpu.SemaphoreType.DMA((2, 2, 3)),
        ],
        compiler_params=pltpu.CompilerParams(vmem_limit_bytes=ADAM_VMEM),
        cost_estimate=cost(25),
    )(scal, total_square, *both, *arrays)


def shards(
    tokens,
    cotangent,
    frame_counts,
    weight_in,
    weight_out,
    vectors,
    moment_in,
    moment_out,
    moment_vec,
    square_in,
    square_out,
    square_vec,
):
    clips, half, here, _ = tokens.shape
    tm, n_pos, n_dp = lax.axis_size("tm"), lax.axis_size("pos"), lax.axis_size("dp")
    slots = half * tm
    per = slots // n_pos
    rows = slots * here
    t, p, z = lax.axis_index("tm"), lax.axis_index("pos"), lax.axis_index("dp")
    count = lax.dynamic_index_in_dim(frame_counts, t, keepdims=False)
    line = n_dp == 4
    core = p % 2 if line else 0
    a = jnp.where(core == 0, t, p // 2)
    b = jnp.where(core == 0, p // 2, t)
    quarters = [2 * a + b, 2 * (1 - a) + b, 2 * a + 1 - b, 2 * (1 - a) + 1 - b]
    quarters += [2 * b + a, 2 * (1 - b) + a, 2 * b + 1 - a, 2 * (1 - b) + 1 - a]
    scal = jnp.stack([count, t, p, z, core, *quarters, a, b, z // 2, z % 2]).astype(jnp.int32)

    own_tokens, peer_tokens, own_cot, peer_cot = (
        lax.dynamic_index_in_dim(v, at, keepdims=False) for v in (tokens, cotangent) for at in (t, 1 - t)
    )
    low_in, low_out = weight_in.astype(BF16), weight_out.astype(BF16)
    vec_low = jnp.pad(vectors.astype(BF16), ((0, 0), (0, LANES - vectors.shape[1])))
    vec_low = jnp.concatenate([vec_low, vec_low], axis=1)

    spans = {"at": (0, 3 * D), "ot": (3 * D, 2 * D), "as": (5 * D, 3 * D), "os": (8 * D, D)}

    def whole(low, *after):
        part = low.shape[0] // (tm * n_pos)
        mine = once(lax.dynamic_slice_in_dim(low, (t * n_pos + p) * part, part, axis=0), *after)
        return lax.all_gather(mine, EVERY, axis=0, tiled=True)

    blk = sds((per, here, D), BF16)
    act = sds((rows, D), BF16)
    wide = sds((rows, 3 * D), BF16)
    full = sds((rows, D), F32)
    par_out = sds((VROWS, D), F32)
    vec_out = sds((8, D), F32)
    scr = pltpu.VMEM((rows, D), F32)
    scr_tiled = pltpu.VMEM((TILES, rows, LANES), F32)
    scr_low = pltpu.VMEM((rows, D), BF16)
    scr_hidden = pltpu.VMEM((rows, FF), BF16)
    scr_t = pltpu.VMEM((D, rows), BF16)

    def halves(cols, height=D):
        return [sds((height, cols), BF16)] * 2

    after_in = after_attn = after_mid = after_space = ()
    if line:
        quarter = lax.dynamic_slice_in_dim(weight_in, quarters[0] * PIECE, PIECE, axis=0)
        vec_quarter = lax.dynamic_slice_in_dim(vec_low[:, :LANES], quarters[0] * PIECE, PIECE, axis=0)

        def half_of(first, width):
            return lax.dynamic_slice_in_dim(quarter, first + core * (width // 2), width // 2, axis=1).astype(BF16)

        def lines(piece, near):
            return [near, far_plane(piece), far_plane(near)]

        def sides(first):
            return first_side(first), second_side(first)

        def cores(group):
            return group + [other_core(v) for v in group]

        piece_0 = jnp.concatenate([half_of(*spans["at"]), vec_quarter], axis=1)
        near_0 = next_plane(piece_0)
        lines_0 = lines(piece_0, near_0)
        part = D // 4 // (tm * n_pos)
        up_rows = lax.dynamic_slice(weight_in, ((t * n_pos + p) * part, 9 * D), (part, FF))
        down_rows = lax.dynamic_slice(
            weight_out.reshape(4, D // 4, D), (0, (t * n_pos + p) * part, 0), (4, part, D)
        )
        hidden = jnp.concatenate([up_rows, *down_rows], axis=1).astype(BF16)
        hidden = lax.all_gather(once(hidden, near_0), EVERY, axis=0, tiled=True)
        peer_tokens = tm_permute(peer_tokens)
        piece_1 = half_of(*spans["ot"])
        piece_2 = jnp.concatenate([half_of(*spans[name]) for name in ("as", "os")], axis=1)
        first_0 = pack(lines_0, piece_1, peer_tokens)
        side_0, far_0 = sides(first_0)
        piece_1 = once(piece_1, first_0)
        near_1 = next_plane(piece_1)
        pair_1 = pack([piece_1, near_1])
        far_pair_1 = far_plane(pair_1)
        both_0 = second_side(once(side_0, own_tokens, scal, vec_low, piece_2, pair_1))
        group_0 = cores([first_0, side_0, far_0, both_0])
        first_1 = pack([near_1, far_pair_1], both_0)
        side_1, far_1 = sides(first_1)
        piece_2 = once(piece_2, first_1)
        near_2 = next_plane(piece_2)
        pair_2 = pack([piece_2, near_2], first_1)
        far_pair_2 = far_plane(pair_2)
        after_in = (first_1, pair_2)
        w_at = Weight(3 * D, shard=low_in, blocks=[spans["at"]], pieces=group_0)
        w_vec = Weight(2 * LANES, shard=vec_low, blocks=[(0, 2 * LANES)], pieces=group_0, offset=3 * D // 2)
    else:
        peer_tokens, peer_cot = tm_permute(peer_tokens), tm_permute(peer_cot)

        w_at, w_ot, w_as, w_os = (
            Weight(width, whole=whole(low_in[:, first : first + width])) for first, width in spans.values()
        )
        up_all, down_all = whole(low_in[:, 9 * D :]), whole(low_out)
        w_vec = Weight(2 * LANES, whole=lax.all_gather(vec_low, "dp", axis=0, tiled=True))

    x, h_t, qkv_t, par = call(
        time_in_kernel, scal, [own_tokens, peer_tokens], [w_at, w_vec], [act, act, wide, par_out], [scr_tiled], after_in
    )
    if line:
        first_2 = pack([near_2, far_pair_2], h_t)
        both_1 = second_side(once(side_1, h_t))
        side_2, far_2 = sides(first_2)
        after_attn = (first_2, side_1)
    (y_t,) = call(functools.partial(time_attn_kernel, slots), scal, [qkv_t], [], [act], [], after_attn)
    if line:
        group_1 = cores(once([first_1, side_1, far_1, both_1], y_t))
        w_ot = Weight(2 * D, shard=low_in, blocks=[spans["ot"]], pieces=group_1)
        both_2 = second_side(once(side_2, y_t))
        after_mid = (side_2,)
    z_t, *x1 = call(time_mid_kernel, scal, [y_t, x, par], [w_ot], [act, blk, blk, blk, blk], [scr_tiled], after_mid)
    x1 = [pos_permute(v, r) for r, v in enumerate(x1)]
    if line:
        peer_cot = tm_permute(once(peer_cot, z_t))
        group_2 = cores(once([first_2, side_2, far_2, both_2], *x1[1:]))
        w_as = Weight(3 * D, shard=low_in, blocks=[spans["as"]], pieces=group_2)
        w_os = Weight(D, shard=low_in, blocks=[spans["os"]], pieces=group_2, offset=3 * D // 2)
        after_space = (peer_cot,)

    x1, h_s, qkv_s = call(space_in_kernel, scal, [*x1, par], [w_as], [act, act, wide], [scr], after_space)
    cot = call(cut_kernel, scal, [own_cot, peer_cot], [], [blk] * 4, [], (h_s,))
    cot = [pos_permute(v, r) for r, v in enumerate(cot)]
    y_s, x2, m = call(
        functools.partial(space_mid_kernel, per), scal, [qkv_s, x1, par], [w_os], [act, full, act], [scr], (cot[0],)
    )
    (dy,) = call(cot_kernel, scal, cot, [], [act], [scr], (m,))

    if not line:
        down_all = down_all.reshape(4, 4, D // 4, D).transpose(0, 2, 1, 3).reshape(D, FF)
        hidden = jnp.concatenate([up_all, down_all], axis=1)
    buffers = [
        pltpu.VMEM((2, D, D), BF16),
        pltpu.VMEM((2, D, D), BF16),
        pltpu.SemaphoreType.DMA((2, 5)),
        scr_low,
        scr_low,
        scr_t,
        pltpu.VMEM((D // NB, D, NB), BF16),
        pltpu.SemaphoreType.DMA((D // NB,)),
        pltpu.VMEM((4, D // 4, D), BF16),
        pltpu.SemaphoreType.DMA((4,)),
    ]
    x3, dm, g_1, g_1t, g_2, g_2t, v_u = call(
        mlp_kernel,
        scal,
        [m, dy, par],
        [],
        [full, full, *halves(FF // 2), *halves(FF // 2), vec_out],
        buffers,
        anywhere=(2, 3, 4, 5),
        left=(hidden,),
    )
    if line:
        group_a = Group(scal, [(g_1, g_1t), (g_2, g_2t)])
    dx2, dys, g_os, g_ost, v_m, *out = call(
        functools.partial(mlp_out_kernel, per),
        scal,
        [x2, x3, dm, dy, y_s, par],
        [w_os],
        [full, act, *halves(D // 2), vec_out, blk, blk, blk, blk],
        [scr, scr_t],
    )
    mine = (jnp.arange(clips, dtype=jnp.int32) == t)[:, None, None, None]

    wait = ()
    if line:
        group_a.chip(v_m)
        wait = (group_a.send,)
    dqkv_s, v_s = call(
        functools.partial(space_back_kernel, per),
        scal,
        [qkv_s, dys],
        [],
        [wide, vec_out],
        [pltpu.VMEM((rows, 3 * D), F32)],
        wait,
    )
    g_as, g_ast, v_n, *dx1 = call(
        functools.partial(space_out_kernel, per),
        scal,
        [dqkv_s, h_s, x1, dx2, par],
        [w_as],
        [*halves(3 * D // 2), vec_out, blk, blk, blk, blk],
        [scr, scr_t],
    )
    dx1 = [pos_permute(v, r) for r, v in enumerate(dx1)]

    if line:
        group_s = Group(scal, [(g_os, g_ost), (g_as, g_ast)])
        group_a.side(v_n, gate=dx1[1:])
        wait = (group_a.send,)
    dx1, dy_t, g_ot, g_ott, v_t = call(
        time_proj_kernel,
        scal,
        [*dx1, y_t, z_t],
        [w_ot],
        [act, act, *halves(D), vec_out],
        [scr_tiled, scr_t, scr_low],
        wait,
    )
    if line:
        group_s.add(g_ot, g_ott)
        group_a.plane(v_t)
        group_s.chip(group_a.send)
        wait = (group_s.send,)
    out = [pos_permute(once(v, v_t), r) for r, v in enumerate(out)]
    dqkv_t, v_a = call(
        functools.partial(time_attn_back_kernel, slots), scal, [qkv_t, dy_t], [], [wide, vec_out], [], wait
    )
    if line:
        group_s.side(v_a)
    out_own, out_peer = call(join_kernel, scal, out, [], [sds((half, here, D), BF16)] * 2, [], (v_a,))
    wait = (group_s.send, out_own) if line else ()
    grad_own, grad_peer, g_at, g_att, g_vec, _ = call(
        time_out_kernel,
        scal,
        [dqkv_t, h_t, x, dx1, par, v_t, v_a, v_n, v_s, v_m, v_u],
        [w_at],
        [
            sds((half, here, D), F32),
            sds((half, here, D), BF16),
            *halves(3 * D // 2),
            sds((D, LANES), BF16),
            vec_out,
        ],
        [scr_tiled, scr_t, pltpu.VMEM((LANES, D), F32)],
        wait,
    )
    if line:
        group_t = Group(scal, [(g_at, g_att), (g_vec, g_vec)])
        square = jnp.zeros((8, LANES), F32)
        group_a.pair(g_vec)
        group_s.plane(group_a.send)
        group_t.chip(group_s.send)
        group_t.side()
        sum_a, square = group_a.total(square, 0, group_t.send)
        sides_a = sides(sum_a)
        group_s.pair(sum_a)
        group_t.plane(group_s.send)
        sum_s, square = group_s.total(square, 0, group_t.send)
        parts_a = [sum_a, *sides_a, second_side(once(sides_a[0], group_t.send))]
        group_t.pair(sum_s)
        sides_s = sides(sum_s)
        parts_s = [sum_s, *sides_s, second_side(once(sides_s[0], group_t.send))]
        sum_t, square = group_t.total(square, LANES, *parts_a, *sides_s)
        parts_t = spread_plane(sum_t)
        parts = [*cores(parts_a), *cores(parts_s), *parts_t]
        out_peer, grad_peer = once(out_peer, parts_t[3]), once(grad_peer, parts_t[3])
    out_peer = tm_permute(out_peer)
    block_out = jnp.where(mine, out_own[None], out_peer[None])
    grad_peer = tm_permute(grad_peer).astype(F32)
    input_grad = jnp.where(mine, grad_own[None], grad_peer[None])

    if line:
        square = square + next_plane(square)
        square = square + far_plane(square)
        square = square + first_side(once(square, *parts_t[1:3]))
        square = square + second_side(once(square, parts_t[3]))
        square = square + other_core(square)
        total_square = square[0, 0]
    else:
        g_in = jnp.concatenate([g_at, g_att, g_ot, g_ott, g_as, g_ast, g_os, g_ost, g_1, g_1t], axis=1)
        g_out = jnp.concatenate([g_2, g_2t], axis=1).reshape(4, D // 4, 4, D).transpose(0, 2, 1, 3).reshape(FF, D)
        g_vec = g_vec[:, : vectors.shape[1]]

        def reduced(grad):
            mine_rows = lax.psum_scatter(grad, "dp", scatter_dimension=0, tiled=True)
            return lax.psum(mine_rows, PLANE).astype(F32)

        g_in, g_out, g_vec = reduced(g_in), reduced(g_out), reduced(g_vec)
        local_square = jnp.sum(g_in * g_in) + jnp.sum(g_out * g_out) + jnp.sum(g_vec * g_vec)
        total_square = lax.psum(local_square, "dp")

    grad_norm = jnp.sqrt(total_square)
    factor = CLIP_NORM / jnp.maximum(grad_norm, CLIP_NORM)
    wide_in, tall_in = (weight_in, moment_in, square_in), (weight_out, moment_out, square_out)
    vec_in = (vectors, moment_vec, square_vec)
    if line:

        def span(name):
            first, width = spans[name]
            return ((first, first + width // 2),)

        shard = weight_out.shape[0]
        jobs = [
            (0, *group_a.packs[0], 0, ((9 * D, 9 * D + FF // 2),)),
            (0, *group_a.packs[1], 1, ((0, shard // 2), (shard // 4, shard // 4 * 3))),
        ]
        for name, (offset, width) in zip(("os", "as", "ot"), group_s.packs):
            jobs.append((8, offset, width, 0, span(name)))
        jobs.append((16, *group_t.packs[0], 0, span("at")))
        jobs.append((16, *group_t.packs[1], 2, ((0, LANES),)))
        fresh = adam_all(scal, square, parts, jobs, 12, wide_in, tall_in, [v.T for v in vec_in])
        *fresh, new_v, first_v, second_v, bias_down = fresh
        fresh += [new_v.T, first_v.T, second_v.T]
        bias_down_grad = bias_down.reshape(-1)
    else:
        fresh = [
            *adam_update(weight_in, g_in, moment_in, square_in, WEIGHT_DECAY, factor, LEARN_RATE),
            *adam_update(weight_out, g_out, moment_out, square_out, WEIGHT_DECAY, factor, LEARN_RATE),
            *adam_update(vectors, g_vec, moment_vec, square_vec, 0.0, factor, LEARN_RATE_VEC),
        ]
        bias_down_grad = g_vec[:, U_2] * factor
    new_in, first_in, second_in, new_out, first_out, second_out, new_vec, first_vec, second_vec = fresh
    return (
        block_out,
        input_grad,
        grad_norm,
        new_in,
        new_out,
        new_vec,
        first_in,
        first_out,
        first_vec,
        second_in,
        second_out,
        second_vec,
        bias_down_grad,
    )


def solution(mesh):
    acts, rows = P("dp", "tm", "pos", None), P("dp", None)
    return jax.shard_map(
        shards,
        mesh=mesh,
        in_specs=(acts, acts, P("dp"), *[rows] * 9),
        out_specs=(acts, acts, P(), *[rows] * 9, P("dp")),
        check_vma=False,
    )
```
